32 devices in a mesh: groups: 2 (over x), ctx: 16 (over z, y, core).
Axes of the slice: x: 2, y: 2, z: 4, core: 2. Of those that a mesh axis runs over, the one named last changes fastest.
Arguments:
- queries: bfloat16 [2048, 4096], P(('groups', 'ctx')), parts along dimension 0, may hold values from -36 to 36
- keys: bfloat16 [2048, 512], P(('groups', 'ctx')), parts along dimension 0, may hold values from -12 to 12
- values: bfloat16 [2048, 512], P(('groups', 'ctx')), parts along dimension 0, may hold values from -6 to 6
- owner: int32 [2048], P('groups'), parts along dimension 0, may hold values from 0 to 15, as said below
- rollout_lengths: int32 [8], P('groups'), parts along dimension 0, may hold values from 1 to 512, 1024 in all
Outputs:
- attended: bfloat16 [2048, 4096], P(('groups', 'ctx')), parts along dimension 0
The draws below stay inside these ranges and needn't reach their ends.
There are 2 independent parts, one for each index of `groups`. The reference program is written for one: setup_inputs(seed, part) draws one part's arguments, and reference() takes and returns one part's arrays. A program takes and returns all parts, laid end to end along the dimension named above; each array names one. Nothing has to cross between parts.
Inputs may be any that keep to these rules, and one draw needn't show every extreme that they name: `owner`: each device index owns exactly 64 tokens. The 64 tokens of one device go to half of the devices, 8 tokens to each, and these owners' indices are alike modulo 2.
All inputs are finite; a program needn't handle non-finite values.
Results may differ from the reference program's by a relative error of at most 0.005.
Values may be sent and summed in bfloat16 or wider, within the bound.
No kernel may reach another device: no remote copies, remote signals or barrier semaphores. Data moves between devices by JAX's collectives and lax.ppermute only.
A program may use at most 64 MiB of HBM per device.

```python
import math
import jax
import jax.numpy as jnp
import numpy as np
from jax import lax

H = 32
KVH = 4
HD = 128
TOK_DEV = 64
ROLL = 4
TOKENS = 1024


def shared_base(seed_key):
    return jnp.clip(jax.random.normal(seed_key, (TOKENS, KVH * HD), jnp.float32), -4.0, 4.0)


def draw_keys(key, part):
    base = shared_base(key)
    result = base
    return result.astype(jnp.bfloat16)


def draw_queries(key, part):
    key = jax.random.fold_in(key, 12)
    fresh = jnp.clip(jax.random.normal(key, (TOKENS, H * HD), jnp.float32), -4.0, 4.0)
    result = fresh
    return result.astype(jnp.bfloat16)


def draw_owner(key, part):
    key = jax.random.fold_in(key, 13)
    node_count = TOKENS // TOK_DEV
    capacity = 2 * TOK_DEV // node_count
    classes = jax.random.permutation(jax.random.fold_in(key, 1), node_count) % 2
    pattern = jnp.repeat(2 * jnp.arange(node_count // 2, dtype=jnp.int32), capacity)
    table = pattern[None, :] + classes[:, None].astype(jnp.int32)
    row_keys = jax.random.split(jax.random.fold_in(key, 2), node_count)
    shuffled = jax.vmap(lambda row_key, row_vals: jax.random.permutation(row_key, row_vals))(row_keys, table)
    return shuffled.reshape(TOKENS).astype(jnp.int32)


def shard_levels(key, extent, shards, smallest, top_value):
    gain, own = 1.0, jax.random.fold_in(key, 6)
    for dim, parts in shards:
        draws = jnp.exp(jax.random.uniform(jax.random.fold_in(own, dim), (parts,), jnp.float32, smallest / len(shards), top_value / len(shards)))
        gain = gain * jnp.repeat(draws, extent[dim] // parts).reshape([-1 if axis == dim else 1 for axis in range(len(extent))])
    return gain


def length_profile(count, total, bound, slope):
    weights = [(1 << 20) // math.isqrt(standing ** slope) + 1 for standing in range(2, count + 1)]
    spare, given = total - bound - (count - 1), [1] * (count - 1)
    while spare > 0:
        movable = [i for i in range(count - 1) if given[i] < bound]
        mass, remaining = sum([weights[i] for i in movable]), spare
        for i in movable:
            extra = min(bound - given[i], max(1, remaining * weights[i] // mass), spare)
            given[i] = given[i] + extra
            spare = spare - extra
    return np.array([bound] + given)


def ragged(own_key, count, total, reach, skew):
    if count == 2:
        one = jax.random.randint(own_key, (), max(1, total - reach), min(reach, total - 1) + 1)
        return jnp.stack([one, total - one])
    sizes = jnp.asarray(length_profile(count, total, reach, skew), jnp.int32)
    pairs = (count - 1) // 2
    giver, taker = sizes[1:1 + 2 * pairs:2], sizes[2:2 + 2 * pairs:2]
    margin = jnp.minimum(giver - 1, reach - taker)
    passed = jax.random.randint(jax.random.fold_in(own_key, 1), (pairs,), 0, 1 << 20) % (margin + 1)
    sizes = sizes.at[1:1 + 2 * pairs:2].set(giver - passed).at[2:2 + 2 * pairs:2].set(taker + passed)
    return sizes[jax.random.permutation(jax.random.fold_in(own_key, 2), count)]


def gaussian(own_key, dims, width, reach, cuts=(), held_as=jnp.bfloat16):
    array = width * jax.random.normal(own_key, dims, jnp.float32)
    if cuts:
        array = array * shard_levels(own_key, dims, cuts, -0.22, 0.18)
    return jnp.clip(array, -reach, reach).astype(held_as)


def setup_inputs(seed: int = 0, part: int = 0) -> dict:
    streams_of = jax.random.split(jax.random.key(seed), 6)
    part_keys = jax.random.split(jax.random.fold_in(streams_of[5], part), 6)
    return {
        "queries": draw_queries(jax.random.fold_in(jax.random.fold_in(streams_of[5], part), 71), part),
        "keys": draw_keys(jax.random.fold_in(jax.random.fold_in(streams_of[5], part), 71), part),
        "values": gaussian(part_keys[2], (TOKENS, KVH * HD), 1.0, 6.0, ((0, 16),)),
        "owner": draw_owner(jax.random.fold_in(jax.random.fold_in(streams_of[5], part), 71), part),
        "rollout_lengths": ragged(part_keys[4], ROLL, TOKENS, TOKENS // 2, 2).astype(jnp.int32),
    }


NEGATIVE = -1e+30

def segment_of(position, rollout_ends):
    return lax.optimization_barrier(jnp.sum((position[:, None] >= rollout_ends[None, :]).astype(jnp.int32), axis=1))

def reference(queries, keys, values, owner, rollout_lengths):
    token_count = queries.shape[0]
    group_size = H // KVH
    rollout_ends = jnp.cumsum(rollout_lengths).astype(jnp.int32)
    position = jnp.arange(token_count, dtype=jnp.int32)
    segment = segment_of(position, rollout_ends)
    key_heads = keys.astype(jnp.float32).reshape(token_count, KVH, HD)
    value_heads = values.astype(jnp.float32).reshape(token_count, KVH, HD)
    block_size = min(token_count, 512)
    pieces = []
    for block_index in range(token_count // block_size):
        lower = block_index * block_size
        upper = lower + block_size
        query_rows = queries[lower:upper].astype(jnp.float32).reshape(block_size, KVH, group_size, HD)
        scores = jnp.einsum('tkgd,ukd->kgtu', query_rows, key_heads[:upper]) / jnp.sqrt(jnp.float32(HD))
        visible = (position[None, :upper] <= position[lower:upper, None]) & (segment[None, :upper] == segment[lower:upper, None])
        scores = jnp.where(visible, scores, NEGATIVE)
        peak = lax.optimization_barrier(jnp.max(scores, axis=-1))
        expo = jnp.where(visible, jnp.exp(scores - peak[..., None]), 0.0)
        denominator = lax.optimization_barrier(jnp.sum(expo, axis=-1))
        probs = lax.optimization_barrier(expo.astype(jnp.bfloat16)).astype(jnp.float32)
        numerator = jnp.einsum('kgtu,ukd->kgtd', probs, value_heads[:upper])
        context = (numerator / denominator[..., None]).transpose(2, 0, 1, 3).reshape(block_size, H * HD)
        pieces.append(context.astype(jnp.bfloat16))
    context_all = jnp.concatenate(pieces, axis=0)
    order = jnp.argsort(owner, stable=True).astype(jnp.int32)
    return context_all[order]
```

```python
import functools
import math

import jax
import jax.numpy as jnp
from jax import lax
from jax.experimental import pallas as pl
from jax.experimental.pallas import tpu as pltpu
from jax.sharding import PartitionSpec as P

H = 32
KVH = 4
HD = 128
GROUP = H // KVH
WIDE = GROUP * HD
NEGATIVE = -1e30
LANES = 128
TILE = 16
VMEM = pltpu.CompilerParams(vmem_limit_bytes=40 * 2**20)


def row_to_column(row):
    size = row.shape[1]
    here = lax.broadcasted_iota(jnp.int32, (size, size), 0)
    there = lax.broadcasted_iota(jnp.int32, (size, size), 1)
    return jnp.sum(jnp.where(here == there, row, 0), axis=1, keepdims=True)


def column_to_row(column):
    size = column.shape[0]
    here = lax.broadcasted_iota(jnp.int32, (size, size), 0)
    there = lax.broadcasted_iota(jnp.int32, (size, size), 1)
    return jnp.sum(jnp.where(here == there, column, 0), axis=0, keepdims=True)


def pack_kernel(levels, per_level, owner_ref, q_ref, k_ref, v_ref, out_ref):
    me = lax.axis_index("ctx")
    rows = q_ref.shape[0]
    both = owner_ref[pl.ds(me // 2, 1), :]
    swapped = jnp.concatenate((both[:, rows:], both[:, :rows]), axis=1)
    own = jnp.where(me % 2 == 1, swapped, both)[:, :rows]
    token = lax.broadcasted_iota(jnp.int32, (1, rows), 1)
    key_row = own * rows + token
    rank = jnp.sum((row_to_column(key_row) < key_row).astype(jnp.int32), axis=0, keepdims=True)
    place = lax.broadcasted_iota(jnp.int32, (rows, rows), 0)
    order = (place == rank).astype(jnp.float32).astype(jnp.bfloat16)
    for member in range(KVH):
        wide = slice(member * WIDE, (member + 1) * WIDE)
        head = slice(member * HD, (member + 1) * HD)
        sorted_q = jnp.dot(order, q_ref[:, wide], preferred_element_type=jnp.float32)
        sorted_q = sorted_q.astype(jnp.bfloat16)
        for level in range(levels):
            dest = level * KVH + member
            part = sorted_q[level * per_level : (level + 1) * per_level]
            if per_level < TILE:
                part = jnp.concatenate((part, jnp.zeros((TILE - per_level, WIDE), part.dtype)), 0)
            out_ref[dest, :TILE, :] = part
            for block in range(rows // TILE):
                here = slice(block * TILE, (block + 1) * TILE)
                col = block * 2 * HD
                out_ref[dest, TILE:, col : col + HD] = k_ref[here, head]
                out_ref[dest, TILE:, col + HD : col + 2 * HD] = v_ref[here, head]


def place_kernel(per_level, lengths_ref, owner_ref, pos_ref, start_ref, order_ref):
    me = lax.axis_index("ctx")
    level, member = me // KVH, me % KVH
    table_rows = owner_ref.shape[0]
    total = table_rows * LANES
    held = pos_ref.shape[0]
    rows = LANES // 2
    shift = per_level.bit_length() - 1
    block_rows = 32
    table_step = table_rows // (held // block_rows)
    first = lax.broadcasted_iota(jnp.int32, (LANES, LANES), 0)
    second = lax.broadcasted_iota(jnp.int32, (LANES, LANES), 1)
    same = (first < rows) == (second < rows)
    lane = lax.broadcasted_iota(jnp.int32, (1, LANES), 1)
    line = lax.broadcasted_iota(jnp.int32, (block_rows, 1), 0)
    wanted = level * per_level + jnp.bitwise_and(line, per_level - 1)
    source = jnp.right_shift(line, shift)
    keys = []
    for block in range(held // block_rows):
        pos = jnp.zeros((block_rows, 1), jnp.int32)
        own = jnp.zeros((block_rows, 1), jnp.int32)
        for step in range(table_step):
            table = block * table_step + step
            owners = owner_ref[table : table + 1, :]
            key_row = owners * LANES + lane
            below = same & (row_to_column(key_row) < key_row)
            rank = jnp.sum(below.astype(jnp.int32), axis=0, keepdims=True)
            lane_source = 2 * step + (lane >= rows).astype(jnp.int32)
            hit = (wanted == rank) & (source == lane_source)
            pos += jnp.sum(jnp.where(hit, lane + table * LANES, 0), axis=1, keepdims=True)
            own += jnp.sum(jnp.where(hit, owners, 0), axis=1, keepdims=True)
        start = jnp.zeros((block_rows, 1), jnp.int32)
        end = jnp.int32(0)
        for rollout in range(lengths_ref.shape[0]):
            end = end + lengths_ref[rollout]
            start = jnp.where(pos >= end, end, start)
        here = slice(block * block_rows, (block + 1) * block_rows)
        pos_ref[here, :] = jnp.broadcast_to(pos, (block_rows, LANES))
        start_ref[here, :] = jnp.broadcast_to(start, (block_rows, LANES))
        keys.append((own - level * KVH) * total + pos)
    key_col = jnp.concatenate(keys, axis=0)
    key_row = column_to_row(key_col)
    slot = jnp.sum((key_col < key_row).astype(jnp.int32), axis=0, keepdims=True)
    slot = jnp.bitwise_xor(slot, member * rows)
    place = lax.broadcasted_iota(jnp.int32, (held, held), 0)
    order_ref[...] = (place == slot).astype(jnp.float32).astype(jnp.bfloat16)


def attend_kernel(q_ref, kv_ref, pos_ref, start_ref, order_ref, *refs):
    out_refs, (k_all, v_all, context) = refs[:KVH], refs[KVH:]
    nodes = kv_ref.shape[0]
    total = k_all.shape[0]
    held = context.shape[0]
    block_rows = 32
    blocks = held // block_rows
    span = total // blocks
    tokens = total // nodes
    scale = math.log2(math.e) / math.sqrt(HD)

    def unpack(node, carry):
        for block in range(tokens // TILE):
            row = pl.ds(pl.multiple_of(node * tokens + block * TILE, TILE), TILE)
            col = block * 2 * HD
            k_all[row, :] = kv_ref[node, :, col : col + HD]
            v_all[row, :HD] = kv_ref[node, :, col + HD : col + 2 * HD]
        return carry

    v_all[:, HD:] = jnp.ones((total, HD), jnp.bfloat16)
    lax.fori_loop(0, nodes, unpack, 0, unroll=nodes <= 16)

    for block in range(blocks):
        here = slice(block * block_rows, (block + 1) * block_rows)
        pieces = []
        for head in range(GROUP):
            for part in range(block_rows // TILE):
                at = block * (block_rows // TILE) + part
                pieces.append(q_ref[at, :, head * HD : (head + 1) * HD])
        queries = jnp.concatenate(pieces, axis=0)
        pos = pos_ref[here, :1]
        start = start_ref[here, :1]
        low, high = max(0, block - blocks // 2) * span, (block + 1) * span
        chunk = high - low if high - low <= 1024 else span
        peak, acc = None, None
        for lower in range(low, high, chunk):
            keys = slice(lower, lower + chunk)
            scores = lax.dot_general(
                queries, k_all[keys, :], (((1,), (1,)), ((), ())), preferred_element_type=jnp.float32
            )
            at = lower + lax.broadcasted_iota(jnp.int32, (block_rows, chunk), 1)
            bias = jnp.where((at <= pos) & (at >= start), 0.0, NEGATIVE)
            scores = scores.reshape(GROUP, block_rows, chunk) + bias[None]
            scores = scores.reshape(GROUP * block_rows, chunk)
            top = jnp.max(scores, axis=1, keepdims=True)
            if peak is not None:
                top = jnp.maximum(peak, top)
            probs = jnp.exp2((scores - top) * scale)
            if chunk != high - low:
                seen = (at <= pos) & (at >= start)
                probs = probs.reshape(GROUP, block_rows, chunk)
                probs = jnp.where(seen[None], probs, 0.0).reshape(GROUP * block_rows, chunk)
            new = jnp.dot(probs.astype(jnp.bfloat16), v_all[keys, :], preferred_element_type=jnp.float32)
            acc = new if acc is None else acc * jnp.exp2((peak - top) * scale) + new
            peak = top
        result = (acc[:, :HD] / acc[:, HD:]).astype(jnp.bfloat16)
        for head in range(GROUP):
            part = result[head * block_rows : (head + 1) * block_rows]
            context[here, head * HD : (head + 1) * HD] = part
    rows = held // KVH
    for member in range(KVH):
        order = order_ref[member * rows : (member + 1) * rows, :]
        moved = jnp.dot(order, context[...], preferred_element_type=jnp.float32)
        out_refs[member][...] = moved.astype(jnp.bfloat16)


def assemble_kernel(*refs):
    member = lax.axis_index("ctx") % KVH
    out_ref = refs[KVH]
    for index in range(KVH):
        col = pl.multiple_of(jnp.bitwise_xor(member, index) * WIDE, WIDE)
        out_ref[:, pl.ds(col, WIDE)] = refs[index][...]


def on_device(queries, keys, values, owner, rollout_lengths):
    rows = queries.shape[0]
    nodes = lax.axis_size("ctx")
    total = owner.shape[0]
    levels = nodes // KVH
    per_level = rows // levels
    held = rows * KVH
    table = owner.reshape(total // LANES, LANES)
    whole = pl.BlockSpec(memory_space=pltpu.VMEM)

    packed = pl.pallas_call(
        functools.partial(pack_kernel, levels, per_level),
        out_shape=jax.ShapeDtypeStruct((nodes, 2 * TILE, WIDE), jnp.bfloat16),
        in_specs=[whole] * 4,
        out_specs=whole,
        compiler_params=VMEM,
        name="pack",
    )(table, queries, keys, values)
    moved = lax.all_to_all(packed, "ctx", split_axis=0, concat_axis=0, tiled=True)

    pos, start, order = pl.pallas_call(
        functools.partial(place_kernel, per_level),
        out_shape=(
            jax.ShapeDtypeStruct((held, LANES), jnp.int32),
            jax.ShapeDtypeStruct((held, LANES), jnp.int32),
            jax.ShapeDtypeStruct((held, held), jnp.bfloat16),
        ),
        in_specs=[pl.BlockSpec(memory_space=pltpu.SMEM), whole],
        out_specs=(whole, whole, whole),
        compiler_params=VMEM,
        name="place",
    )(rollout_lengths, table)

    half = functools.partial(pl.BlockSpec, (nodes, TILE, WIDE))
    q_part, q_spec = moved, half(lambda i: (0, 0, 0))
    if per_level < TILE:
        q_part = moved[:, :per_level].reshape(held // TILE, TILE, WIDE)
        q_spec = pl.BlockSpec((held // TILE, TILE, WIDE), lambda i: (0, 0, 0))
    flat = lambda shape: pl.BlockSpec(shape, lambda i: (0, 0))
    blocks = pl.pallas_call(
        attend_kernel,
        grid=(1,),
        out_shape=tuple(jax.ShapeDtypeStruct((rows, WIDE), jnp.bfloat16) for _ in range(KVH)),
        in_specs=[
            q_spec,
            half(lambda i: (0, 1, 0)),
            flat((held, LANES)),
            flat((held, LANES)),
            flat((held, held)),
        ],
        out_specs=tuple(flat((rows, WIDE)) for _ in range(KVH)),
        scratch_shapes=[
            pltpu.VMEM((total, HD), jnp.bfloat16),
            pltpu.VMEM((total, 2 * HD), jnp.bfloat16),
            pltpu.VMEM((held, WIDE), jnp.bfloat16),
        ],
        compiler_params=VMEM,
        name="attend",
    )(q_part, moved, pos, start, order)

    returned = [blocks[0]]
    for index in range(1, KVH):
        pairs = [(node, node ^ index) for node in range(nodes)]
        returned.append(lax.ppermute(blocks[index], "ctx", pairs))
    return pl.pallas_call(
        assemble_kernel,
        out_shape=jax.ShapeDtypeStruct((rows, H * HD), jnp.bfloat16),
        in_specs=[whole] * KVH,
        out_specs=whole,
        compiler_params=VMEM,
        name="assemble",
    )(*returned)


def solution(mesh):
    placed = (
        P(("groups", "ctx"), None),
        P(("groups", "ctx"), None),
        P(("groups", "ctx"), None),
        P("groups"),
        P("groups"),
    )
    return jax.shard_map(
        on_device, mesh=mesh, in_specs=placed, out_specs=P(("groups", "ctx"), None), check_vma=False
    )
```

```python
import functools
import math

import jax
import jax.numpy as jnp
from jax import lax
from jax.experimental import pallas as pl
from jax.experimental.pallas import tpu as pltpu
from jax.sharding import PartitionSpec as P

H = 32
KVH = 4
HD = 128
GROUP = H // KVH
WIDE = GROUP * HD
NEGATIVE = -1e30
LANES = 128
TILE = 16
VMEM = pltpu.CompilerParams(vmem_limit_bytes=40 * 2**20)
ALL_VMEM = pltpu.CompilerParams(vmem_limit_bytes=64 * 2**20 - 2**17)


def row_to_column(row):
    size = row.shape[1]
    here = lax.broadcasted_iota(jnp.int32, (size, size), 0)
    there = lax.broadcasted_iota(jnp.int32, (size, size), 1)
    return jnp.sum(jnp.where(here == there, row, 0), axis=1, keepdims=True)


def column_to_row(column):
    size = column.shape[0]
    here = lax.broadcasted_iota(jnp.int32, (size, size), 0)
    there = lax.broadcasted_iota(jnp.int32, (size, size), 1)
    return jnp.sum(jnp.where(here == there, column, 0), axis=0, keepdims=True)


def pack_kernel(levels, per_level, owner_hbm, q_hbm, k_hbm, v_hbm, out_hbm, *scratch):
    owner_ref, q_ref, k_ref, v_ref, out_ref, in_sems, q_sems, out_sems = scratch
    me = lax.axis_index("ctx")
    rows = q_ref.shape[0]
    arrivals = []
    for index, (source, target) in enumerate(((owner_hbm, owner_ref), (k_hbm, k_ref), (v_hbm, v_ref))):
        arrivals.append(pltpu.make_async_copy(source, target, in_sems.at[index]))
    queries = []
    for member in range(KVH):
        wide = pl.ds(member * WIDE, WIDE)
        queries.append(
            pltpu.make_async_copy(q_hbm.at[:, wide], q_ref.at[:, wide], q_sems.at[member])
        )
    arrivals[0].start()
    queries[0].start()
    arrivals[1].start()
    arrivals[2].start()
    for copy in queries[1:]:
        copy.start()
    arrivals[0].wait()
    both = owner_ref[pl.ds(me // 2, 1), :]
    swapped = jnp.concatenate((both[:, rows:], both[:, :rows]), axis=1)
    own = jnp.where(me % 2 == 1, swapped, both)[:, :rows]
    token = lax.broadcasted_iota(jnp.int32, (1, rows), 1)
    key_row = own * rows + token
    rank = jnp.sum((row_to_column(key_row) < key_row).astype(jnp.int32), axis=0, keepdims=True)
    place = lax.broadcasted_iota(jnp.int32, (rows, rows), 0)
    order = (place == rank).astype(jnp.float32).astype(jnp.bfloat16)
    departures = []
    for member in range(KVH):
        wide = slice(member * WIDE, (member + 1) * WIDE)
        head = slice(member * HD, (member + 1) * HD)
        queries[member].wait()
        sorted_q = jnp.dot(order, q_ref[:, wide], preferred_element_type=jnp.float32)
        sorted_q = sorted_q.astype(jnp.bfloat16)
        if member == 0:
            arrivals[1].wait()
            arrivals[2].wait()
        for level in range(levels):
            dest = level * KVH + member
            part = sorted_q[level * per_level : (level + 1) * per_level]
            if per_level < TILE:
                part = jnp.concatenate((part, jnp.zeros((TILE - per_level, WIDE), part.dtype)), 0)
            out_ref[dest, :TILE, :] = part
            for block in range(rows // TILE):
                here = slice(block * TILE, (block + 1) * TILE)
                col = block * 2 * HD
                out_ref[dest, TILE:, col : col + HD] = k_ref[here, head]
                out_ref[dest, TILE:, col + HD : col + 2 * HD] = v_ref[here, head]
            copy = pltpu.make_async_copy(out_ref.at[dest], out_hbm.at[dest], out_sems.at[dest])
            copy.start()
            departures.append(copy)
    for copy in departures:
        copy.wait()


def place_kernel(per_level, lengths_ref, owner_ref, pos_ref, start_ref, order_ref):
    me = lax.axis_index("ctx")
    level, member = me // KVH, me % KVH
    table_rows = owner_ref.shape[0]
    total = table_rows * LANES
    held = pos_ref.shape[0]
    rows = LANES // 2
    shift = per_level.bit_length() - 1
    block_rows = 32
    table_step = table_rows // (held // block_rows)
    first = lax.broadcasted_iota(jnp.int32, (LANES, LANES), 0)
    second = lax.broadcasted_iota(jnp.int32, (LANES, LANES), 1)
    same = (first < rows) == (second < rows)
    lane = lax.broadcasted_iota(jnp.int32, (1, LANES), 1)
    line = lax.broadcasted_iota(jnp.int32, (block_rows, 1), 0)
    wanted = level * per_level + jnp.bitwise_and(line, per_level - 1)
    source = jnp.right_shift(line, shift)
    keys = []
    for block in range(held // block_rows):
        pos = jnp.zeros((block_rows, 1), jnp.int32)
        own = jnp.zeros((block_rows, 1), jnp.int32)
        for step in range(table_step):
            table = block * table_step + step
            owners = owner_ref[table : table + 1, :]
            key_row = owners * LANES + lane
            below = same & (row_to_column(key_row) < key_row)
            rank = jnp.sum(below.astype(jnp.int32), axis=0, keepdims=True)
            lane_source = 2 * step + (lane >= rows).astype(jnp.int32)
            hit = (wanted == rank) & (source == lane_source)
            pos += jnp.sum(jnp.where(hit, lane + table * LANES, 0), axis=1, keepdims=True)
            own += jnp.sum(jnp.where(hit, owners, 0), axis=1, keepdims=True)
        start = jnp.zeros((block_rows, 1), jnp.int32)
        end = jnp.int32(0)
        for rollout in range(lengths_ref.shape[0]):
            end = end + lengths_ref[rollout]
            start = jnp.where(pos >= end, end, start)
        here = slice(block * block_rows, (block + 1) * block_rows)
        pos_ref[here, :] = jnp.broadcast_to(pos, (block_rows, LANES))
        start_ref[here, :] = jnp.broadcast_to(start, (block_rows, LANES))
        keys.append((own - level * KVH) * total + pos)
    key_col = jnp.concatenate(keys, axis=0)
    key_row = column_to_row(key_col)
    slot = jnp.sum((key_col < key_row).astype(jnp.int32), axis=0, keepdims=True)
    slot = jnp.bitwise_xor(slot, member * rows)
    place = lax.broadcasted_iota(jnp.int32, (held, held), 0)
    order_ref[...] = (place == slot).astype(jnp.float32).astype(jnp.bfloat16)


def attend_kernel(q_ref, kv_ref, pos_ref, start_ref, order_ref, *refs):
    out_refs, (k_all, v_all, context) = refs[:KVH], refs[KVH:]
    nodes = kv_ref.shape[0]
    total = k_all.shape[0]
    held = context.shape[0]
    block_rows = 32
    blocks = held // block_rows
    span = total // blocks
    tokens = total // nodes
    scale = math.log2(math.e) / math.sqrt(HD)

    def unpack(node, carry):
        for block in range(tokens // TILE):
            row = pl.ds(pl.multiple_of(node * tokens + block * TILE, TILE), TILE)
            col = block * 2 * HD
            k_all[row, :] = kv_ref[node, :, col : col + HD]
            v_all[row, :HD] = kv_ref[node, :, col + HD : col + 2 * HD]
        return carry

    v_all[:, HD:] = jnp.ones((total, HD), jnp.bfloat16)
    lax.fori_loop(0, nodes, unpack, 0, unroll=nodes <= 16)

    for block in range(blocks):
        here = slice(block * block_rows, (block + 1) * block_rows)
        pieces = []
        for head in range(GROUP):
            for part in range(block_rows // TILE):
                at = block * (block_rows // TILE) + part
                pieces.append(q_ref[at, :, head * HD : (head + 1) * HD])
        queries = jnp.concatenate(pieces, axis=0)
        pos = pos_ref[here, :1]
        start = start_ref[here, :1]
        low, high = max(0, block - blocks // 2) * span, (block + 1) * span
        chunk = high - low if high - low <= 1024 else span
        peak, acc = None, None
        for lower in range(low, high, chunk):
            keys = slice(lower, lower + chunk)
            scores = lax.dot_general(
                queries, k_all[keys, :], (((1,), (1,)), ((), ())), preferred_element_type=jnp.float32
            )
            at = lower + lax.broadcasted_iota(jnp.int32, (block_rows, chunk), 1)
            bias = jnp.where((at <= pos) & (at >= start), 0.0, NEGATIVE)
            scores = scores.reshape(GROUP, block_rows, chunk) + bias[None]
            scores = scores.reshape(GROUP * block_rows, chunk)
            top = jnp.max(scores, axis=1, keepdims=True)
            if peak is not None:
                top = jnp.maximum(peak, top)
            probs = jnp.exp2((scores - top) * scale)
            if chunk != high - low:
                seen = (at <= pos) & (at >= start)
                probs = probs.reshape(GROUP, block_rows, chunk)
                probs = jnp.where(seen[None], probs, 0.0).reshape(GROUP * block_rows, chunk)
            new = jnp.dot(probs.astype(jnp.bfloat16), v_all[keys, :], preferred_element_type=jnp.float32)
            acc = new if acc is None else acc * jnp.exp2((peak - top) * scale) + new
            peak = top
        result = (acc[:, :HD] / acc[:, HD:]).astype(jnp.bfloat16)
        for head in range(GROUP):
            part = result[head * block_rows : (head + 1) * block_rows]
            context[here, head * HD : (head + 1) * HD] = part
    rows = held // KVH
    for member in range(KVH):
        order = order_ref[member * rows : (member + 1) * rows, :]
        moved = jnp.dot(order, context[...], preferred_element_type=jnp.float32)
        out_refs[member][...] = moved.astype(jnp.bfloat16)


def assemble_kernel(*refs):
    member = lax.axis_index("ctx") % KVH
    out_ref = refs[KVH]
    for index in range(KVH):
        col = pl.multiple_of(jnp.bitwise_xor(member, index) * WIDE, WIDE)
        out_ref[:, pl.ds(col, WIDE)] = refs[index][...]


def on_device(queries, keys, values, owner, rollout_lengths):
    rows = queries.shape[0]
    nodes = lax.axis_size("ctx")
    total = owner.shape[0]
    levels = nodes // KVH
    per_level = rows // levels
    held = rows * KVH
    table = owner.reshape(total // LANES, LANES)
    whole = pl.BlockSpec(memory_space=pltpu.VMEM)
    hbm = pl.BlockSpec(memory_space=pltpu.HBM)

    packed = pl.pallas_call(
        functools.partial(pack_kernel, levels, per_level),
        out_shape=jax.ShapeDtypeStruct((nodes, 2 * TILE, WIDE), jnp.bfloat16),
        in_specs=[hbm] * 4,
        out_specs=hbm,
        scratch_shapes=[
            pltpu.VMEM(table.shape, jnp.int32),
            pltpu.VMEM(queries.shape, jnp.bfloat16),
            pltpu.VMEM(keys.shape, jnp.bfloat16),
            pltpu.VMEM(values.shape, jnp.bfloat16),
            pltpu.VMEM((nodes, 2 * TILE, WIDE), jnp.bfloat16),
            pltpu.SemaphoreType.DMA((3,)),
            pltpu.SemaphoreType.DMA((KVH,)),
            pltpu.SemaphoreType.DMA((nodes,)),
        ],
        compiler_params=ALL_VMEM,
        name="pack",
    )(table, queries, keys, values)
    moved = lax.all_to_all(packed, "ctx", split_axis=0, concat_axis=0, tiled=True)

    pos, start, order = pl.pallas_call(
        functools.partial(place_kernel, per_level),
        out_shape=(
            jax.ShapeDtypeStruct((held, LANES), jnp.int32),
            jax.ShapeDtypeStruct((held, LANES), jnp.int32),
            jax.ShapeDtypeStruct((held, held), jnp.bfloat16),
        ),
        in_specs=[pl.BlockSpec(memory_space=pltpu.SMEM), whole],
        out_specs=(whole, whole, whole),
        compiler_params=VMEM,
        name="place",
    )(rollout_lengths, table)

    half = functools.partial(pl.BlockSpec, (nodes, TILE, WIDE))
    q_part, q_spec = moved, half(lambda i: (0, 0, 0))
    if per_level < TILE:
        q_part = moved[:, :per_level].reshape(held // TILE, TILE, WIDE)
        q_spec = pl.BlockSpec((held // TILE, TILE, WIDE), lambda i: (0, 0, 0))
    flat = lambda shape: pl.BlockSpec(shape, lambda i: (0, 0))
    blocks = pl.pallas_call(
        attend_kernel,
        grid=(1,),
        out_shape=tuple(jax.ShapeDtypeStruct((rows, WIDE), jnp.bfloat16) for _ in range(KVH)),
        in_specs=[
            q_spec,
            half(lambda i: (0, 1, 0)),
            flat((held, LANES)),
            flat((held, LANES)),
            flat((held, held)),
        ],
        out_specs=tuple(flat((rows, WIDE)) for _ in range(KVH)),
        scratch_shapes=[
            pltpu.VMEM((total, HD), jnp.bfloat16),
            pltpu.VMEM((total, 2 * HD), jnp.bfloat16),
            pltpu.VMEM((held, WIDE), jnp.bfloat16),
        ],
        compiler_params=VMEM,
        name="attend",
    )(q_part, moved, pos, start, order)

    returned = [blocks[0]]
    for index in range(1, KVH):
        pairs = [(node, node ^ index) for node in range(nodes)]
        returned.append(lax.ppermute(blocks[index], "ctx", pairs))
    return pl.pallas_call(
        assemble_kernel,
        out_shape=jax.ShapeDtypeStruct((rows, H * HD), jnp.bfloat16),
        in_specs=[whole] * KVH,
        out_specs=whole,
        compiler_params=VMEM,
        name="assemble",
    )(*returned)


def solution(mesh):
    placed = (
        P(("groups", "ctx"), None),
        P(("groups", "ctx"), None),
        P(("groups", "ctx"), None),
        P("groups"),
        P("groups"),
    )
    return jax.shard_map(
        on_device, mesh=mesh, in_specs=placed, out_specs=P(("groups", "ctx"), None), check_vma=False
    )
```

```python
import functools
import math

import jax
import jax.numpy as jnp
from jax import lax
from jax.experimental import pallas as pl
from jax.experimental.pallas import tpu as pltpu
from jax.sharding import PartitionSpec as P

H = 32
KVH = 4
HD = 128
GROUP = H // KVH
WIDE = GROUP * HD
CORES = 2
HEADS = KVH // CORES
NEGATIVE = -1e30
LANES = 128
SUB = 8
Q_ROWS = HEADS * SUB
VMEM = pltpu.CompilerParams(vmem_limit_bytes=40 * 2**20)
ALL_VMEM = pltpu.CompilerParams(vmem_limit_bytes=64 * 2**20 - 2**17)


def row_to_column(row):
    size = row.shape[1]
    here = lax.broadcasted_iota(jnp.int32, (size, size), 0)
    there = lax.broadcasted_iota(jnp.int32, (size, size), 1)
    return jnp.sum(jnp.where(here == there, row, 0), axis=1, keepdims=True)


def column_to_row(column):
    size = column.shape[0]
    here = lax.broadcasted_iota(jnp.int32, (size, size), 0)
    there = lax.broadcasted_iota(jnp.int32, (size, size), 1)
    return jnp.sum(jnp.where(here == there, column, 0), axis=0, keepdims=True)


def pack_kernel(chips, owner_hbm, q_hbm, *refs):
    with_kv = len(refs) > 6
    kv_hbm, refs = (refs[:2], refs[2:]) if with_kv else ((), refs)
    out_hbm, owner_ref, q_ref, out_ref, in_sems, out_sems = refs[:6]
    kv_refs = refs[6:]
    me = lax.axis_index("ctx")
    rows = q_ref.shape[0]
    per_chip = rows // chips
    first = pltpu.make_async_copy(owner_hbm, owner_ref, in_sems.at[KVH])
    queries = []
    for head in range(KVH):
        wide = pl.ds(head * WIDE, WIDE)
        queries.append(pltpu.make_async_copy(q_hbm.at[:, wide], q_ref.at[:, wide], in_sems.at[head]))
    arrivals = []
    for index, (source, target) in enumerate(zip(kv_hbm, kv_refs)):
        arrivals.append(pltpu.make_async_copy(source, target, in_sems.at[KVH + 1 + index]))
    for copy in [first] + queries + arrivals:
        copy.start()
    first.wait()
    both = owner_ref[pl.ds(me // 2, 1), :]
    swapped = jnp.concatenate((both[:, rows:], both[:, :rows]), axis=1)
    own = jnp.where(me % 2 == 1, swapped, both)[:, :rows]
    token = lax.broadcasted_iota(jnp.int32, (1, rows), 1)
    key_row = own * rows + token
    rank = jnp.sum((row_to_column(key_row) < key_row).astype(jnp.int32), axis=0, keepdims=True)
    place = lax.broadcasted_iota(jnp.int32, (rows, rows), 0)
    order = (place == rank).astype(jnp.float32).astype(jnp.bfloat16)
    for copy in arrivals:
        copy.wait()
    departures = []
    for core in range(CORES):
        sorted_q = []
        for head in range(core * HEADS, (core + 1) * HEADS):
            queries[head].wait()
            wide = slice(head * WIDE, (head + 1) * WIDE)
            sorted_q.append(jnp.dot(order, q_ref[:, wide], preferred_element_type=jnp.float32))
        for chip in range(chips):
            dest = chip * CORES + core
            parts = []
            for array in sorted_q:
                parts.append(array[chip * per_chip : (chip + 1) * per_chip])
                if per_chip < SUB:
                    parts.append(jnp.zeros((SUB - per_chip, WIDE), jnp.float32))
            out_ref[dest, :Q_ROWS, :] = jnp.concatenate(parts, axis=0).astype(jnp.bfloat16)
            if with_kv:
                width = HEADS * HD
                side = slice(core * width, (core + 1) * width)
                half = rows // 2
                for part in range(2):
                    here = slice(part * half, (part + 1) * half)
                    for index in range(2):
                        col = (2 * part + index) * width
                        out_ref[dest, Q_ROWS:, col : col + width] = kv_refs[index][here, side]
            copy = pltpu.make_async_copy(out_ref.at[dest], out_hbm.at[dest], out_sems.at[dest])
            copy.start()
            departures.append(copy)
    for copy in departures:
        copy.wait()


def join_kernel(k_hbm, v_hbm, out_ref, sems):
    width = k_hbm.shape[1]
    copies = [
        pltpu.make_async_copy(k_hbm, out_ref.at[:, pl.ds(0, width)], sems.at[0]),
        pltpu.make_async_copy(v_hbm, out_ref.at[:, pl.ds(width, width)], sems.at[1]),
    ]
    for copy in copies:
        copy.start()
    for copy in copies:
        copy.wait()


def heads_kernel(*refs):
    lanes, outs = refs[:-CORES], refs[-CORES:]
    core = lax.axis_index("ctx") % CORES
    rows = lanes[0].shape[0]
    width = HEADS * HD
    for index in range(CORES):
        col = jnp.bitwise_xor(core, index) * width
        for lane, ref in enumerate(lanes):
            here = slice(lane * rows, (lane + 1) * rows)
            for half in range(2):
                side = pl.ds(pl.multiple_of(col + half * KVH * HD, width), width)
                outs[index][here, half * width : (half + 1) * width] = ref[:, side]


def place_kernel(per_chip, lengths_ref, owner_ref, pos_ref, start_ref, order_ref):
    me = lax.axis_index("ctx")
    chip, core = me // CORES, me % CORES
    table_rows = owner_ref.shape[0]
    total = table_rows * LANES
    held = pos_ref.shape[0]
    rows = LANES // 2
    shift = per_chip.bit_length() - 1
    block_rows = 32
    table_step = table_rows // (held // block_rows)
    first = lax.broadcasted_iota(jnp.int32, (LANES, LANES), 0)
    second = lax.broadcasted_iota(jnp.int32, (LANES, LANES), 1)
    same = (first < rows) == (second < rows)
    lane = lax.broadcasted_iota(jnp.int32, (1, LANES), 1)
    line = lax.broadcasted_iota(jnp.int32, (block_rows, 1), 0)
    wanted = chip * per_chip + jnp.bitwise_and(line, per_chip - 1)
    source = jnp.right_shift(line, shift)
    keys = []
    for block in range(held // block_rows):
        pos = jnp.zeros((block_rows, 1), jnp.int32)
        own = jnp.zeros((block_rows, 1), jnp.int32)
        for step in range(table_step):
            table = block * table_step + step
            owners = owner_ref[table : table + 1, :]
            key_row = owners * LANES + lane
            below = same & (row_to_column(key_row) < key_row)
            rank = jnp.sum(below.astype(jnp.int32), axis=0, keepdims=True)
            lane_source = 2 * step + (lane >= rows).astype(jnp.int32)
            hit = (wanted == rank) & (source == lane_source)
            pos += jnp.sum(jnp.where(hit, lane + table * LANES, 0), axis=1, keepdims=True)
            own += jnp.sum(jnp.where(hit, owners, 0), axis=1, keepdims=True)
        start = jnp.zeros((block_rows, 1), jnp.int32)
        end = jnp.int32(0)
        for rollout in range(lengths_ref.shape[0]):
            end = end + lengths_ref[rollout]
            start = jnp.where(pos >= end, end, start)
        here = slice(block * block_rows, (block + 1) * block_rows)
        pos_ref[here, :] = jnp.broadcast_to(pos, (block_rows, LANES))
        start_ref[here, :] = jnp.broadcast_to(start, (block_rows, LANES))
        keys.append((own - chip * CORES) * total + pos)
    key_col = jnp.concatenate(keys, axis=0)
    key_row = column_to_row(key_col)
    slot = jnp.sum((key_col < key_row).astype(jnp.int32), axis=0, keepdims=True)
    slot = jnp.bitwise_xor(slot, core * rows)
    place = lax.broadcasted_iota(jnp.int32, (held, held), 0)
    order_ref[...] = (place == slot).astype(jnp.float32).astype(jnp.bfloat16)


def unpack_moved(moved_ref, k_all, v_all):
    nodes = moved_ref.shape[0]
    tokens = k_all.shape[0] // nodes
    half = tokens // 2
    width = HEADS * HD

    def unpack(node, carry):
        for part in range(2):
            row = pl.ds(pl.multiple_of(node * tokens + part * half, half), half)
            col = 2 * part * width
            k_all[row, :] = moved_ref[node, Q_ROWS:, col : col + width]
            for head in range(HEADS):
                at = col + width + head * HD
                v_all[row, 2 * head * HD : (2 * head + 1) * HD] = moved_ref[node, Q_ROWS:, at : at + HD]
        return carry

    lax.fori_loop(0, nodes, unpack, 0)


def unpack_pieces(pieces, tokens, k_all, v_all):
    me = lax.axis_index("ctx")
    width = HEADS * HD
    for index, ref in enumerate(pieces):
        for lane in range(ref.shape[0] // tokens):
            node = jnp.bitwise_xor(me, index ^ (lane * len(pieces)))
            row = pl.ds(pl.multiple_of(node * tokens, tokens), tokens)
            here = slice(lane * tokens, (lane + 1) * tokens)
            k_all[row, :] = ref[here, :width]
            for head in range(HEADS):
                at = width + head * HD
                v_all[row, 2 * head * HD : (2 * head + 1) * HD] = ref[here, at : at + HD]


def attend_kernel(q_ref, pos_ref, start_ref, order_ref, *refs):
    kv_refs, refs = refs[: -CORES - 3], refs[-CORES - 3 :]
    out_refs, (k_all, v_all, context) = refs[:CORES], refs[CORES:]
    total = k_all.shape[0]
    held = context.shape[0]
    block_rows = 32
    blocks = held // block_rows
    span = total // blocks
    scale = math.log2(math.e) / math.sqrt(HD)

    for head in range(HEADS):
        v_all[:, (2 * head + 1) * HD : (2 * head + 2) * HD] = jnp.ones((total, HD), jnp.bfloat16)
    if len(kv_refs) == 1:
        unpack_moved(kv_refs[0], k_all, v_all)
    else:
        unpack_pieces(kv_refs, held // CORES, k_all, v_all)

    for block in range(blocks):
        here = slice(block * block_rows, (block + 1) * block_rows)
        parts = block_rows // SUB
        messages = [q_ref[block * parts + part].astype(jnp.float32) for part in range(parts)]
        pos = pos_ref[here, :1]
        start = start_ref[here, :1]
        low, high = max(0, block - blocks // 2) * span, (block + 1) * span
        chunk = min(high - low, 1024)
        for head in range(HEADS):
            pieces = []
            for group in range(GROUP):
                for message in messages:
                    rows = slice(head * SUB, (head + 1) * SUB)
                    pieces.append(message[rows, group * HD : (group + 1) * HD])
            queries = jnp.concatenate(pieces, axis=0).astype(jnp.bfloat16)
            peak, acc = None, None
            for lower in range(low, high, chunk):
                keys = slice(lower, lower + chunk)
                scores = lax.dot_general(
                    queries,
                    k_all[keys, head * HD : (head + 1) * HD],
                    (((1,), (1,)), ((), ())),
                    preferred_element_type=jnp.float32,
                )
                at = lower + lax.broadcasted_iota(jnp.int32, (block_rows, chunk), 1)
                seen = (at <= pos) & (at >= start)
                bias = jnp.where(seen, 0.0, NEGATIVE)
                scores = scores.reshape(GROUP, block_rows, chunk) + bias[None]
                scores = scores.reshape(GROUP * block_rows, chunk)
                top = jnp.max(scores, axis=1, keepdims=True)
                if peak is not None:
                    top = jnp.maximum(peak, top)
                probs = jnp.exp2((scores - top) * scale)
                if chunk != high - low:
                    probs = probs.reshape(GROUP, block_rows, chunk)
                    probs = jnp.where(seen[None], probs, 0.0).reshape(GROUP * block_rows, chunk)
                new = jnp.dot(
                    probs.astype(jnp.bfloat16),
                    v_all[keys, 2 * head * HD : (2 * head + 2) * HD],
                    preferred_element_type=jnp.float32,
                )
                acc = new if acc is None else acc * jnp.exp2((peak - top) * scale) + new
                peak = top
            result = (acc[:, :HD] / acc[:, HD:]).astype(jnp.bfloat16)
            for group in range(GROUP):
                col = head * WIDE + group * HD
                context[here, col : col + HD] = result[group * block_rows : (group + 1) * block_rows]
    rows = held // CORES
    for core in range(CORES):
        order = order_ref[core * rows : (core + 1) * rows, :]
        moved = jnp.dot(order, context[...], preferred_element_type=jnp.float32)
        out_refs[core][...] = moved.astype(jnp.bfloat16)


def assemble_kernel(*refs):
    core = lax.axis_index("ctx") % CORES
    width = HEADS * WIDE
    for index in range(CORES):
        col = pl.multiple_of(jnp.bitwise_xor(core, index) * width, width)
        refs[CORES][:, pl.ds(col, width)] = refs[index][...]


def on_device(queries, keys, values, owner, rollout_lengths):
    rows = queries.shape[0]
    nodes = lax.axis_size("ctx")
    total = owner.shape[0]
    chips = nodes // CORES
    per_chip = rows // chips
    held = rows * CORES
    table = owner.reshape(total // LANES, LANES)
    whole = pl.BlockSpec(memory_space=pltpu.VMEM)
    hbm = pl.BlockSpec(memory_space=pltpu.HBM)
    near = 4
    apart = nodes == 4 * near

    def swap(array, offset):
        return lax.ppermute(array, "ctx", [(node, node ^ offset) for node in range(nodes)])

    if apart:
        joined = pl.pallas_call(
            join_kernel,
            out_shape=jax.ShapeDtypeStruct((rows, 2 * KVH * HD), jnp.bfloat16),
            in_specs=[hbm] * 2,
            out_specs=whole,
            scratch_shapes=[pltpu.SemaphoreType.DMA((2,))],
            compiler_params=ALL_VMEM,
            name="join",
        )(keys, values)
        lanes = [joined] + [swap(joined, offset) for offset in range(near, nodes, near)]

    kv_rows = 0 if apart else rows // 2
    message = (nodes, Q_ROWS + kv_rows, WIDE)
    kv_scratch = [pltpu.VMEM(keys.shape, jnp.bfloat16), pltpu.VMEM(values.shape, jnp.bfloat16)]
    operands = (table, queries) if apart else (table, queries, keys, values)
    packed = pl.pallas_call(
        functools.partial(pack_kernel, chips),
        out_shape=jax.ShapeDtypeStruct(message, jnp.bfloat16),
        in_specs=[hbm] * len(operands),
        out_specs=hbm,
        scratch_shapes=[
            pltpu.VMEM(table.shape, jnp.int32),
            pltpu.VMEM(queries.shape, jnp.bfloat16),
            pltpu.VMEM(message, jnp.bfloat16),
            pltpu.SemaphoreType.DMA((KVH + 3,)),
            pltpu.SemaphoreType.DMA((nodes,)),
        ]
        + ([] if apart else kv_scratch),
        compiler_params=ALL_VMEM,
        cost_estimate=pl.CostEstimate(
            flops=2 * rows * rows * H * HD, bytes_accessed=4 * rows * H * HD, transcendentals=0
        ),
        name="pack",
    )(*operands)
    moved = lax.all_to_all(packed, "ctx", split_axis=0, concat_axis=0, tiled=True)

    if apart:
        mine, others = pl.pallas_call(
            heads_kernel,
            out_shape=(jax.ShapeDtypeStruct((near * rows, 2 * HEADS * HD), jnp.bfloat16),) * CORES,
            in_specs=[whole] * len(lanes),
            out_specs=(whole,) * CORES,
            compiler_params=VMEM,
            cost_estimate=pl.CostEstimate(
                flops=2 * 10**10, bytes_accessed=64 * 2**20, transcendentals=0
            ),
            name="heads",
        )(*lanes)
        kv_parts = [mine, swap(others, 1), swap(mine, 2), swap(others, 3)]
        q_part = moved
    else:
        kv_parts = [moved]
        groups = held // SUB
        q_part = moved[:, :Q_ROWS].reshape(groups, nodes // groups, HEADS, SUB, WIDE)[:, :, :, :per_chip]
        q_part = q_part.transpose(0, 2, 1, 3, 4).reshape(groups, Q_ROWS, WIDE)

    pos, start, order = pl.pallas_call(
        functools.partial(place_kernel, per_chip),
        out_shape=(
            jax.ShapeDtypeStruct((held, LANES), jnp.int32),
            jax.ShapeDtypeStruct((held, LANES), jnp.int32),
            jax.ShapeDtypeStruct((held, held), jnp.bfloat16),
        ),
        in_specs=[pl.BlockSpec(memory_space=pltpu.SMEM), whole],
        out_specs=(whole, whole, whole),
        compiler_params=VMEM,
        name="place",
    )(rollout_lengths, table)

    own, other = pl.pallas_call(
        attend_kernel,
        out_shape=(jax.ShapeDtypeStruct((rows, HEADS * WIDE), jnp.bfloat16),) * CORES,
        in_specs=[whole] * (4 + len(kv_parts)),
        out_specs=(whole,) * CORES,
        scratch_shapes=[
            pltpu.VMEM((total, HEADS * HD), jnp.bfloat16),
            pltpu.VMEM((total, HEADS * 2 * HD), jnp.bfloat16),
            pltpu.VMEM((held, HEADS * WIDE), jnp.bfloat16),
        ],
        compiler_params=VMEM,
        name="attend",
    )(q_part, pos, start, order, *kv_parts)

    return pl.pallas_call(
        assemble_kernel,
        out_shape=jax.ShapeDtypeStruct((rows, H * HD), jnp.bfloat16),
        in_specs=[whole] * CORES,
        out_specs=whole,
        compiler_params=VMEM,
        name="assemble",
    )(own, swap(other, 1))


def solution(mesh):
    placed = (
        P(("groups", "ctx"), None),
        P(("groups", "ctx"), None),
        P(("groups", "ctx"), None),
        P("groups"),
        P("groups"),
    )
    return jax.shard_map(
        on_device, mesh=mesh, in_specs=placed, out_specs=P(("groups", "ctx"), None), check_vma=False
    )
```

```python
import functools
import math

import jax
import jax.numpy as jnp
from jax import lax
from jax.experimental import pallas as pl
from jax.experimental.pallas import tpu as pltpu
from jax.sharding import PartitionSpec as P

H = 32
KVH = 4
HD = 128
GROUP = H // KVH
WIDE = GROUP * HD
CORES = 2
HEADS = KVH // CORES
NEGATIVE = -1e30
LANES = 128
SUB = 8
Q_ROWS = HEADS * SUB
VMEM = pltpu.CompilerParams(vmem_limit_bytes=40 * 2**20)
ALL_VMEM = pltpu.CompilerParams(vmem_limit_bytes=64 * 2**20 - 2**17)


def row_to_column(row):
    size = row.shape[1]
    here = lax.broadcasted_iota(jnp.int32, (size, size), 0)
    there = lax.broadcasted_iota(jnp.int32, (size, size), 1)
    return jnp.sum(jnp.where(here == there, row, 0), axis=1, keepdims=True)


def column_to_row(column):
    size = column.shape[0]
    here = lax.broadcasted_iota(jnp.int32, (size, size), 0)
    there = lax.broadcasted_iota(jnp.int32, (size, size), 1)
    return jnp.sum(jnp.where(here == there, column, 0), axis=0, keepdims=True)


def pack_kernel(chips, owner_hbm, q_hbm, *refs):
    with_kv = len(refs) > 6
    kv_hbm, refs = (refs[:2], refs[2:]) if with_kv else ((), refs)
    out_hbm, owner_ref, q_ref, out_ref, in_sems, out_sems = refs[:6]
    kv_refs = refs[6:]
    me = lax.axis_index("ctx")
    rows = q_ref.shape[0]
    per_chip = rows // chips
    first = pltpu.make_async_copy(owner_hbm, owner_ref, in_sems.at[KVH])
    queries = []
    for head in range(KVH):
        wide = pl.ds(head * WIDE, WIDE)
        queries.append(pltpu.make_async_copy(q_hbm.at[:, wide], q_ref.at[:, wide], in_sems.at[head]))
    arrivals = []
    for index, (source, target) in enumerate(zip(kv_hbm, kv_refs)):
        arrivals.append(pltpu.make_async_copy(source, target, in_sems.at[KVH + 1 + index]))
    for copy in [first] + queries + arrivals:
        copy.start()
    first.wait()
    both = owner_ref[pl.ds(me // 2, 1), :]
    swapped = jnp.concatenate((both[:, rows:], both[:, :rows]), axis=1)
    own = jnp.where(me % 2 == 1, swapped, both)[:, :rows]
    token = lax.broadcasted_iota(jnp.int32, (1, rows), 1)
    key_row = own * rows + token
    rank = jnp.sum((row_to_column(key_row) < key_row).astype(jnp.int32), axis=0, keepdims=True)
    place = lax.broadcasted_iota(jnp.int32, (rows, rows), 0)
    order = (place == rank).astype(jnp.float32).astype(jnp.bfloat16)
    for copy in arrivals:
        copy.wait()
    departures = []
    for core in range(CORES):
        sorted_q = []
        for head in range(core * HEADS, (core + 1) * HEADS):
            queries[head].wait()
            wide = slice(head * WIDE, (head + 1) * WIDE)
            sorted_q.append(jnp.dot(order, q_ref[:, wide], preferred_element_type=jnp.float32))
        for chip in range(chips):
            dest = chip * CORES + core
            parts = []
            for array in sorted_q:
                parts.append(array[chip * per_chip : (chip + 1) * per_chip])
                if per_chip < SUB:
                    parts.append(jnp.zeros((SUB - per_chip, WIDE), jnp.float32))
            out_ref[dest, :Q_ROWS, :] = jnp.concatenate(parts, axis=0).astype(jnp.bfloat16)
            if with_kv:
                width = HEADS * HD
                side = slice(core * width, (core + 1) * width)
                half = rows // 2
                for part in range(2):
                    here = slice(part * half, (part + 1) * half)
                    for index in range(2):
                        col = (2 * part + index) * width
                        out_ref[dest, Q_ROWS:, col : col + width] = kv_refs[index][here, side]
            copy = pltpu.make_async_copy(out_ref.at[dest], out_hbm.at[dest], out_sems.at[dest])
            copy.start()
            departures.append(copy)
    for copy in departures:
        copy.wait()


def block_offsets(nodes):
    return [0, CORES] + list(range(2 * CORES, nodes, 2 * CORES))


def join_kernel(k_hbm, v_hbm, out_ref, sems):
    width = k_hbm.shape[1]
    copies = [
        pltpu.make_async_copy(k_hbm, out_ref.at[:, pl.ds(0, width)], sems.at[0]),
        pltpu.make_async_copy(v_hbm, out_ref.at[:, pl.ds(width, width)], sems.at[1]),
    ]
    for copy in copies:
        copy.start()
    for copy in copies:
        copy.wait()


def heads_kernel(*refs):
    lanes, near, far = refs[: -2 * CORES], refs[-2 * CORES : -CORES], refs[-CORES:]
    core = lax.axis_index("ctx") % CORES
    rows = lanes[0].shape[0]
    width = HEADS * HD
    for index in range(CORES):
        col = jnp.bitwise_xor(core, index) * width
        for lane, ref in enumerate(lanes):
            for half in range(2):
                block = ref[:, pl.ds(pl.multiple_of(col + half * KVH * HD, width), width)]
                side = slice(half * width, (half + 1) * width)
                near[index][lane * rows : (lane + 1) * rows, side] = block
                if lane >= 2:
                    far[index][(lane - 2) * rows : (lane - 1) * rows, side] = block


def place_kernel(per_chip, lengths_ref, owner_ref, pos_ref, start_ref, order_ref):
    me = lax.axis_index("ctx")
    chip, core = me // CORES, me % CORES
    table_rows = owner_ref.shape[0]
    total = table_rows * LANES
    held = pos_ref.shape[0]
    rows = LANES // 2
    shift = per_chip.bit_length() - 1
    block_rows = 32
    table_step = table_rows // (held // block_rows)
    first = lax.broadcasted_iota(jnp.int32, (LANES, LANES), 0)
    second = lax.broadcasted_iota(jnp.int32, (LANES, LANES), 1)
    same = (first < rows) == (second < rows)
    lane = lax.broadcasted_iota(jnp.int32, (1, LANES), 1)
    line = lax.broadcasted_iota(jnp.int32, (block_rows, 1), 0)
    wanted = chip * per_chip + jnp.bitwise_and(line, per_chip - 1)
    source = jnp.right_shift(line, shift)
    keys = []
    for block in range(held // block_rows):
        pos = jnp.zeros((block_rows, 1), jnp.int32)
        own = jnp.zeros((block_rows, 1), jnp.int32)
        for step in range(table_step):
            table = block * table_step + step
            owners = owner_ref[table : table + 1, :]
            key_row = owners * LANES + lane
            below = same & (row_to_column(key_row) < key_row)
            rank = jnp.sum(below.astype(jnp.int32), axis=0, keepdims=True)
            lane_source = 2 * step + (lane >= rows).astype(jnp.int32)
            hit = (wanted == rank) & (source == lane_source)
            pos += jnp.sum(jnp.where(hit, lane + table * LANES, 0), axis=1, keepdims=True)
            own += jnp.sum(jnp.where(hit, owners, 0), axis=1, keepdims=True)
        start = jnp.zeros((block_rows, 1), jnp.int32)
        end = jnp.int32(0)
        for rollout in range(lengths_ref.shape[0]):
            end = end + lengths_ref[rollout]
            start = jnp.where(pos >= end, end, start)
        here = slice(block * block_rows, (block + 1) * block_rows)
        pos_ref[here, :] = jnp.broadcast_to(pos, (block_rows, LANES))
        start_ref[here, :] = jnp.broadcast_to(start, (block_rows, LANES))
        keys.append((own - chip * CORES) * total + pos)
    key_col = jnp.concatenate(keys, axis=0)
    key_row = column_to_row(key_col)
    slot = jnp.sum((key_col < key_row).astype(jnp.int32), axis=0, keepdims=True)
    slot = jnp.bitwise_xor(slot, core * rows)
    place = lax.broadcasted_iota(jnp.int32, (held, held), 0)
    order_ref[...] = (place == slot).astype(jnp.float32).astype(jnp.bfloat16)


def unpack_moved(moved_ref, k_all, v_all):
    nodes = moved_ref.shape[0]
    tokens = k_all.shape[0] // nodes
    half = tokens // 2
    width = HEADS * HD

    def unpack(node, carry):
        for part in range(2):
            row = pl.ds(pl.multiple_of(node * tokens + part * half, half), half)
            col = 2 * part * width
            k_all[row, :] = moved_ref[node, Q_ROWS:, col : col + width]
            for head in range(HEADS):
                at = col + width + head * HD
                v_all[row, 2 * head * HD : (2 * head + 1) * HD] = moved_ref[node, Q_ROWS:, at : at + HD]
        return carry

    lax.fori_loop(0, nodes, unpack, 0)


def unpack_pieces(pieces, tokens, k_all, v_all):
    me = lax.axis_index("ctx")
    offsets = block_offsets(k_all.shape[0] // tokens)
    width = HEADS * HD
    for index, ref in enumerate(pieces):
        held = offsets if index < CORES else offsets[2:]
        for lane, offset in enumerate(held):
            node = jnp.bitwise_xor(me, index ^ offset)
            row = pl.ds(pl.multiple_of(node * tokens, tokens), tokens)
            here = slice(lane * tokens, (lane + 1) * tokens)
            k_all[row, :] = ref[here, :width]
            for head in range(HEADS):
                at = width + head * HD
                v_all[row, 2 * head * HD : (2 * head + 1) * HD] = ref[here, at : at + HD]


def attend_kernel(q_ref, pos_ref, start_ref, order_ref, *refs):
    kv_refs, refs = refs[: -CORES - 3], refs[-CORES - 3 :]
    out_refs, (k_all, v_all, context) = refs[:CORES], refs[CORES:]
    total = k_all.shape[0]
    held = context.shape[0]
    block_rows = 32
    blocks = held // block_rows
    span = total // blocks
    scale = math.log2(math.e) / math.sqrt(HD)

    for head in range(HEADS):
        v_all[:, (2 * head + 1) * HD : (2 * head + 2) * HD] = jnp.ones((total, HD), jnp.bfloat16)
    if len(kv_refs) == 1:
        unpack_moved(kv_refs[0], k_all, v_all)
    else:
        unpack_pieces(kv_refs, held // CORES, k_all, v_all)

    for block in range(blocks):
        here = slice(block * block_rows, (block + 1) * block_rows)
        parts = block_rows // SUB
        messages = [q_ref[block * parts + part].astype(jnp.float32) for part in range(parts)]
        pos = pos_ref[here, :1]
        start = start_ref[here, :1]
        low, high = max(0, block - blocks // 2) * span, (block + 1) * span
        chunk = min(high - low, 1024)
        for head in range(HEADS):
            pieces = []
            for group in range(GROUP):
                for message in messages:
                    rows = slice(head * SUB, (head + 1) * SUB)
                    pieces.append(message[rows, group * HD : (group + 1) * HD])
            queries = jnp.concatenate(pieces, axis=0).astype(jnp.bfloat16)
            peak, acc = None, None
            for lower in range(low, high, chunk):
                keys = slice(lower, lower + chunk)
                scores = lax.dot_general(
                    queries,
                    k_all[keys, head * HD : (head + 1) * HD],
                    (((1,), (1,)), ((), ())),
                    preferred_element_type=jnp.float32,
                )
                at = lower + lax.broadcasted_iota(jnp.int32, (block_rows, chunk), 1)
                seen = (at <= pos) & (at >= start)
                bias = jnp.where(seen, 0.0, NEGATIVE)
                scores = scores.reshape(GROUP, block_rows, chunk) + bias[None]
                scores = scores.reshape(GROUP * block_rows, chunk)
                top = jnp.max(scores, axis=1, keepdims=True)
                if peak is not None:
                    top = jnp.maximum(peak, top)
                probs = jnp.exp2((scores - top) * scale)
                if chunk != high - low:
                    probs = probs.reshape(GROUP, block_rows, chunk)
                    probs = jnp.where(seen[None], probs, 0.0).reshape(GROUP * block_rows, chunk)
                new = jnp.dot(
                    probs.astype(jnp.bfloat16),
                    v_all[keys, 2 * head * HD : (2 * head + 2) * HD],
                    preferred_element_type=jnp.float32,
                )
                acc = new if acc is None else acc * jnp.exp2((peak - top) * scale) + new
                peak = top
            result = (acc[:, :HD] / acc[:, HD:]).astype(jnp.bfloat16)
            for group in range(GROUP):
                col = head * WIDE + group * HD
                context[here, col : col + HD] = result[group * block_rows : (group + 1) * block_rows]
    rows = held // CORES
    for core in range(CORES):
        order = order_ref[core * rows : (core + 1) * rows, :]
        moved = jnp.dot(order, context[...], preferred_element_type=jnp.float32)
        out_refs[core][...] = moved.astype(jnp.bfloat16)


def assemble_kernel(*refs):
    core = lax.axis_index("ctx") % CORES
    width = HEADS * WIDE
    for index in range(CORES):
        col = pl.multiple_of(jnp.bitwise_xor(core, index) * width, width)
        refs[CORES][:, pl.ds(col, width)] = refs[index][...]


def on_device(queries, keys, values, owner, rollout_lengths):
    rows = queries.shape[0]
    nodes = lax.axis_size("ctx")
    total = owner.shape[0]
    chips = nodes // CORES
    per_chip = rows // chips
    held = rows * CORES
    table = owner.reshape(total // LANES, LANES)
    whole = pl.BlockSpec(memory_space=pltpu.VMEM)
    hbm = pl.BlockSpec(memory_space=pltpu.HBM)
    apart = nodes == 16

    def swap(array, offset):
        return lax.ppermute(array, "ctx", [(node, node ^ offset) for node in range(nodes)])

    if apart:
        joined = pl.pallas_call(
            join_kernel,
            out_shape=jax.ShapeDtypeStruct((rows, 2 * KVH * HD), jnp.bfloat16),
            in_specs=[hbm] * 2,
            out_specs=whole,
            scratch_shapes=[pltpu.SemaphoreType.DMA((2,))],
            compiler_params=ALL_VMEM,
            name="join",
        )(keys, values)
        offsets = block_offsets(nodes)
        lanes = [joined] + [swap(joined, offset) for offset in offsets[1:]]

    kv_rows = 0 if apart else rows // 2
    message = (nodes, Q_ROWS + kv_rows, WIDE)
    kv_scratch = [pltpu.VMEM(keys.shape, jnp.bfloat16), pltpu.VMEM(values.shape, jnp.bfloat16)]
    operands = (table, queries) if apart else (table, queries, keys, values)
    packed = pl.pallas_call(
        functools.partial(pack_kernel, chips),
        out_shape=jax.ShapeDtypeStruct(message, jnp.bfloat16),
        in_specs=[hbm] * len(operands),
        out_specs=hbm,
        scratch_shapes=[
            pltpu.VMEM(table.shape, jnp.int32),
            pltpu.VMEM(queries.shape, jnp.bfloat16),
            pltpu.VMEM(message, jnp.bfloat16),
            pltpu.SemaphoreType.DMA((KVH + 3,)),
            pltpu.SemaphoreType.DMA((nodes,)),
        ]
        + ([] if apart else kv_scratch),
        compiler_params=ALL_VMEM,
        cost_estimate=pl.CostEstimate(
            flops=2 * rows * rows * H * HD, bytes_accessed=4 * rows * H * HD, transcendentals=0
        ),
        name="pack",
    )(*operands)
    moved = lax.all_to_all(packed, "ctx", split_axis=0, concat_axis=0, tiled=True)

    if apart:
        near, far = len(lanes) * rows, (len(lanes) - 2) * rows
        pieces = pl.pallas_call(
            heads_kernel,
            out_shape=[
                jax.ShapeDtypeStruct((count, 2 * HEADS * HD), jnp.bfloat16)
                for count in (near, near, far, far)
            ],
            in_specs=[whole] * len(lanes),
            out_specs=[whole] * (2 * CORES),
            compiler_params=VMEM,
            cost_estimate=pl.CostEstimate(
                flops=2 * 10**10, bytes_accessed=64 * 2**20, transcendentals=0
            ),
            name="heads",
        )(*lanes)
        kv_parts = [swap(piece, index) if index else piece for index, piece in enumerate(pieces)]
        q_part = moved
    else:
        kv_parts = [moved]
        groups = held // SUB
        q_part = moved[:, :Q_ROWS].reshape(groups, nodes // groups, HEADS, SUB, WIDE)[:, :, :, :per_chip]
        q_part = q_part.transpose(0, 2, 1, 3, 4).reshape(groups, Q_ROWS, WIDE)

    pos, start, order = pl.pallas_call(
        functools.partial(place_kernel, per_chip),
        out_shape=(
            jax.ShapeDtypeStruct((held, LANES), jnp.int32),
            jax.ShapeDtypeStruct((held, LANES), jnp.int32),
            jax.ShapeDtypeStruct((held, held), jnp.bfloat16),
        ),
        in_specs=[pl.BlockSpec(memory_space=pltpu.SMEM), whole],
        out_specs=(whole, whole, whole),
        compiler_params=VMEM,
        name="place",
    )(rollout_lengths, table)

    own, other = pl.pallas_call(
        attend_kernel,
        out_shape=(jax.ShapeDtypeStruct((rows, HEADS * WIDE), jnp.bfloat16),) * CORES,
        in_specs=[whole] * (4 + len(kv_parts)),
        out_specs=(whole,) * CORES,
        scratch_shapes=[
            pltpu.VMEM((total, HEADS * HD), jnp.bfloat16),
            pltpu.VMEM((total, HEADS * 2 * HD), jnp.bfloat16),
            pltpu.VMEM((held, HEADS * WIDE), jnp.bfloat16),
        ],
        compiler_params=VMEM,
        name="attend",
    )(q_part, pos, start, order, *kv_parts)

    return pl.pallas_call(
        assemble_kernel,
        out_shape=jax.ShapeDtypeStruct((rows, H * HD), jnp.bfloat16),
        in_specs=[whole] * CORES,
        out_specs=whole,
        compiler_params=VMEM,
        name="assemble",
    )(own, swap(other, 1))


def solution(mesh):
    placed = (
        P(("groups", "ctx"), None),
        P(("groups", "ctx"), None),
        P(("groups", "ctx"), None),
        P("groups"),
        P("groups"),
    )
    return jax.shard_map(
        on_device, mesh=mesh, in_specs=placed, out_specs=P(("groups", "ctx"), None), check_vma=False
    )
```

```python
import functools
import math

import jax
import jax.numpy as jnp
from jax import lax
from jax.experimental import pallas as pl
from jax.experimental.pallas import tpu as pltpu
from jax.sharding import PartitionSpec as P

H = 32
KVH = 4
HD = 128
GROUP = H // KVH
WIDE = GROUP * HD
CORES = 2
HEADS = KVH // CORES
NEGATIVE = -1e30
LANES = 128
SUB = 8
Q_ROWS = HEADS * SUB
VMEM = pltpu.CompilerParams(vmem_limit_bytes=40 * 2**20)
ALL_VMEM = pltpu.CompilerParams(vmem_limit_bytes=64 * 2**20 - 2**17)


def row_to_column(row):
    size = row.shape[1]
    here = lax.broadcasted_iota(jnp.int32, (size, size), 0)
    there = lax.broadcasted_iota(jnp.int32, (size, size), 1)
    return jnp.sum(jnp.where(here == there, row, 0), axis=1, keepdims=True)


def column_to_row(column):
    size = column.shape[0]
    here = lax.broadcasted_iota(jnp.int32, (size, size), 0)
    there = lax.broadcasted_iota(jnp.int32, (size, size), 1)
    return jnp.sum(jnp.where(here == there, column, 0), axis=0, keepdims=True)


def pack_kernel(chips, owner_ref, q_ref, *refs):
    kv_refs, out_ref = refs[:-1], refs[-1]
    me = lax.axis_index("ctx")
    rows = q_ref.shape[0]
    per_chip = rows // chips
    both = owner_ref[pl.ds(me // 2, 1), :]
    swapped = jnp.concatenate((both[:, rows:], both[:, :rows]), axis=1)
    own = jnp.where(me % 2 == 1, swapped, both)[:, :rows]
    token = lax.broadcasted_iota(jnp.int32, (1, rows), 1)
    key_row = own * rows + token
    rank = jnp.sum((row_to_column(key_row) < key_row).astype(jnp.int32), axis=0, keepdims=True)
    place = lax.broadcasted_iota(jnp.int32, (rows, rows), 0)
    order = (place == rank).astype(jnp.float32).astype(jnp.bfloat16)
    for core in range(CORES):
        sorted_q = []
        for head in range(core * HEADS, (core + 1) * HEADS):
            wide = slice(head * WIDE, (head + 1) * WIDE)
            sorted_q.append(jnp.dot(order, q_ref[:, wide], preferred_element_type=jnp.float32))
        for chip in range(chips):
            dest = chip * CORES + core
            parts = []
            for array in sorted_q:
                parts.append(array[chip * per_chip : (chip + 1) * per_chip])
                if per_chip < SUB:
                    parts.append(jnp.zeros((SUB - per_chip, WIDE), jnp.float32))
            out_ref[dest, :Q_ROWS, :] = jnp.concatenate(parts, axis=0).astype(jnp.bfloat16)
            if kv_refs:
                width = HEADS * HD
                side = slice(core * width, (core + 1) * width)
                half = rows // 2
                for part in range(2):
                    here = slice(part * half, (part + 1) * half)
                    for index in range(2):
                        col = (2 * part + index) * width
                        out_ref[dest, Q_ROWS:, col : col + width] = kv_refs[index][here, side]


def block_offsets(nodes):
    return [0, CORES, 2 * CORES, 3 * CORES] + list(range(4 * CORES, nodes, 2 * CORES))


def join_kernel(k_hbm, v_hbm, out_ref, sems):
    width = k_hbm.shape[1]
    copies = [
        pltpu.make_async_copy(k_hbm, out_ref.at[:, pl.ds(0, width)], sems.at[0]),
        pltpu.make_async_copy(v_hbm, out_ref.at[:, pl.ds(width, width)], sems.at[1]),
    ]
    for copy in copies:
        copy.start()
    for copy in copies:
        copy.wait()


def heads_kernel(*refs):
    lanes, near, far = refs[: -2 * CORES], refs[-2 * CORES : -CORES], refs[-CORES:]
    core = lax.axis_index("ctx") % CORES
    rows = lanes[0].shape[0]
    width = HEADS * HD
    for index in range(CORES):
        col = jnp.bitwise_xor(core, index) * width
        for lane, ref in enumerate(lanes):
            for half in range(2):
                block = ref[:, pl.ds(pl.multiple_of(col + half * KVH * HD, width), width)]
                side = slice(half * width, (half + 1) * width)
                near[index][lane * rows : (lane + 1) * rows, side] = block
                if lane >= 4:
                    far[index][(lane - 4) * rows : (lane - 3) * rows, side] = block


def place_kernel(per_chip, lengths_ref, owner_ref, pos_ref, start_ref, order_ref):
    me = lax.axis_index("ctx")
    chip, core = me // CORES, me % CORES
    table_rows = owner_ref.shape[0]
    total = table_rows * LANES
    held = pos_ref.shape[0]
    rows = LANES // 2
    shift = per_chip.bit_length() - 1
    block_rows = 32
    table_step = table_rows // (held // block_rows)
    first = lax.broadcasted_iota(jnp.int32, (LANES, LANES), 0)
    second = lax.broadcasted_iota(jnp.int32, (LANES, LANES), 1)
    same = (first < rows) == (second < rows)
    lane = lax.broadcasted_iota(jnp.int32, (1, LANES), 1)
    line = lax.broadcasted_iota(jnp.int32, (block_rows, 1), 0)
    wanted = chip * per_chip + jnp.bitwise_and(line, per_chip - 1)
    source = jnp.right_shift(line, shift)
    keys = []
    for block in range(held // block_rows):
        pos = jnp.zeros((block_rows, 1), jnp.int32)
        own = jnp.zeros((block_rows, 1), jnp.int32)
        for step in range(table_step):
            table = block * table_step + step
            owners = owner_ref[table : table + 1, :]
            key_row = owners * LANES + lane
            below = same & (row_to_column(key_row) < key_row)
            rank = jnp.sum(below.astype(jnp.int32), axis=0, keepdims=True)
            lane_source = 2 * step + (lane >= rows).astype(jnp.int32)
            hit = (wanted == rank) & (source == lane_source)
            pos += jnp.sum(jnp.where(hit, lane + table * LANES, 0), axis=1, keepdims=True)
            own += jnp.sum(jnp.where(hit, owners, 0), axis=1, keepdims=True)
        start = jnp.zeros((block_rows, 1), jnp.int32)
        end = jnp.int32(0)
        for rollout in range(lengths_ref.shape[0]):
            end = end + lengths_ref[rollout]
            start = jnp.where(pos >= end, end, start)
        here = slice(block * block_rows, (block + 1) * block_rows)
        pos_ref[here, :] = jnp.broadcast_to(pos, (block_rows, LANES))
        start_ref[here, :] = jnp.broadcast_to(start, (block_rows, LANES))
        keys.append((own - chip * CORES) * total + pos)
    key_col = jnp.concatenate(keys, axis=0)
    key_row = column_to_row(key_col)
    slot = jnp.sum((key_col < key_row).astype(jnp.int32), axis=0, keepdims=True)
    slot = jnp.bitwise_xor(slot, core * rows)
    place = lax.broadcasted_iota(jnp.int32, (held, held), 0)
    order_ref[...] = (place == slot).astype(jnp.float32).astype(jnp.bfloat16)


def unpack_moved(moved_ref, k_all, v_all):
    nodes = moved_ref.shape[0]
    tokens = k_all.shape[0] // nodes
    half = tokens // 2
    width = HEADS * HD

    def unpack(node, carry):
        for part in range(2):
            row = pl.ds(pl.multiple_of(node * tokens + part * half, half), half)
            col = 2 * part * width
            k_all[row, :] = moved_ref[node, Q_ROWS:, col : col + width]
            for head in range(HEADS):
                at = col + width + head * HD
                v_all[row, 2 * head * HD : (2 * head + 1) * HD] = moved_ref[node, Q_ROWS:, at : at + HD]
        return carry

    lax.fori_loop(0, nodes, unpack, 0)


def unpack_pieces(pieces, tokens, k_all, v_all):
    me = lax.axis_index("ctx")
    offsets = block_offsets(k_all.shape[0] // tokens)
    width = HEADS * HD
    for index, ref in enumerate(pieces):
        held = offsets if index < CORES else offsets[4:]
        for lane, offset in enumerate(held):
            node = jnp.bitwise_xor(me, index ^ offset)
            row = pl.ds(pl.multiple_of(node * tokens, tokens), tokens)
            here = slice(lane * tokens, (lane + 1) * tokens)
            k_all[row, :] = ref[here, :width]
            for head in range(HEADS):
                at = width + head * HD
                v_all[row, 2 * head * HD : (2 * head + 1) * HD] = ref[here, at : at + HD]


def attend_kernel(q_ref, pos_ref, start_ref, order_ref, *refs):
    kv_refs, refs = refs[: -CORES - 3], refs[-CORES - 3 :]
    out_refs, (k_all, v_all, context) = refs[:CORES], refs[CORES:]
    total = k_all.shape[0]
    held = context.shape[0]
    block_rows = 32
    blocks = held // block_rows
    span = total // blocks
    scale = math.log2(math.e) / math.sqrt(HD)

    for head in range(HEADS):
        v_all[:, (2 * head + 1) * HD : (2 * head + 2) * HD] = jnp.ones((total, HD), jnp.bfloat16)
    if len(kv_refs) == 1:
        unpack_moved(kv_refs[0], k_all, v_all)
    else:
        unpack_pieces(kv_refs, held // CORES, k_all, v_all)

    for block in range(blocks):
        here = slice(block * block_rows, (block + 1) * block_rows)
        parts = block_rows // SUB
        messages = [q_ref[block * parts + part].astype(jnp.float32) for part in range(parts)]
        pos = pos_ref[here, :1]
        start = start_ref[here, :1]
        low, high = max(0, block - blocks // 2) * span, (block + 1) * span
        chunk = min(high - low, 1024)
        for head in range(HEADS):
            pieces = []
            for group in range(GROUP):
                for message in messages:
                    rows = slice(head * SUB, (head + 1) * SUB)
                    pieces.append(message[rows, group * HD : (group + 1) * HD])
            queries = jnp.concatenate(pieces, axis=0).astype(jnp.bfloat16)
            peak, acc = None, None
            for lower in range(low, high, chunk):
                keys = slice(lower, lower + chunk)
                scores = lax.dot_general(
                    queries,
                    k_all[keys, head * HD : (head + 1) * HD],
                    (((1,), (1,)), ((), ())),
                    preferred_element_type=jnp.float32,
                )
                at = lower + lax.broadcasted_iota(jnp.int32, (block_rows, chunk), 1)
                seen = (at <= pos) & (at >= start)
                bias = jnp.where(seen, 0.0, NEGATIVE)
                scores = scores.reshape(GROUP, block_rows, chunk) + bias[None]
                scores = scores.reshape(GROUP * block_rows, chunk)
                top = jnp.max(scores, axis=1, keepdims=True)
                if peak is not None:
                    top = jnp.maximum(peak, top)
                probs = jnp.exp2((scores - top) * scale)
                if chunk != high - low:
                    probs = probs.reshape(GROUP, block_rows, chunk)
                    probs = jnp.where(seen[None], probs, 0.0).reshape(GROUP * block_rows, chunk)
                new = jnp.dot(
                    probs.astype(jnp.bfloat16),
                    v_all[keys, 2 * head * HD : (2 * head + 2) * HD],
                    preferred_element_type=jnp.float32,
                )
                acc = new if acc is None else acc * jnp.exp2((peak - top) * scale) + new
                peak = top
            result = (acc[:, :HD] / acc[:, HD:]).astype(jnp.bfloat16)
            for group in range(GROUP):
                col = head * WIDE + group * HD
                context[here, col : col + HD] = result[group * block_rows : (group + 1) * block_rows]
    rows = held // CORES
    for core in range(CORES):
        order = order_ref[core * rows : (core + 1) * rows, :]
        moved = jnp.dot(order, context[...], preferred_element_type=jnp.float32)
        out_refs[core][...] = moved.astype(jnp.bfloat16)


def assemble_kernel(*refs):
    core = lax.axis_index("ctx") % CORES
    width = HEADS * WIDE
    for index in range(CORES):
        col = pl.multiple_of(jnp.bitwise_xor(core, index) * width, width)
        refs[CORES][:, pl.ds(col, width)] = refs[index][...]


def on_device(queries, keys, values, owner, rollout_lengths):
    rows = queries.shape[0]
    nodes = lax.axis_size("ctx")
    total = owner.shape[0]
    chips = nodes // CORES
    per_chip = rows // chips
    held = rows * CORES
    table = owner.reshape(total // LANES, LANES)
    whole = pl.BlockSpec(memory_space=pltpu.VMEM)
    hbm = pl.BlockSpec(memory_space=pltpu.HBM)
    apart = nodes == 16

    def swap(array, offset):
        return lax.ppermute(array, "ctx", [(node, node ^ offset) for node in range(nodes)])

    if apart:
        joined = pl.pallas_call(
            join_kernel,
            out_shape=jax.ShapeDtypeStruct((rows, 2 * KVH * HD), jnp.bfloat16),
            in_specs=[hbm] * 2,
            out_specs=whole,
            scratch_shapes=[pltpu.SemaphoreType.DMA((2,))],
            compiler_params=ALL_VMEM,
            name="join",
        )(keys, values)
        offsets = block_offsets(nodes)
        lanes = [joined] + [swap(joined, offset) for offset in offsets[1:]]

    kv_rows = 0 if apart else rows // 2
    message = (nodes, Q_ROWS + kv_rows, WIDE)
    operands = (table, queries) if apart else (table, queries, keys, values)
    packed = pl.pallas_call(
        functools.partial(pack_kernel, chips),
        out_shape=jax.ShapeDtypeStruct(message, jnp.bfloat16),
        in_specs=[whole] * len(operands),
        out_specs=whole,
        compiler_params=VMEM,
        cost_estimate=pl.CostEstimate(
            flops=2 * rows * rows * H * HD, bytes_accessed=4 * rows * H * HD, transcendentals=0
        ),
        name="pack",
    )(*operands)
    moved = lax.all_to_all(packed, "ctx", split_axis=0, concat_axis=0, tiled=True)

    if apart:
        near, far = len(lanes) * rows, (len(lanes) - 4) * rows
        pieces = pl.pallas_call(
            heads_kernel,
            out_shape=[
                jax.ShapeDtypeStruct((count, 2 * HEADS * HD), jnp.bfloat16)
                for count in (near, near, far, far)
            ],
            in_specs=[whole] * len(lanes),
            out_specs=[whole] * (2 * CORES),
            compiler_params=VMEM,
            cost_estimate=pl.CostEstimate(
                flops=2 * 10**10, bytes_accessed=64 * 2**20, transcendentals=0
            ),
            name="heads",
        )(*lanes)
        kv_parts = [swap(piece, index) if index else piece for index, piece in enumerate(pieces)]
        q_part = moved
    else:
        kv_parts = [moved]
        groups = held // SUB
        q_part = moved[:, :Q_ROWS].reshape(groups, nodes // groups, HEADS, SUB, WIDE)[:, :, :, :per_chip]
        q_part = q_part.transpose(0, 2, 1, 3, 4).reshape(groups, Q_ROWS, WIDE)

    pos, start, order = pl.pallas_call(
        functools.partial(place_kernel, per_chip),
        out_shape=(
            jax.ShapeDtypeStruct((held, LANES), jnp.int32),
            jax.ShapeDtypeStruct((held, LANES), jnp.int32),
            jax.ShapeDtypeStruct((held, held), jnp.bfloat16),
        ),
        in_specs=[pl.BlockSpec(memory_space=pltpu.SMEM), whole],
        out_specs=(whole, whole, whole),
        compiler_params=VMEM,
        name="place",
    )(rollout_lengths, table)

    own, other = pl.pallas_call(
        attend_kernel,
        out_shape=(jax.ShapeDtypeStruct((rows, HEADS * WIDE), jnp.bfloat16),) * CORES,
        in_specs=[whole] * (4 + len(kv_parts)),
        out_specs=(whole,) * CORES,
        scratch_shapes=[
            pltpu.VMEM((total, HEADS * HD), jnp.bfloat16),
            pltpu.VMEM((total, HEADS * 2 * HD), jnp.bfloat16),
            pltpu.VMEM((held, HEADS * WIDE), jnp.bfloat16),
        ],
        compiler_params=VMEM,
        name="attend",
    )(q_part, pos, start, order, *kv_parts)

    return pl.pallas_call(
        assemble_kernel,
        out_shape=jax.ShapeDtypeStruct((rows, H * HD), jnp.bfloat16),
        in_specs=[whole] * CORES,
        out_specs=whole,
        compiler_params=VMEM,
        name="assemble",
    )(own, swap(other, 1))


def solution(mesh):
    placed = (
        P(("groups", "ctx"), None),
        P(("groups", "ctx"), None),
        P(("groups", "ctx"), None),
        P("groups"),
        P("groups"),
    )
    return jax.shard_map(
        on_device, mesh=mesh, in_specs=placed, out_specs=P(("groups", "ctx"), None), check_vma=False
    )
```

```python
import functools
import math

import jax
import jax.numpy as jnp
from jax import lax
from jax.experimental import pallas as pl
from jax.experimental.pallas import tpu as pltpu
from jax.sharding import PartitionSpec as P

H = 32
KVH = 4
HD = 128
GROUP = H // KVH
WIDE = GROUP * HD
CORES = 2
HEADS = KVH // CORES
NEGATIVE = -1e30
LANES = 128
SUB = 8
Q_ROWS = HEADS * SUB
VMEM = pltpu.CompilerParams(vmem_limit_bytes=40 * 2**20)
ALL_VMEM = pltpu.CompilerParams(vmem_limit_bytes=64 * 2**20 - 2**17)


def row_to_column(row):
    size = row.shape[1]
    here = lax.broadcasted_iota(jnp.int32, (size, size), 0)
    there = lax.broadcasted_iota(jnp.int32, (size, size), 1)
    return jnp.sum(jnp.where(here == there, row, 0), axis=1, keepdims=True)


def column_to_row(column):
    size = column.shape[0]
    here = lax.broadcasted_iota(jnp.int32, (size, size), 0)
    there = lax.broadcasted_iota(jnp.int32, (size, size), 1)
    return jnp.sum(jnp.where(here == there, column, 0), axis=0, keepdims=True)


def pack_kernel(chips, owner_ref, q_ref, *refs):
    kv_refs, out_ref = refs[:-1], refs[-1]
    me = lax.axis_index("ctx")
    rows = q_ref.shape[0]
    per_chip = rows // chips
    both = owner_ref[pl.ds(me // 2, 1), :]
    swapped = jnp.concatenate((both[:, rows:], both[:, :rows]), axis=1)
    own = jnp.where(me % 2 == 1, swapped, both)[:, :rows]
    token = lax.broadcasted_iota(jnp.int32, (1, rows), 1)
    key_row = own * rows + token
    rank = jnp.sum((row_to_column(key_row) < key_row).astype(jnp.int32), axis=0, keepdims=True)
    place = lax.broadcasted_iota(jnp.int32, (rows, rows), 0)
    order = (place == rank).astype(jnp.float32).astype(jnp.bfloat16)
    for core in range(CORES):
        sorted_q = []
        for head in range(core * HEADS, (core + 1) * HEADS):
            wide = slice(head * WIDE, (head + 1) * WIDE)
            sorted_q.append(jnp.dot(order, q_ref[:, wide], preferred_element_type=jnp.float32))
        for chip in range(chips):
            dest = chip * CORES + core
            parts = []
            for array in sorted_q:
                parts.append(array[chip * per_chip : (chip + 1) * per_chip])
                if per_chip < SUB:
                    parts.append(jnp.zeros((SUB - per_chip, WIDE), jnp.float32))
            out_ref[dest, :Q_ROWS, :] = jnp.concatenate(parts, axis=0).astype(jnp.bfloat16)
            if kv_refs:
                width = HEADS * HD
                side = slice(core * width, (core + 1) * width)
                half = rows // 2
                for part in range(2):
                    here = slice(part * half, (part + 1) * half)
                    for index in range(2):
                        col = (2 * part + index) * width
                        out_ref[dest, Q_ROWS:, col : col + width] = kv_refs[index][here, side]


def fetch_kernel(q_hbm, k_hbm, v_hbm, q_ref, kv_ref, sems):
    width = k_hbm.shape[1]
    copies = [
        pltpu.make_async_copy(k_hbm, kv_ref.at[:, pl.ds(0, width)], sems.at[0]),
        pltpu.make_async_copy(v_hbm, kv_ref.at[:, pl.ds(width, width)], sems.at[1]),
        pltpu.make_async_copy(q_hbm, q_ref, sems.at[2]),
    ]
    for copy in copies:
        copy.start()
    for copy in copies:
        copy.wait()


def block_offsets(nodes):
    return list(range(nodes - 2 * CORES, 3 * CORES, -2 * CORES)) + [3 * CORES, 2 * CORES, CORES, 0]


def heads_kernel(*refs):
    lanes, near, far = refs[: -2 * CORES], refs[-2 * CORES : -CORES], refs[-CORES:]
    core = lax.axis_index("ctx") % CORES
    rows = lanes[0].shape[0]
    width = HEADS * HD
    for index in range(CORES):
        col = jnp.bitwise_xor(core, index) * width
        for lane, ref in enumerate(lanes):
            for half in range(2):
                block = ref[:, pl.ds(pl.multiple_of(col + half * KVH * HD, width), width)]
                side = slice(half * width, (half + 1) * width)
                near[index][lane * rows : (lane + 1) * rows, side] = block
                if lane < len(lanes) - 4:
                    far[index][lane * rows : (lane + 1) * rows, side] = block


def place_kernel(per_chip, lengths_ref, owner_ref, pos_ref, start_ref, order_ref):
    me = lax.axis_index("ctx")
    chip, core = me // CORES, me % CORES
    table_rows = owner_ref.shape[0]
    total = table_rows * LANES
    held = pos_ref.shape[0]
    rows = LANES // 2
    shift = per_chip.bit_length() - 1
    block_rows = 32
    table_step = table_rows // (held // block_rows)
    first = lax.broadcasted_iota(jnp.int32, (LANES, LANES), 0)
    second = lax.broadcasted_iota(jnp.int32, (LANES, LANES), 1)
    same = (first < rows) == (second < rows)
    lane = lax.broadcasted_iota(jnp.int32, (1, LANES), 1)
    line = lax.broadcasted_iota(jnp.int32, (block_rows, 1), 0)
    wanted = chip * per_chip + jnp.bitwise_and(line, per_chip - 1)
    source = jnp.right_shift(line, shift)
    keys = []
    for block in range(held // block_rows):
        pos = jnp.zeros((block_rows, 1), jnp.int32)
        own = jnp.zeros((block_rows, 1), jnp.int32)
        for step in range(table_step):
            table = block * table_step + step
            owners = owner_ref[table : table + 1, :]
            key_row = owners * LANES + lane
            below = same & (row_to_column(key_row) < key_row)
            rank = jnp.sum(below.astype(jnp.int32), axis=0, keepdims=True)
            lane_source = 2 * step + (lane >= rows).astype(jnp.int32)
            hit = (wanted == rank) & (source == lane_source)
            pos += jnp.sum(jnp.where(hit, lane + table * LANES, 0), axis=1, keepdims=True)
            own += jnp.sum(jnp.where(hit, owners, 0), axis=1, keepdims=True)
        start = jnp.zeros((block_rows, 1), jnp.int32)
        end = jnp.int32(0)
        for rollout in range(lengths_ref.shape[0]):
            end = end + lengths_ref[rollout]
            start = jnp.where(pos >= end, end, start)
        here = slice(block * block_rows, (block + 1) * block_rows)
        pos_ref[here, :] = jnp.broadcast_to(pos, (block_rows, LANES))
        start_ref[here, :] = jnp.broadcast_to(start, (block_rows, LANES))
        keys.append((own - chip * CORES) * total + pos)
    key_col = jnp.concatenate(keys, axis=0)
    key_row = column_to_row(key_col)
    slot = jnp.sum((key_col < key_row).astype(jnp.int32), axis=0, keepdims=True)
    slot = jnp.bitwise_xor(slot, core * rows)
    place = lax.broadcasted_iota(jnp.int32, (held, held), 0)
    order_ref[...] = (place == slot).astype(jnp.float32).astype(jnp.bfloat16)


def unpack_moved(moved_ref, k_all, v_all):
    nodes = moved_ref.shape[0]
    tokens = k_all.shape[0] // nodes
    half = tokens // 2
    width = HEADS * HD

    def unpack(node, carry):
        for part in range(2):
            row = pl.ds(pl.multiple_of(node * tokens + part * half, half), half)
            col = 2 * part * width
            k_all[row, :] = moved_ref[node, Q_ROWS:, col : col + width]
            for head in range(HEADS):
                at = col + width + head * HD
                v_all[row, 2 * head * HD : (2 * head + 1) * HD] = moved_ref[node, Q_ROWS:, at : at + HD]
        return carry

    lax.fori_loop(0, nodes, unpack, 0)


def unpack_pieces(pieces, tokens, k_all, v_all):
    me = lax.axis_index("ctx")
    offsets = block_offsets(k_all.shape[0] // tokens)
    width = HEADS * HD
    for index, ref in enumerate(pieces):
        held = offsets if index < CORES else offsets[:-4]
        for lane, offset in enumerate(held):
            node = jnp.bitwise_xor(me, index ^ offset)
            row = pl.ds(pl.multiple_of(node * tokens, tokens), tokens)
            here = slice(lane * tokens, (lane + 1) * tokens)
            k_all[row, :] = ref[here, :width]
            for head in range(HEADS):
                at = width + head * HD
                v_all[row, 2 * head * HD : (2 * head + 1) * HD] = ref[here, at : at + HD]


def attend_kernel(q_ref, pos_ref, start_ref, order_ref, *refs):
    kv_refs, refs = refs[: -CORES - 3], refs[-CORES - 3 :]
    out_refs, (k_all, v_all, context) = refs[:CORES], refs[CORES:]
    total = k_all.shape[0]
    held = context.shape[0]
    block_rows = 32
    blocks = held // block_rows
    span = total // blocks
    scale = math.log2(math.e) / math.sqrt(HD)

    for head in range(HEADS):
        v_all[:, (2 * head + 1) * HD : (2 * head + 2) * HD] = jnp.ones((total, HD), jnp.bfloat16)
    if len(kv_refs) == 1:
        unpack_moved(kv_refs[0], k_all, v_all)
    else:
        unpack_pieces(kv_refs, held // CORES, k_all, v_all)

    for block in range(blocks):
        here = slice(block * block_rows, (block + 1) * block_rows)
        parts = block_rows // SUB
        messages = [q_ref[block * parts + part].astype(jnp.float32) for part in range(parts)]
        pos = pos_ref[here, :1]
        start = start_ref[here, :1]
        low, high = max(0, block - blocks // 2) * span, (block + 1) * span
        chunk = min(high - low, 1024)
        for head in range(HEADS):
            pieces = []
            for group in range(GROUP):
                for message in messages:
                    rows = slice(head * SUB, (head + 1) * SUB)
                    pieces.append(message[rows, group * HD : (group + 1) * HD])
            queries = jnp.concatenate(pieces, axis=0).astype(jnp.bfloat16)
            peak, acc = None, None
            for lower in range(low, high, chunk):
                keys = slice(lower, lower + chunk)
                scores = lax.dot_general(
                    queries,
                    k_all[keys, head * HD : (head + 1) * HD],
                    (((1,), (1,)), ((), ())),
                    preferred_element_type=jnp.float32,
                )
                at = lower + lax.broadcasted_iota(jnp.int32, (block_rows, chunk), 1)
                seen = (at <= pos) & (at >= start)
                bias = jnp.where(seen, 0.0, NEGATIVE)
                scores = scores.reshape(GROUP, block_rows, chunk) + bias[None]
                scores = scores.reshape(GROUP * block_rows, chunk)
                top = jnp.max(scores, axis=1, keepdims=True)
                if peak is not None:
                    top = jnp.maximum(peak, top)
                probs = jnp.exp2((scores - top) * scale)
                if chunk != high - low:
                    probs = probs.reshape(GROUP, block_rows, chunk)
                    probs = jnp.where(seen[None], probs, 0.0).reshape(GROUP * block_rows, chunk)
                new = jnp.dot(
                    probs.astype(jnp.bfloat16),
                    v_all[keys, 2 * head * HD : (2 * head + 2) * HD],
                    preferred_element_type=jnp.float32,
                )
                acc = new if acc is None else acc * jnp.exp2((peak - top) * scale) + new
                peak = top
            result = (acc[:, :HD] / acc[:, HD:]).astype(jnp.bfloat16)
            for group in range(GROUP):
                col = head * WIDE + group * HD
                context[here, col : col + HD] = result[group * block_rows : (group + 1) * block_rows]
    rows = held // CORES
    for core in range(CORES):
        order = order_ref[core * rows : (core + 1) * rows, :]
        moved = jnp.dot(order, context[...], preferred_element_type=jnp.float32)
        out_refs[core][...] = moved.astype(jnp.bfloat16)


def assemble_kernel(*refs):
    core = lax.axis_index("ctx") % CORES
    width = HEADS * WIDE
    for index in range(CORES):
        col = pl.multiple_of(jnp.bitwise_xor(core, index) * width, width)
        refs[CORES][:, pl.ds(col, width)] = refs[index][...]


def on_device(queries, keys, values, owner, rollout_lengths):
    rows = queries.shape[0]
    nodes = lax.axis_size("ctx")
    total = owner.shape[0]
    chips = nodes // CORES
    per_chip = rows // chips
    held = rows * CORES
    table = owner.reshape(total // LANES, LANES)
    whole = pl.BlockSpec(memory_space=pltpu.VMEM)
    hbm = pl.BlockSpec(memory_space=pltpu.HBM)
    apart = nodes == 16

    def swap(array, offset):
        return lax.ppermute(array, "ctx", [(node, node ^ offset) for node in range(nodes)])

    kv_rows = 0 if apart else rows // 2
    message = jax.ShapeDtypeStruct((nodes, Q_ROWS + kv_rows, WIDE), jnp.bfloat16)
    joined = jax.ShapeDtypeStruct((rows, 2 * KVH * HD), jnp.bfloat16)
    if apart:
        q_near, kv_near = pl.pallas_call(
            fetch_kernel,
            out_shape=[jax.ShapeDtypeStruct(queries.shape, jnp.bfloat16), joined],
            in_specs=[hbm] * 3,
            out_specs=[whole] * 2,
            scratch_shapes=[pltpu.SemaphoreType.DMA((3,))],
            compiler_params=VMEM,
            name="fetch",
        )(pltpu.with_memory_space_constraint(queries, pltpu.HBM), pltpu.with_memory_space_constraint(keys, pltpu.HBM), pltpu.with_memory_space_constraint(values, pltpu.HBM))
        lanes = [kv_near]
    operands = (table, q_near) if apart else (table, queries, keys, values)
    packed = pl.pallas_call(
        functools.partial(pack_kernel, chips),
        out_shape=message,
        in_specs=[whole] * len(operands),
        out_specs=whole,
        compiler_params=VMEM,
        cost_estimate=pl.CostEstimate(
            flops=2 * rows * rows * H * HD, bytes_accessed=4 * rows * H * HD, transcendentals=0
        ),
        name="pack",
    )(*operands)
    if apart:
        lanes = [swap(lanes[0], offset) if offset else lanes[0] for offset in block_offsets(nodes)]

    moved = lax.all_to_all(packed, "ctx", split_axis=0, concat_axis=0, tiled=True)

    if apart:
        near, far = len(lanes) * rows, (len(lanes) - 4) * rows
        pieces = pl.pallas_call(
            heads_kernel,
            out_shape=[
                jax.ShapeDtypeStruct((count, 2 * HEADS * HD), jnp.bfloat16)
                for count in (near, near, far, far)
            ],
            in_specs=[whole] * len(lanes),
            out_specs=[whole] * (2 * CORES),
            compiler_params=VMEM,
            cost_estimate=pl.CostEstimate(
                flops=2 * 10**10, bytes_accessed=64 * 2**20, transcendentals=0
            ),
            name="heads",
        )(*lanes)
        kv_parts = [swap(piece, index) if index else piece for index, piece in enumerate(pieces)]
        q_part = moved
    else:
        kv_parts = [moved]
        groups = held // SUB
        q_part = moved[:, :Q_ROWS].reshape(groups, nodes // groups, HEADS, SUB, WIDE)[:, :, :, :per_chip]
        q_part = q_part.transpose(0, 2, 1, 3, 4).reshape(groups, Q_ROWS, WIDE)

    pos, start, order = pl.pallas_call(
        functools.partial(place_kernel, per_chip),
        out_shape=(
            jax.ShapeDtypeStruct((held, LANES), jnp.int32),
            jax.ShapeDtypeStruct((held, LANES), jnp.int32),
            jax.ShapeDtypeStruct((held, held), jnp.bfloat16),
        ),
        in_specs=[pl.BlockSpec(memory_space=pltpu.SMEM), whole],
        out_specs=(whole, whole, whole),
        compiler_params=VMEM,
        name="place",
    )(rollout_lengths, table)

    own, other = pl.pallas_call(
        attend_kernel,
        out_shape=(jax.ShapeDtypeStruct((rows, HEADS * WIDE), jnp.bfloat16),) * CORES,
        in_specs=[whole] * (4 + len(kv_parts)),
        out_specs=(whole,) * CORES,
        scratch_shapes=[
            pltpu.VMEM((total, HEADS * HD), jnp.bfloat16),
            pltpu.VMEM((total, HEADS * 2 * HD), jnp.bfloat16),
            pltpu.VMEM((held, HEADS * WIDE), jnp.bfloat16),
        ],
        compiler_params=VMEM,
        name="attend",
    )(q_part, pos, start, order, *kv_parts)

    return pl.pallas_call(
        assemble_kernel,
        out_shape=jax.ShapeDtypeStruct((rows, H * HD), jnp.bfloat16),
        in_specs=[whole] * CORES,
        out_specs=whole,
        compiler_params=VMEM,
        name="assemble",
    )(own, swap(other, 1))


def solution(mesh):
    placed = (
        P(("groups", "ctx"), None),
        P(("groups", "ctx"), None),
        P(("groups", "ctx"), None),
        P("groups"),
        P("groups"),
    )
    return jax.shard_map(
        on_device, mesh=mesh, in_specs=placed, out_specs=P(("groups", "ctx"), None), check_vma=False
    )
```

```python
import functools
import math

import jax
import jax.numpy as jnp
from jax import lax
from jax.experimental import pallas as pl
from jax.experimental.pallas import tpu as pltpu
from jax.sharding import PartitionSpec as P

H = 32
KVH = 4
HD = 128
GROUP = H // KVH
WIDE = GROUP * HD
CORES = 2
HEADS = KVH // CORES
NEGATIVE = -1e30
LANES = 128
SUB = 8
Q_ROWS = HEADS * SUB
VMEM = pltpu.CompilerParams(vmem_limit_bytes=40 * 2**20)


def row_to_column(row):
    size = row.shape[1]
    here = lax.broadcasted_iota(jnp.int32, (size, size), 0)
    there = lax.broadcasted_iota(jnp.int32, (size, size), 1)
    return jnp.sum(jnp.where(here == there, row, 0), axis=1, keepdims=True)


def column_to_row(column):
    size = column.shape[0]
    here = lax.broadcasted_iota(jnp.int32, (size, size), 0)
    there = lax.broadcasted_iota(jnp.int32, (size, size), 1)
    return jnp.sum(jnp.where(here == there, column, 0), axis=0, keepdims=True)


def fetch_kernel(owner_hbm, q_hbm, k_hbm, v_hbm, order_ref, q_ref, kv_ref, owner_ref, sems):
    me = lax.axis_index("ctx")
    rows, width = k_hbm.shape
    copies = [
        pltpu.make_async_copy(owner_hbm, owner_ref, sems.at[0]),
        pltpu.make_async_copy(k_hbm, kv_ref.at[:, pl.ds(0, width)], sems.at[1]),
        pltpu.make_async_copy(v_hbm, kv_ref.at[:, pl.ds(width, width)], sems.at[2]),
        pltpu.make_async_copy(q_hbm, q_ref, sems.at[3]),
    ]
    for copy in copies:
        copy.start()
    copies[0].wait()
    both = owner_ref[pl.ds(me // 2, 1), :]
    swapped = jnp.concatenate((both[:, rows:], both[:, :rows]), axis=1)
    own = jnp.where(me % 2 == 1, swapped, both)[:, :rows]
    token = lax.broadcasted_iota(jnp.int32, (1, rows), 1)
    key_row = own * rows + token
    rank = jnp.sum((row_to_column(key_row) < key_row).astype(jnp.int32), axis=0, keepdims=True)
    place = lax.broadcasted_iota(jnp.int32, (rows, rows), 0)
    order_ref[...] = (place == rank).astype(jnp.float32).astype(jnp.bfloat16)
    for copy in copies[1:]:
        copy.wait()


def pack_kernel(chips, order_ref, q_ref, *refs):
    kv_refs, out_ref = refs[:-1], refs[-1]
    rows = q_ref.shape[0]
    per_chip = rows // chips
    order = order_ref[...]
    for core in range(CORES):
        sorted_q = []
        for head in range(core * HEADS, (core + 1) * HEADS):
            wide = slice(head * WIDE, (head + 1) * WIDE)
            sorted_q.append(jnp.dot(order, q_ref[:, wide], preferred_element_type=jnp.float32))
        for chip in range(chips):
            dest = chip * CORES + core
            parts = []
            for array in sorted_q:
                parts.append(array[chip * per_chip : (chip + 1) * per_chip])
                if per_chip < SUB:
                    parts.append(jnp.zeros((SUB - per_chip, WIDE), jnp.float32))
            out_ref[dest, :Q_ROWS, :] = jnp.concatenate(parts, axis=0).astype(jnp.bfloat16)
            if kv_refs:
                width = HEADS * HD
                half = rows // 2
                for part in range(2):
                    here = slice(part * half, (part + 1) * half)
                    for index in range(2):
                        col = (2 * part + index) * width
                        side = index * KVH * HD + core * width
                        block = kv_refs[0][here, side : side + width]
                        out_ref[dest, Q_ROWS:, col : col + width] = block


def block_offsets(nodes):
    return list(range(nodes - 2 * CORES, 3 * CORES, -2 * CORES)) + [3 * CORES, 2 * CORES, CORES, 0]


def heads_kernel(*refs):
    lanes, near, far = refs[: -2 * CORES], refs[-2 * CORES : -CORES], refs[-CORES:]
    core = lax.axis_index("ctx") % CORES
    rows = lanes[0].shape[0]
    width = HEADS * HD
    for index in range(CORES):
        col = jnp.bitwise_xor(core, index) * width
        for lane, ref in enumerate(lanes):
            for half in range(2):
                block = ref[:, pl.ds(pl.multiple_of(col + half * KVH * HD, width), width)]
                side = slice(half * width, (half + 1) * width)
                near[index][lane * rows : (lane + 1) * rows, side] = block
                if lane < len(lanes) - 4:
                    far[index][lane * rows : (lane + 1) * rows, side] = block


def place_kernel(per_chip, lengths_ref, owner_ref, pos_ref, start_ref, order_ref):
    me = lax.axis_index("ctx")
    chip, core = me // CORES, me % CORES
    table_rows = owner_ref.shape[0]
    total = table_rows * LANES
    held = pos_ref.shape[0]
    rows = LANES // 2
    shift = per_chip.bit_length() - 1
    block_rows = 32
    table_step = table_rows // (held // block_rows)
    first = lax.broadcasted_iota(jnp.int32, (LANES, LANES), 0)
    second = lax.broadcasted_iota(jnp.int32, (LANES, LANES), 1)
    same = (first < rows) == (second < rows)
    lane = lax.broadcasted_iota(jnp.int32, (1, LANES), 1)
    line = lax.broadcasted_iota(jnp.int32, (block_rows, 1), 0)
    wanted = chip * per_chip + jnp.bitwise_and(line, per_chip - 1)
    source = jnp.right_shift(line, shift)
    keys = []
    for block in range(held // block_rows):
        pos = jnp.zeros((block_rows, 1), jnp.int32)
        own = jnp.zeros((block_rows, 1), jnp.int32)
        for step in range(table_step):
            table = block * table_step + step
            owners = owner_ref[table : table + 1, :]
            key_row = owners * LANES + lane
            below = same & (row_to_column(key_row) < key_row)
            rank = jnp.sum(below.astype(jnp.int32), axis=0, keepdims=True)
            lane_source = 2 * step + (lane >= rows).astype(jnp.int32)
            hit = (wanted == rank) & (source == lane_source)
            pos += jnp.sum(jnp.where(hit, lane + table * LANES, 0), axis=1, keepdims=True)
            own += jnp.sum(jnp.where(hit, owners, 0), axis=1, keepdims=True)
        start = jnp.zeros((block_rows, 1), jnp.int32)
        end = jnp.int32(0)
        for rollout in range(lengths_ref.shape[0]):
            end = end + lengths_ref[rollout]
            start = jnp.where(pos >= end, end, start)
        here = slice(block * block_rows, (block + 1) * block_rows)
        pos_ref[here, :] = jnp.broadcast_to(pos, (block_rows, LANES))
        start_ref[here, :] = jnp.broadcast_to(start, (block_rows, LANES))
        keys.append((own - chip * CORES) * total + pos)
    key_col = jnp.concatenate(keys, axis=0)
    key_row = column_to_row(key_col)
    slot = jnp.sum((key_col < key_row).astype(jnp.int32), axis=0, keepdims=True)
    slot = jnp.bitwise_xor(slot, core * rows)
    place = lax.broadcasted_iota(jnp.int32, (held, held), 0)
    order_ref[...] = (place == slot).astype(jnp.float32).astype(jnp.bfloat16)


def unpack_moved(moved_ref, k_all, v_all):
    nodes = moved_ref.shape[0]
    tokens = k_all.shape[0] // nodes
    half = tokens // 2
    width = HEADS * HD

    def unpack(node, carry):
        for part in range(2):
            row = pl.ds(pl.multiple_of(node * tokens + part * half, half), half)
            col = 2 * part * width
            k_all[row, :] = moved_ref[node, Q_ROWS:, col : col + width]
            for head in range(HEADS):
                at = col + width + head * HD
                v_all[row, 2 * head * HD : (2 * head + 1) * HD] = moved_ref[node, Q_ROWS:, at : at + HD]
        return carry

    lax.fori_loop(0, nodes, unpack, 0)


def unpack_pieces(pieces, tokens, k_all, v_all):
    me = lax.axis_index("ctx")
    offsets = block_offsets(k_all.shape[0] // tokens)
    width = HEADS * HD
    for index, ref in enumerate(pieces):
        held = offsets if index < CORES else offsets[:-4]
        for lane, offset in enumerate(held):
            node = jnp.bitwise_xor(me, index ^ offset)
            row = pl.ds(pl.multiple_of(node * tokens, tokens), tokens)
            here = slice(lane * tokens, (lane + 1) * tokens)
            k_all[row, :] = ref[here, :width]
            for head in range(HEADS):
                at = width + head * HD
                v_all[row, 2 * head * HD : (2 * head + 1) * HD] = ref[here, at : at + HD]


def attend_kernel(q_ref, pos_ref, start_ref, order_ref, *refs):
    kv_refs, refs = refs[: -CORES - 3], refs[-CORES - 3 :]
    out_refs, (k_all, v_all, context) = refs[:CORES], refs[CORES:]
    total = k_all.shape[0]
    held = context.shape[0]
    block_rows = 32
    blocks = held // block_rows
    span = total // blocks
    scale = math.log2(math.e) / math.sqrt(HD)

    for head in range(HEADS):
        v_all[:, (2 * head + 1) * HD : (2 * head + 2) * HD] = jnp.ones((total, HD), jnp.bfloat16)
    if len(kv_refs) == 1:
        unpack_moved(kv_refs[0], k_all, v_all)
    else:
        unpack_pieces(kv_refs, held // CORES, k_all, v_all)

    def rows_of(block):
        return slice(block * block_rows, (block + 1) * block_rows)

    def scores_of(block, head, keys):
        parts = block_rows // SUB
        mine = slice(head * SUB, (head + 1) * SUB)
        messages = [q_ref[block * parts + part].astype(jnp.float32)[mine] for part in range(parts)]
        pieces = []
        for group in range(GROUP):
            for message in messages:
                pieces.append(message[:, group * HD : (group + 1) * HD])
        return lax.dot_general(
            jnp.concatenate(pieces, axis=0).astype(jnp.bfloat16),
            k_all[keys, head * HD : (head + 1) * HD],
            (((1,), (1,)), ((), ())),
            preferred_element_type=jnp.float32,
        )

    def weights_of(block, keys, scores, peak=None):
        count = keys.stop - keys.start
        at = keys.start + lax.broadcasted_iota(jnp.int32, (block_rows, count), 1)
        seen = (at <= pos_ref[rows_of(block), :1]) & (at >= start_ref[rows_of(block), :1])
        scores = scores.reshape(GROUP, block_rows, count) + jnp.where(seen, 0.0, NEGATIVE)[None]
        scores = scores.reshape(GROUP * block_rows, count)
        top = jnp.max(scores, axis=1, keepdims=True)
        if peak is None:
            return top, jnp.exp2((scores - top) * scale).astype(jnp.bfloat16)
        top = jnp.maximum(peak, top)
        weights = jnp.exp2((scores - top) * scale).reshape(GROUP, block_rows, count)
        weights = jnp.where(seen[None], weights, 0.0).reshape(GROUP * block_rows, count)
        return top, weights.astype(jnp.bfloat16)

    def sums_of(head, keys, weights):
        values = v_all[keys, 2 * head * HD : (2 * head + 2) * HD]
        return jnp.dot(weights, values, preferred_element_type=jnp.float32)

    def store(block, head, sums):
        result = (sums[:, :HD] / sums[:, HD:]).astype(jnp.bfloat16)
        for group in range(GROUP):
            col = head * WIDE + group * HD
            part = result[group * block_rows : (group + 1) * block_rows]
            context[rows_of(block), col : col + HD] = part

    tasks = [
        (block, head, slice(max(0, block - blocks // 2) * span, (block + 1) * span))
        for block in reversed(range(blocks))
        for head in range(HEADS)
    ]
    most = 1024
    if max(keys.stop - keys.start for _, _, keys in tasks) <= most:
        scores, last = scores_of(*tasks[0]), None
        for index, (block, head, keys) in enumerate(tasks):
            later = scores_of(*tasks[index + 1]) if index + 1 < len(tasks) else None
            _, weights = weights_of(block, keys, scores)
            if last is not None:
                store(*last[:2], sums_of(*last[1:]))
            scores, last = later, (block, head, keys, weights)
        store(*last[:2], sums_of(*last[1:]))
    else:
        for block, head, keys in tasks:
            peak = jnp.full((GROUP * block_rows, 1), NEGATIVE, jnp.float32)
            sums = jnp.zeros((GROUP * block_rows, 2 * HD), jnp.float32)
            for lower in range(keys.start, keys.stop, most):
                part = slice(lower, min(lower + most, keys.stop))
                top, weights = weights_of(block, part, scores_of(block, head, part), peak)
                sums = sums * jnp.exp2((peak - top) * scale) + sums_of(head, part, weights)
                peak = top
            store(block, head, sums)

    rows = held // CORES
    for core in range(CORES):
        order = order_ref[core * rows : (core + 1) * rows, :]
        moved = jnp.dot(order, context[...], preferred_element_type=jnp.float32)
        out_refs[core][...] = moved.astype(jnp.bfloat16)


def write_kernel(other, heads_ref, *refs):
    out_hbm, sem = refs[-2:]
    core = jnp.bitwise_xor(lax.axis_index("ctx") % CORES, other)
    width = HEADS * WIDE
    side = pl.ds(pl.multiple_of(core * width, width), width)
    copy = pltpu.make_async_copy(heads_ref, out_hbm.at[:, side], sem)
    copy.start()
    copy.wait()


def on_device(queries, keys, values, owner, rollout_lengths):
    rows = queries.shape[0]
    nodes = lax.axis_size("ctx")
    total = owner.shape[0]
    chips = nodes // CORES
    per_chip = rows // chips
    held = rows * CORES
    table = owner.reshape(total // LANES, LANES)
    whole = pl.BlockSpec(memory_space=pltpu.VMEM)
    hbm = pl.BlockSpec(memory_space=pltpu.HBM)
    apart = nodes == 16

    def swap(array, offset):
        return lax.ppermute(array, "ctx", [(node, node ^ offset) for node in range(nodes)])

    kv_rows = 0 if apart else rows // 2
    message = jax.ShapeDtypeStruct((nodes, Q_ROWS + kv_rows, WIDE), jnp.bfloat16)
    order_in, q_near, kv_near = pl.pallas_call(
        fetch_kernel,
        out_shape=[
            jax.ShapeDtypeStruct((rows, rows), jnp.bfloat16),
            jax.ShapeDtypeStruct(queries.shape, jnp.bfloat16),
            jax.ShapeDtypeStruct((rows, 2 * KVH * HD), jnp.bfloat16),
        ],
        in_specs=[hbm] * 4,
        out_specs=[whole] * 3,
        scratch_shapes=[pltpu.VMEM(table.shape, jnp.int32), pltpu.SemaphoreType.DMA((4,))],
        compiler_params=VMEM,
        name="fetch",
    )(*(pltpu.with_memory_space_constraint(x, pltpu.HBM) for x in (table, queries, keys, values)))
    operands = (order_in, q_near) if apart else (order_in, q_near, kv_near)
    packed = pl.pallas_call(
        functools.partial(pack_kernel, chips),
        out_shape=message,
        in_specs=[whole] * len(operands),
        out_specs=whole,
        compiler_params=VMEM,
        cost_estimate=pl.CostEstimate(
            flops=2 * rows * rows * H * HD, bytes_accessed=4 * rows * H * HD, transcendentals=0
        ),
        name="pack",
    )(*operands)
    if apart:
        lanes = [swap(kv_near, offset) if offset else kv_near for offset in block_offsets(nodes)]

    moved = lax.all_to_all(packed, "ctx", split_axis=0, concat_axis=0, tiled=True)

    if apart:
        near, far = len(lanes) * rows, (len(lanes) - 4) * rows
        pieces = pl.pallas_call(
            heads_kernel,
            out_shape=[
                jax.ShapeDtypeStruct((count, 2 * HEADS * HD), jnp.bfloat16)
                for count in (near, near, far, far)
            ],
            in_specs=[whole] * len(lanes),
            out_specs=[whole] * (2 * CORES),
            compiler_params=VMEM,
            cost_estimate=pl.CostEstimate(
                flops=2 * 10**10, bytes_accessed=64 * 2**20, transcendentals=0
            ),
            name="heads",
        )(*lanes)
        kv_parts = [swap(piece, index) if index else piece for index, piece in enumerate(pieces)]
        q_part = moved
    else:
        kv_parts = [moved]
        groups = held // SUB
        q_part = moved[:, :Q_ROWS].reshape(groups, nodes // groups, HEADS, SUB, WIDE)[:, :, :, :per_chip]
        q_part = q_part.transpose(0, 2, 1, 3, 4).reshape(groups, Q_ROWS, WIDE)

    pos, start, order = pl.pallas_call(
        functools.partial(place_kernel, per_chip),
        out_shape=(
            jax.ShapeDtypeStruct((held, LANES), jnp.int32),
            jax.ShapeDtypeStruct((held, LANES), jnp.int32),
            jax.ShapeDtypeStruct((held, held), jnp.bfloat16),
        ),
        in_specs=[pl.BlockSpec(memory_space=pltpu.SMEM), whole],
        out_specs=(whole, whole, whole),
        compiler_params=VMEM,
        name="place",
    )(rollout_lengths, table)

    own, other = pl.pallas_call(
        attend_kernel,
        out_shape=(jax.ShapeDtypeStruct((rows, HEADS * WIDE), jnp.bfloat16),) * CORES,
        in_specs=[whole] * (4 + len(kv_parts)),
        out_specs=(whole,) * CORES,
        scratch_shapes=[
            pltpu.VMEM((total, HEADS * HD), jnp.bfloat16),
            pltpu.VMEM((total, HEADS * 2 * HD), jnp.bfloat16),
            pltpu.VMEM((held, HEADS * WIDE), jnp.bfloat16),
        ],
        compiler_params=VMEM,
        name="attend",
    )(q_part, pos, start, order, *kv_parts)

    result = jax.ShapeDtypeStruct((rows, H * HD), jnp.bfloat16)
    half = pl.pallas_call(
        functools.partial(write_kernel, 0),
        out_shape=result,
        in_specs=[whole],
        out_specs=hbm,
        scratch_shapes=[pltpu.SemaphoreType.DMA],
        compiler_params=VMEM,
        name="write_own",
    )(own)
    return pl.pallas_call(
        functools.partial(write_kernel, 1),
        out_shape=result,
        in_specs=[whole, hbm],
        out_specs=hbm,
        scratch_shapes=[pltpu.SemaphoreType.DMA],
        input_output_aliases={1: 0},
        compiler_params=VMEM,
        name="write_received",
    )(swap(other, 1), half)


def solution(mesh):
    placed = (
        P(("groups", "ctx"), None),
        P(("groups", "ctx"), None),
        P(("groups", "ctx"), None),
        P("groups"),
        P("groups"),
    )
    return jax.shard_map(
        on_device, mesh=mesh, in_specs=placed, out_specs=P(("groups", "ctx"), None), check_vma=False
    )
```

```python
import functools
import math

import jax
import jax.numpy as jnp
from jax import lax
from jax.experimental import pallas as pl
from jax.experimental.pallas import tpu as pltpu
from jax.sharding import PartitionSpec as P

H = 32
KVH = 4
HD = 128
GROUP = H // KVH
WIDE = GROUP * HD
CORES = 2
HEADS = KVH // CORES
NEGATIVE = -1e30
LANES = 128
SUB = 8
Q_ROWS = HEADS * SUB
VMEM = pltpu.CompilerParams(vmem_limit_bytes=40 * 2**20)


def row_to_column(row):
    size = row.shape[1]
    here = lax.broadcasted_iota(jnp.int32, (size, size), 0)
    there = lax.broadcasted_iota(jnp.int32, (size, size), 1)
    return jnp.sum(jnp.where(here == there, row, 0), axis=1, keepdims=True)


def column_to_row(column):
    size = column.shape[0]
    here = lax.broadcasted_iota(jnp.int32, (size, size), 0)
    there = lax.broadcasted_iota(jnp.int32, (size, size), 1)
    return jnp.sum(jnp.where(here == there, column, 0), axis=0, keepdims=True)


def fetch_kernel(owner_hbm, q_hbm, k_hbm, v_hbm, order_ref, q_ref, kv_ref, owner_ref, sems):
    me = lax.axis_index("ctx")
    rows, width = k_hbm.shape
    copies = [
        pltpu.make_async_copy(owner_hbm, owner_ref, sems.at[0]),
        pltpu.make_async_copy(k_hbm, kv_ref.at[:, pl.ds(0, width)], sems.at[1]),
        pltpu.make_async_copy(v_hbm, kv_ref.at[:, pl.ds(width, width)], sems.at[2]),
        pltpu.make_async_copy(q_hbm, q_ref, sems.at[3]),
    ]
    for copy in copies:
        copy.start()
    copies[0].wait()
    both = owner_ref[pl.ds(me // 2, 1), :]
    swapped = jnp.concatenate((both[:, rows:], both[:, :rows]), axis=1)
    own = jnp.where(me % 2 == 1, swapped, both)[:, :rows]
    token = lax.broadcasted_iota(jnp.int32, (1, rows), 1)
    key_row = own * rows + token
    rank = jnp.sum((row_to_column(key_row) < key_row).astype(jnp.int32), axis=0, keepdims=True)
    place = lax.broadcasted_iota(jnp.int32, (rows, rows), 0)
    order_ref[...] = (place == rank).astype(jnp.float32).astype(jnp.bfloat16)
    for copy in copies[1:]:
        copy.wait()


def pack_kernel(chips, order_ref, q_ref, *refs):
    kv_refs, out_ref = refs[:-1], refs[-1]
    rows = q_ref.shape[0]
    per_chip = rows // chips
    order = order_ref[...]
    for core in range(CORES):
        sorted_q = []
        for head in range(core * HEADS, (core + 1) * HEADS):
            wide = slice(head * WIDE, (head + 1) * WIDE)
            sorted_q.append(jnp.dot(order, q_ref[:, wide], preferred_element_type=jnp.float32))
        for chip in range(chips):
            dest = chip * CORES + core
            parts = []
            for array in sorted_q:
                parts.append(array[chip * per_chip : (chip + 1) * per_chip])
                if per_chip < SUB:
                    parts.append(jnp.zeros((SUB - per_chip, WIDE), jnp.float32))
            out_ref[dest, :Q_ROWS, :] = jnp.concatenate(parts, axis=0).astype(jnp.bfloat16)
            if kv_refs:
                width = HEADS * HD
                half = rows // 2
                for part in range(2):
                    here = slice(part * half, (part + 1) * half)
                    for index in range(2):
                        col = (2 * part + index) * width
                        side = index * KVH * HD + core * width
                        block = kv_refs[0][here, side : side + width]
                        out_ref[dest, Q_ROWS:, col : col + width] = block


WHOLE = ((12, 8), (6, 4), (2, 0))
HALVES = ((0, WHOLE[0]), (1, WHOLE[0]), (2, WHOLE[0]), (3, WHOLE[0])) + tuple(
    (core, pair) for pair in WHOLE[1:] for core in range(CORES)
)


def heads_kernel(*refs):
    lanes, outs = refs[:-CORES], refs[-CORES:]
    core = lax.axis_index("ctx") % CORES
    rows = lanes[0].shape[0]
    width = HEADS * HD
    for index in range(CORES):
        col = jnp.bitwise_xor(core, index) * width
        for lane, ref in enumerate(lanes):
            here = slice(lane * rows, (lane + 1) * rows)
            for half in range(2):
                side = pl.ds(pl.multiple_of(col + half * KVH * HD, width), width)
                outs[index][here, half * width : (half + 1) * width] = ref[:, side]


def place_kernel(per_chip, lengths_ref, owner_ref, pos_ref, start_ref, order_ref):
    me = lax.axis_index("ctx")
    chip, core = me // CORES, me % CORES
    table_rows = owner_ref.shape[0]
    total = table_rows * LANES
    held = pos_ref.shape[0]
    rows = LANES // 2
    shift = per_chip.bit_length() - 1
    block_rows = 32
    table_step = table_rows // (held // block_rows)
    first = lax.broadcasted_iota(jnp.int32, (LANES, LANES), 0)
    second = lax.broadcasted_iota(jnp.int32, (LANES, LANES), 1)
    same = (first < rows) == (second < rows)
    lane = lax.broadcasted_iota(jnp.int32, (1, LANES), 1)
    line = lax.broadcasted_iota(jnp.int32, (block_rows, 1), 0)
    wanted = chip * per_chip + jnp.bitwise_and(line, per_chip - 1)
    source = jnp.right_shift(line, shift)
    keys = []
    for block in range(held // block_rows):
        pos = jnp.zeros((block_rows, 1), jnp.int32)
        own = jnp.zeros((block_rows, 1), jnp.int32)
        for step in range(table_step):
            table = block * table_step + step
            owners = owner_ref[table : table + 1, :]
            key_row = owners * LANES + lane
            below = same & (row_to_column(key_row) < key_row)
            rank = jnp.sum(below.astype(jnp.int32), axis=0, keepdims=True)
            lane_source = 2 * step + (lane >= rows).astype(jnp.int32)
            hit = (wanted == rank) & (source == lane_source)
            pos += jnp.sum(jnp.where(hit, lane + table * LANES, 0), axis=1, keepdims=True)
            own += jnp.sum(jnp.where(hit, owners, 0), axis=1, keepdims=True)
        start = jnp.zeros((block_rows, 1), jnp.int32)
        end = jnp.int32(0)
        for rollout in range(lengths_ref.shape[0]):
            end = end + lengths_ref[rollout]
            start = jnp.where(pos >= end, end, start)
        here = slice(block * block_rows, (block + 1) * block_rows)
        pos_ref[here, :] = jnp.broadcast_to(pos, (block_rows, LANES))
        start_ref[here, :] = jnp.broadcast_to(start, (block_rows, LANES))
        keys.append((own - chip * CORES) * total + pos)
    key_col = jnp.concatenate(keys, axis=0)
    key_row = column_to_row(key_col)
    slot = jnp.sum((key_col < key_row).astype(jnp.int32), axis=0, keepdims=True)
    slot = jnp.bitwise_xor(slot, core * rows)
    place = lax.broadcasted_iota(jnp.int32, (held, held), 0)
    order_ref[...] = (place == slot).astype(jnp.float32).astype(jnp.bfloat16)


def unpack_moved(moved_ref, k_all, v_all):
    nodes = moved_ref.shape[0]
    tokens = k_all.shape[0] // nodes
    half = tokens // 2
    width = HEADS * HD

    def unpack(node, carry):
        for part in range(2):
            row = pl.ds(pl.multiple_of(node * tokens + part * half, half), half)
            col = 2 * part * width
            k_all[row, :] = moved_ref[node, Q_ROWS:, col : col + width]
            for head in range(HEADS):
                at = col + width + head * HD
                v_all[row, 2 * head * HD : (2 * head + 1) * HD] = moved_ref[node, Q_ROWS:, at : at + HD]
        return carry

    lax.fori_loop(0, nodes, unpack, 0)


def unpack_pieces(pieces, tokens, k_all, v_all):
    me = lax.axis_index("ctx")
    width = HEADS * HD
    for ref, (sender, blocks) in zip(pieces, HALVES):
        for place, offset in enumerate(blocks):
            node = jnp.bitwise_xor(me, sender ^ offset)
            row = pl.ds(pl.multiple_of(node * tokens, tokens), tokens)
            here = slice(place * tokens, (place + 1) * tokens)
            k_all[row, :] = ref[here, :width]
            for head in range(HEADS):
                at = width + head * HD
                v_all[row, 2 * head * HD : (2 * head + 1) * HD] = ref[here, at : at + HD]


def unpack_kernel(tokens, *refs):
    kv_refs, (k_all, v_all) = refs[:-2], refs[-2:]
    for head in range(HEADS):
        ones = jnp.ones((v_all.shape[0], HD), jnp.bfloat16)
        v_all[:, (2 * head + 1) * HD : (2 * head + 2) * HD] = ones
    if len(kv_refs) == 1:
        unpack_moved(kv_refs[0], k_all, v_all)
    else:
        unpack_pieces(kv_refs, tokens, k_all, v_all)


def attend_kernel(q_ref, pos_ref, start_ref, order_ref, k_all, v_all, *refs):
    out_refs, context = refs[:CORES], refs[CORES]
    total = k_all.shape[0]
    held = context.shape[0]
    block_rows = 32
    blocks = held // block_rows
    span = total // blocks
    scale = math.log2(math.e) / math.sqrt(HD)

    def rows_of(block):
        return slice(block * block_rows, (block + 1) * block_rows)

    def scores_of(block, head, keys):
        parts = block_rows // SUB
        mine = slice(head * SUB, (head + 1) * SUB)
        messages = [q_ref[block * parts + part].astype(jnp.float32)[mine] for part in range(parts)]
        pieces = []
        for group in range(GROUP):
            for message in messages:
                pieces.append(message[:, group * HD : (group + 1) * HD])
        return lax.dot_general(
            jnp.concatenate(pieces, axis=0).astype(jnp.bfloat16),
            k_all[keys, head * HD : (head + 1) * HD],
            (((1,), (1,)), ((), ())),
            preferred_element_type=jnp.float32,
        )

    def weights_of(block, keys, scores, peak=None):
        count = keys.stop - keys.start
        at = keys.start + lax.broadcasted_iota(jnp.int32, (block_rows, count), 1)
        seen = (at <= pos_ref[rows_of(block), :1]) & (at >= start_ref[rows_of(block), :1])
        scores = scores.reshape(GROUP, block_rows, count) + jnp.where(seen, 0.0, NEGATIVE)[None]
        scores = scores.reshape(GROUP * block_rows, count)
        top = jnp.max(scores, axis=1, keepdims=True)
        if peak is None:
            return top, jnp.exp2((scores - top) * scale).astype(jnp.bfloat16)
        top = jnp.maximum(peak, top)
        weights = jnp.exp2((scores - top) * scale).reshape(GROUP, block_rows, count)
        weights = jnp.where(seen[None], weights, 0.0).reshape(GROUP * block_rows, count)
        return top, weights.astype(jnp.bfloat16)

    def sums_of(head, keys, weights):
        values = v_all[keys, 2 * head * HD : (2 * head + 2) * HD]
        return jnp.dot(weights, values, preferred_element_type=jnp.float32)

    def store(block, head, sums):
        result = (sums[:, :HD] / sums[:, HD:]).astype(jnp.bfloat16)
        for group in range(GROUP):
            col = head * WIDE + group * HD
            part = result[group * block_rows : (group + 1) * block_rows]
            context[rows_of(block), col : col + HD] = part

    tasks = [
        (block, head, slice(max(0, block - blocks // 2) * span, (block + 1) * span))
        for block in reversed(range(blocks))
        for head in range(HEADS)
    ]
    most = 1024
    if max(keys.stop - keys.start for _, _, keys in tasks) <= most:
        scores, last = scores_of(*tasks[0]), None
        for index, (block, head, keys) in enumerate(tasks):
            later = scores_of(*tasks[index + 1]) if index + 1 < len(tasks) else None
            _, weights = weights_of(block, keys, scores)
            if last is not None:
                store(*last[:2], sums_of(*last[1:]))
            scores, last = later, (block, head, keys, weights)
        store(*last[:2], sums_of(*last[1:]))
    else:
        for block, head, keys in tasks:
            peak = jnp.full((GROUP * block_rows, 1), NEGATIVE, jnp.float32)
            sums = jnp.zeros((GROUP * block_rows, 2 * HD), jnp.float32)
            for lower in range(keys.start, keys.stop, most):
                part = slice(lower, min(lower + most, keys.stop))
                top, weights = weights_of(block, part, scores_of(block, head, part), peak)
                sums = sums * jnp.exp2((peak - top) * scale) + sums_of(head, part, weights)
                peak = top
            store(block, head, sums)

    rows = held // CORES
    for core in range(CORES):
        order = order_ref[core * rows : (core + 1) * rows, :]
        moved = jnp.dot(order, context[...], preferred_element_type=jnp.float32)
        out_refs[core][...] = moved.astype(jnp.bfloat16)


def write_kernel(other, heads_ref, *refs):
    out_hbm, sem = refs[-2:]
    core = jnp.bitwise_xor(lax.axis_index("ctx") % CORES, other)
    width = HEADS * WIDE
    side = pl.ds(pl.multiple_of(core * width, width), width)
    copy = pltpu.make_async_copy(heads_ref, out_hbm.at[:, side], sem)
    copy.start()
    copy.wait()


def on_device(queries, keys, values, owner, rollout_lengths):
    rows = queries.shape[0]
    nodes = lax.axis_size("ctx")
    total = owner.shape[0]
    chips = nodes // CORES
    per_chip = rows // chips
    held = rows * CORES
    table = owner.reshape(total // LANES, LANES)
    whole = pl.BlockSpec(memory_space=pltpu.VMEM)
    hbm = pl.BlockSpec(memory_space=pltpu.HBM)
    apart = nodes == 16

    def swap(array, offset):
        return lax.ppermute(array, "ctx", [(node, node ^ offset) for node in range(nodes)])

    kv_rows = 0 if apart else rows // 2
    message = jax.ShapeDtypeStruct((nodes, Q_ROWS + kv_rows, WIDE), jnp.bfloat16)
    order_in, q_near, kv_near = pl.pallas_call(
        fetch_kernel,
        out_shape=[
            jax.ShapeDtypeStruct((rows, rows), jnp.bfloat16),
            jax.ShapeDtypeStruct(queries.shape, jnp.bfloat16),
            jax.ShapeDtypeStruct((rows, 2 * KVH * HD), jnp.bfloat16),
        ],
        in_specs=[hbm] * 4,
        out_specs=[whole] * 3,
        scratch_shapes=[pltpu.VMEM(table.shape, jnp.int32), pltpu.SemaphoreType.DMA((4,))],
        compiler_params=VMEM,
        name="fetch",
    )(*(pltpu.with_memory_space_constraint(x, pltpu.HBM) for x in (table, queries, keys, values)))
    operands = (order_in, q_near) if apart else (order_in, q_near, kv_near)
    packed = pl.pallas_call(
        functools.partial(pack_kernel, chips),
        out_shape=message,
        in_specs=[whole] * len(operands),
        out_specs=whole,
        compiler_params=VMEM,
        cost_estimate=pl.CostEstimate(
            flops=2 * rows * rows * H * HD, bytes_accessed=4 * rows * H * HD, transcendentals=0
        ),
        name="pack",
    )(*operands)
    if apart:
        lanes = {offset: swap(kv_near, offset) if offset else kv_near for pair in WHOLE for offset in pair}

    moved = lax.all_to_all(packed, "ctx", split_axis=0, concat_axis=0, tiled=True)

    if apart:
        halves = {}
        for pair, flops in zip(WHOLE, (2 * 10**10, 2 * 10**10, 2 * 10**10)):
            halves[pair] = pl.pallas_call(
                heads_kernel,
                out_shape=[jax.ShapeDtypeStruct((2 * rows, 2 * HEADS * HD), jnp.bfloat16)] * CORES,
                in_specs=[whole] * 2,
                out_specs=[whole] * CORES,
                compiler_params=VMEM,
                cost_estimate=pl.CostEstimate(flops=flops, bytes_accessed=2**20, transcendentals=0),
                name="heads",
            )(*(lanes[offset] for offset in pair))
        kv_parts = []
        for sender, pair in HALVES:
            part = halves[pair][sender % CORES]
            kv_parts.append(swap(part, sender) if sender else part)
        q_part = moved
    else:
        kv_parts = [moved]
        groups = held // SUB
        q_part = moved[:, :Q_ROWS].reshape(groups, nodes // groups, HEADS, SUB, WIDE)[:, :, :, :per_chip]
        q_part = q_part.transpose(0, 2, 1, 3, 4).reshape(groups, Q_ROWS, WIDE)

    pos, start, order = pl.pallas_call(
        functools.partial(place_kernel, per_chip),
        out_shape=(
            jax.ShapeDtypeStruct((held, LANES), jnp.int32),
            jax.ShapeDtypeStruct((held, LANES), jnp.int32),
            jax.ShapeDtypeStruct((held, held), jnp.bfloat16),
        ),
        in_specs=[pl.BlockSpec(memory_space=pltpu.SMEM), whole],
        out_specs=(whole, whole, whole),
        compiler_params=VMEM,
        name="place",
    )(rollout_lengths, table)

    k_all, v_all = pl.pallas_call(
        functools.partial(unpack_kernel, rows),
        out_shape=[
            jax.ShapeDtypeStruct((total, HEADS * HD), jnp.bfloat16),
            jax.ShapeDtypeStruct((total, HEADS * 2 * HD), jnp.bfloat16),
        ],
        in_specs=[whole] * len(kv_parts),
        out_specs=[whole] * 2,
        compiler_params=VMEM,
        name="unpack",
    )(*kv_parts)
    own, other = pl.pallas_call(
        attend_kernel,
        out_shape=(jax.ShapeDtypeStruct((rows, HEADS * WIDE), jnp.bfloat16),) * CORES,
        in_specs=[whole] * 6,
        out_specs=(whole,) * CORES,
        scratch_shapes=[pltpu.VMEM((held, HEADS * WIDE), jnp.bfloat16)],
        compiler_params=VMEM,
        name="attend",
    )(q_part, pos, start, order, k_all, v_all)

    result = jax.ShapeDtypeStruct((rows, H * HD), jnp.bfloat16)
    half = pl.pallas_call(
        functools.partial(write_kernel, 0),
        out_shape=result,
        in_specs=[whole],
        out_specs=hbm,
        scratch_shapes=[pltpu.SemaphoreType.DMA],
        compiler_params=VMEM,
        name="write_own",
    )(own)
    return pl.pallas_call(
        functools.partial(write_kernel, 1),
        out_shape=result,
        in_specs=[whole, hbm],
        out_specs=hbm,
        scratch_shapes=[pltpu.SemaphoreType.DMA],
        input_output_aliases={1: 0},
        compiler_params=VMEM,
        name="write_received",
    )(swap(other, 1), half)


def solution(mesh):
    placed = (
        P(("groups", "ctx"), None),
        P(("groups", "ctx"), None),
        P(("groups", "ctx"), None),
        P("groups"),
        P("groups"),
    )
    return jax.shard_map(
        on_device, mesh=mesh, in_specs=placed, out_specs=P(("groups", "ctx"), None), check_vma=False
    )
```

```python
import functools
import math

import jax
import jax.numpy as jnp
from jax import lax
from jax.experimental import pallas as pl
from jax.experimental.pallas import tpu as pltpu
from jax.sharding import PartitionSpec as P

H = 32
KVH = 4
HD = 128
GROUP = H // KVH
WIDE = GROUP * HD
CORES = 2
HEADS = KVH // CORES
NEGATIVE = -1e30
LANES = 128
SUB = 8
Q_ROWS = HEADS * SUB
VMEM = pltpu.CompilerParams(vmem_limit_bytes=40 * 2**20)


def row_to_column(row):
    size = row.shape[1]
    here = lax.broadcasted_iota(jnp.int32, (size, size), 0)
    there = lax.broadcasted_iota(jnp.int32, (size, size), 1)
    return jnp.sum(jnp.where(here == there, row, 0), axis=1, keepdims=True)


def column_to_row(column):
    size = column.shape[0]
    here = lax.broadcasted_iota(jnp.int32, (size, size), 0)
    there = lax.broadcasted_iota(jnp.int32, (size, size), 1)
    return jnp.sum(jnp.where(here == there, column, 0), axis=0, keepdims=True)


def fetch_kernel(owner_hbm, q_hbm, k_hbm, v_hbm, order_ref, q_ref, kv_ref, owner_ref, sems):
    me = lax.axis_index("ctx")
    rows, width = k_hbm.shape
    copies = [
        pltpu.make_async_copy(owner_hbm, owner_ref, sems.at[0]),
        pltpu.make_async_copy(k_hbm, kv_ref.at[:, pl.ds(0, width)], sems.at[1]),
        pltpu.make_async_copy(v_hbm, kv_ref.at[:, pl.ds(width, width)], sems.at[2]),
        pltpu.make_async_copy(q_hbm, q_ref, sems.at[3]),
    ]
    for copy in copies:
        copy.start()
    copies[0].wait()
    both = owner_ref[pl.ds(me // 2, 1), :]
    swapped = jnp.concatenate((both[:, rows:], both[:, :rows]), axis=1)
    own = jnp.where(me % 2 == 1, swapped, both)[:, :rows]
    token = lax.broadcasted_iota(jnp.int32, (1, rows), 1)
    key_row = own * rows + token
    rank = jnp.sum((row_to_column(key_row) < key_row).astype(jnp.int32), axis=0, keepdims=True)
    place = lax.broadcasted_iota(jnp.int32, (rows, rows), 0)
    order_ref[...] = (place == rank).astype(jnp.float32).astype(jnp.bfloat16)
    for copy in copies[1:]:
        copy.wait()


def pack_kernel(chips, order_ref, q_ref, *refs):
    kv_refs, out_ref = refs[:-1], refs[-1]
    rows = q_ref.shape[0]
    per_chip = rows // chips
    order = order_ref[...]
    for core in range(CORES):
        sorted_q = []
        for head in range(core * HEADS, (core + 1) * HEADS):
            wide = slice(head * WIDE, (head + 1) * WIDE)
            sorted_q.append(jnp.dot(order, q_ref[:, wide], preferred_element_type=jnp.float32))
        for chip in range(chips):
            dest = chip * CORES + core
            parts = []
            for array in sorted_q:
                parts.append(array[chip * per_chip : (chip + 1) * per_chip])
                if per_chip < SUB:
                    parts.append(jnp.zeros((SUB - per_chip, WIDE), jnp.float32))
            out_ref[dest, :Q_ROWS, :] = jnp.concatenate(parts, axis=0).astype(jnp.bfloat16)
            if kv_refs:
                width = HEADS * HD
                half = rows // 2
                for part in range(2):
                    here = slice(part * half, (part + 1) * half)
                    for index in range(2):
                        col = (2 * part + index) * width
                        side = index * KVH * HD + core * width
                        block = kv_refs[0][here, side : side + width]
                        out_ref[dest, Q_ROWS:, col : col + width] = block


FAR = (12, 8)
DIAGONAL = 6
ALONG, ACROSS = 4, 2


def pair_kernel(mine_ref, other_ref, out_ref):
    rows = mine_ref.shape[0]
    core = lax.axis_index("ctx") % CORES
    out_ref[pl.ds(pl.multiple_of(core * rows, rows), rows), :] = mine_ref[...]
    out_ref[pl.ds(pl.multiple_of((1 - core) * rows, rows), rows), :] = other_ref[...]


def heads_kernel(*refs):
    outs = refs[-CORES:]
    core = lax.axis_index("ctx") % CORES
    width = HEADS * HD
    for index in range(CORES):
        col = jnp.bitwise_xor(core, index) * width
        first = 0
        for ref in refs[:-CORES]:
            here = slice(first, first + ref.shape[0])
            first = here.stop
            for half in range(2):
                side = pl.ds(pl.multiple_of(col + half * KVH * HD, width), width)
                outs[index][here, half * width : (half + 1) * width] = ref[:, side]


def place_kernel(per_chip, lengths_ref, owner_ref, pos_ref, start_ref, order_ref):
    me = lax.axis_index("ctx")
    chip, core = me // CORES, me % CORES
    table_rows = owner_ref.shape[0]
    total = table_rows * LANES
    held = pos_ref.shape[0]
    rows = LANES // 2
    shift = per_chip.bit_length() - 1
    block_rows = 32
    table_step = table_rows // (held // block_rows)
    first = lax.broadcasted_iota(jnp.int32, (LANES, LANES), 0)
    second = lax.broadcasted_iota(jnp.int32, (LANES, LANES), 1)
    same = (first < rows) == (second < rows)
    lane = lax.broadcasted_iota(jnp.int32, (1, LANES), 1)
    line = lax.broadcasted_iota(jnp.int32, (block_rows, 1), 0)
    wanted = chip * per_chip + jnp.bitwise_and(line, per_chip - 1)
    source = jnp.right_shift(line, shift)
    keys = []
    for block in range(held // block_rows):
        pos = jnp.zeros((block_rows, 1), jnp.int32)
        own = jnp.zeros((block_rows, 1), jnp.int32)
        for step in range(table_step):
            table = block * table_step + step
            owners = owner_ref[table : table + 1, :]
            key_row = owners * LANES + lane
            below = same & (row_to_column(key_row) < key_row)
            rank = jnp.sum(below.astype(jnp.int32), axis=0, keepdims=True)
            lane_source = 2 * step + (lane >= rows).astype(jnp.int32)
            hit = (wanted == rank) & (source == lane_source)
            pos += jnp.sum(jnp.where(hit, lane + table * LANES, 0), axis=1, keepdims=True)
            own += jnp.sum(jnp.where(hit, owners, 0), axis=1, keepdims=True)
        start = jnp.zeros((block_rows, 1), jnp.int32)
        end = jnp.int32(0)
        for rollout in range(lengths_ref.shape[0]):
            end = end + lengths_ref[rollout]
            start = jnp.where(pos >= end, end, start)
        here = slice(block * block_rows, (block + 1) * block_rows)
        pos_ref[here, :] = jnp.broadcast_to(pos, (block_rows, LANES))
        start_ref[here, :] = jnp.broadcast_to(start, (block_rows, LANES))
        keys.append((own - chip * CORES) * total + pos)
    key_col = jnp.concatenate(keys, axis=0)
    key_row = column_to_row(key_col)
    slot = jnp.sum((key_col < key_row).astype(jnp.int32), axis=0, keepdims=True)
    slot = jnp.bitwise_xor(slot, core * rows)
    place = lax.broadcasted_iota(jnp.int32, (held, held), 0)
    order_ref[...] = (place == slot).astype(jnp.float32).astype(jnp.bfloat16)


def unpack_moved(moved_ref, k_all, v_all):
    nodes = moved_ref.shape[0]
    tokens = k_all.shape[0] // nodes
    half = tokens // 2
    width = HEADS * HD

    def unpack(node, carry):
        for part in range(2):
            row = pl.ds(pl.multiple_of(node * tokens + part * half, half), half)
            col = 2 * part * width
            k_all[row, :] = moved_ref[node, Q_ROWS:, col : col + width]
            for head in range(HEADS):
                at = col + width + head * HD
                v_all[row, 2 * head * HD : (2 * head + 1) * HD] = moved_ref[node, Q_ROWS:, at : at + HD]
        return carry

    lax.fori_loop(0, nodes, unpack, 0)


def unpack_pieces(pieces, tokens, k_all, v_all):
    me = lax.axis_index("ctx")
    width = HEADS * HD

    def chip_of(sender):
        offset = jnp.where(sender % CORES == 0, ALONG, ACROSS)
        chip = jnp.bitwise_xor(sender, offset) // CORES
        return [chip * CORES + core for core in range(CORES)]

    senders = [jnp.bitwise_xor(me, index) for index in range(2 * CORES)]
    nodes = [[jnp.bitwise_xor(sender, offset) for offset in FAR] for sender in senders]
    nodes += [[jnp.bitwise_xor(sender, DIAGONAL)] + chip_of(sender) for sender in senders[:CORES]]
    nodes.append([me // CORES * CORES + core for core in range(CORES)])
    for ref, held in zip(pieces, nodes):
        for place, node in enumerate(held):
            row = pl.ds(pl.multiple_of(node * tokens, tokens), tokens)
            here = slice(place * tokens, (place + 1) * tokens)
            k_all[row, :] = ref[here, :width]
            for head in range(HEADS):
                at = width + head * HD
                v_all[row, 2 * head * HD : (2 * head + 1) * HD] = ref[here, at : at + HD]


def unpack_kernel(tokens, *refs):
    kv_refs, (k_all, v_all) = refs[:-2], refs[-2:]
    for head in range(HEADS):
        ones = jnp.ones((v_all.shape[0], HD), jnp.bfloat16)
        v_all[:, (2 * head + 1) * HD : (2 * head + 2) * HD] = ones
    if len(kv_refs) == 1:
        unpack_moved(kv_refs[0], k_all, v_all)
    else:
        unpack_pieces(kv_refs, tokens, k_all, v_all)


def attend_kernel(q_ref, pos_ref, start_ref, order_ref, k_all, v_all, *refs):
    out_refs, context = refs[:CORES], refs[CORES]
    total = k_all.shape[0]
    held = context.shape[0]
    block_rows = 32
    blocks = held // block_rows
    span = total // blocks
    scale = math.log2(math.e) / math.sqrt(HD)

    def rows_of(block):
        return slice(block * block_rows, (block + 1) * block_rows)

    def scores_of(block, head, keys):
        parts = block_rows // SUB
        mine = slice(head * SUB, (head + 1) * SUB)
        messages = [q_ref[block * parts + part].astype(jnp.float32)[mine] for part in range(parts)]
        pieces = []
        for group in range(GROUP):
            for message in messages:
                pieces.append(message[:, group * HD : (group + 1) * HD])
        return lax.dot_general(
            jnp.concatenate(pieces, axis=0).astype(jnp.bfloat16),
            k_all[keys, head * HD : (head + 1) * HD],
            (((1,), (1,)), ((), ())),
            preferred_element_type=jnp.float32,
        )

    def weights_of(block, keys, scores, peak=None):
        count = keys.stop - keys.start
        at = keys.start + lax.broadcasted_iota(jnp.int32, (block_rows, count), 1)
        seen = (at <= pos_ref[rows_of(block), :1]) & (at >= start_ref[rows_of(block), :1])
        scores = scores.reshape(GROUP, block_rows, count) + jnp.where(seen, 0.0, NEGATIVE)[None]
        scores = scores.reshape(GROUP * block_rows, count)
        top = jnp.max(scores, axis=1, keepdims=True)
        if peak is None:
            return top, jnp.exp2((scores - top) * scale).astype(jnp.bfloat16)
        top = jnp.maximum(peak, top)
        weights = jnp.exp2((scores - top) * scale).reshape(GROUP, block_rows, count)
        weights = jnp.where(seen[None], weights, 0.0).reshape(GROUP * block_rows, count)
        return top, weights.astype(jnp.bfloat16)

    def sums_of(head, keys, weights):
        values = v_all[keys, 2 * head * HD : (2 * head + 2) * HD]
        return jnp.dot(weights, values, preferred_element_type=jnp.float32)

    def store(block, head, sums):
        result = (sums[:, :HD] / sums[:, HD:]).astype(jnp.bfloat16)
        for group in range(GROUP):
            col = head * WIDE + group * HD
            part = result[group * block_rows : (group + 1) * block_rows]
            context[rows_of(block), col : col + HD] = part

    tasks = [
        (block, head, slice(max(0, block - blocks // 2) * span, (block + 1) * span))
        for block in reversed(range(blocks))
        for head in range(HEADS)
    ]
    most = 1024
    if max(keys.stop - keys.start for _, _, keys in tasks) <= most:
        scores, last = scores_of(*tasks[0]), None
        for index, (block, head, keys) in enumerate(tasks):
            later = scores_of(*tasks[index + 1]) if index + 1 < len(tasks) else None
            _, weights = weights_of(block, keys, scores)
            if last is not None:
                store(*last[:2], sums_of(*last[1:]))
            scores, last = later, (block, head, keys, weights)
        store(*last[:2], sums_of(*last[1:]))
    else:
        for block, head, keys in tasks:
            peak = jnp.full((GROUP * block_rows, 1), NEGATIVE, jnp.float32)
            sums = jnp.zeros((GROUP * block_rows, 2 * HD), jnp.float32)
            for lower in range(keys.start, keys.stop, most):
                part = slice(lower, min(lower + most, keys.stop))
                top, weights = weights_of(block, part, scores_of(block, head, part), peak)
                sums = sums * jnp.exp2((peak - top) * scale) + sums_of(head, part, weights)
                peak = top
            store(block, head, sums)

    rows = held // CORES
    for core in range(CORES):
        order = order_ref[core * rows : (core + 1) * rows, :]
        moved = jnp.dot(order, context[...], preferred_element_type=jnp.float32)
        out_refs[core][...] = moved.astype(jnp.bfloat16)


def write_kernel(other, heads_ref, *refs):
    out_hbm, sem = refs[-2:]
    core = jnp.bitwise_xor(lax.axis_index("ctx") % CORES, other)
    width = HEADS * WIDE
    side = pl.ds(pl.multiple_of(core * width, width), width)
    copy = pltpu.make_async_copy(heads_ref, out_hbm.at[:, side], sem)
    copy.start()
    copy.wait()


def on_device(queries, keys, values, owner, rollout_lengths):
    rows = queries.shape[0]
    nodes = lax.axis_size("ctx")
    total = owner.shape[0]
    chips = nodes // CORES
    per_chip = rows // chips
    held = rows * CORES
    table = owner.reshape(total // LANES, LANES)
    whole = pl.BlockSpec(memory_space=pltpu.VMEM)
    hbm = pl.BlockSpec(memory_space=pltpu.HBM)
    apart = nodes == 16

    def swap(array, *offsets):
        pairs = [(node, node ^ offsets[node % len(offsets)]) for node in range(nodes)]
        return lax.ppermute(array, "ctx", pairs)

    kv_rows = 0 if apart else rows // 2
    message = jax.ShapeDtypeStruct((nodes, Q_ROWS + kv_rows, WIDE), jnp.bfloat16)
    order_in, q_near, kv_near = pl.pallas_call(
        fetch_kernel,
        out_shape=[
            jax.ShapeDtypeStruct((rows, rows), jnp.bfloat16),
            jax.ShapeDtypeStruct(queries.shape, jnp.bfloat16),
            jax.ShapeDtypeStruct((rows, 2 * KVH * HD), jnp.bfloat16),
        ],
        in_specs=[hbm] * 4,
        out_specs=[whole] * 3,
        scratch_shapes=[pltpu.VMEM(table.shape, jnp.int32), pltpu.SemaphoreType.DMA((4,))],
        compiler_params=VMEM,
        name="fetch",
    )(*(pltpu.with_memory_space_constraint(x, pltpu.HBM) for x in (table, queries, keys, values)))
    if apart:
        other = swap(kv_near, 1)
        far = [swap(kv_near, offset) for offset in FAR]
        diagonal = swap(kv_near, DIAGONAL)
        chip = pl.pallas_call(
            pair_kernel,
            out_shape=jax.ShapeDtypeStruct((CORES * rows, 2 * KVH * HD), jnp.bfloat16),
            in_specs=[whole] * 2,
            out_specs=whole,
            compiler_params=VMEM,
            name="pair",
        )(kv_near, other)
        next_chip = swap(chip, ALONG, ACROSS)
        q_near, _ = lax.optimization_barrier((q_near, chip))

    operands = (order_in, q_near) if apart else (order_in, q_near, kv_near)
    packed = pl.pallas_call(
        functools.partial(pack_kernel, chips),
        out_shape=message,
        in_specs=[whole] * len(operands),
        out_specs=whole,
        compiler_params=VMEM,
        cost_estimate=pl.CostEstimate(
            flops=2 * rows * rows * H * HD, bytes_accessed=4 * rows * H * HD, transcendentals=0
        ),
        name="pack",
    )(*operands)
    moved = lax.all_to_all(packed, "ctx", split_axis=0, concat_axis=0, tiled=True)

    pos, start, order = pl.pallas_call(
        functools.partial(place_kernel, per_chip),
        out_shape=(
            jax.ShapeDtypeStruct((held, LANES), jnp.int32),
            jax.ShapeDtypeStruct((held, LANES), jnp.int32),
            jax.ShapeDtypeStruct((held, held), jnp.bfloat16),
        ),
        in_specs=[pl.BlockSpec(memory_space=pltpu.SMEM), whole],
        out_specs=(whole, whole, whole),
        compiler_params=VMEM,
        name="place",
    )(rollout_lengths, table)

    if apart:

        def heads_of(flops, *blocks):
            count = sum(block.shape[0] for block in blocks)
            return pl.pallas_call(
                heads_kernel,
                out_shape=[jax.ShapeDtypeStruct((count, 2 * HEADS * HD), jnp.bfloat16)] * CORES,
                in_specs=[whole] * len(blocks),
                out_specs=[whole] * CORES,
                compiler_params=VMEM,
                cost_estimate=pl.CostEstimate(flops=flops, bytes_accessed=2**20, transcendentals=0),
                name="heads",
            )(*blocks)

        mine_far, other_far = heads_of(2 * 10**10, *far)
        from_core, from_y, from_both = swap(other_far, 1), swap(mine_far, 2), swap(other_far, 3)
        mine_chip, _ = heads_of(10**6, chip)
        diagonal, next_chip, *_ = lax.optimization_barrier(
            (diagonal, next_chip, from_core, from_y, from_both, mine_chip, order)
        )
        mine_near, other_near = heads_of(10**6, diagonal, next_chip)
        kv_parts = [mine_far, from_core, from_y, from_both]
        kv_parts += [mine_near, swap(other_near, 1), mine_chip]
        q_part = moved
    else:
        kv_parts = [moved]
        groups = held // SUB
        q_part = moved[:, :Q_ROWS].reshape(groups, nodes // groups, HEADS, SUB, WIDE)[:, :, :, :per_chip]
        q_part = q_part.transpose(0, 2, 1, 3, 4).reshape(groups, Q_ROWS, WIDE)

    k_all, v_all = pl.pallas_call(
        functools.partial(unpack_kernel, rows),
        out_shape=[
            jax.ShapeDtypeStruct((total, HEADS * HD), jnp.bfloat16),
            jax.ShapeDtypeStruct((total, HEADS * 2 * HD), jnp.bfloat16),
        ],
        in_specs=[whole] * len(kv_parts),
        out_specs=[whole] * 2,
        compiler_params=VMEM,
        name="unpack",
    )(*kv_parts)
    own, other = pl.pallas_call(
        attend_kernel,
        out_shape=(jax.ShapeDtypeStruct((rows, HEADS * WIDE), jnp.bfloat16),) * CORES,
        in_specs=[whole] * 6,
        out_specs=(whole,) * CORES,
        scratch_shapes=[pltpu.VMEM((held, HEADS * WIDE), jnp.bfloat16)],
        compiler_params=VMEM,
        name="attend",
    )(q_part, pos, start, order, k_all, v_all)

    result = jax.ShapeDtypeStruct((rows, H * HD), jnp.bfloat16)
    half = pl.pallas_call(
        functools.partial(write_kernel, 0),
        out_shape=result,
        in_specs=[whole],
        out_specs=hbm,
        scratch_shapes=[pltpu.SemaphoreType.DMA],
        compiler_params=VMEM,
        name="write_own",
    )(own)
    return pl.pallas_call(
        functools.partial(write_kernel, 1),
        out_shape=result,
        in_specs=[whole, hbm],
        out_specs=hbm,
        scratch_shapes=[pltpu.SemaphoreType.DMA],
        input_output_aliases={1: 0},
        compiler_params=VMEM,
        name="write_received",
    )(swap(other, 1), half)


def solution(mesh):
    placed = (
        P(("groups", "ctx"), None),
        P(("groups", "ctx"), None),
        P(("groups", "ctx"), None),
        P("groups"),
        P("groups"),
    )
    return jax.shard_map(
        on_device, mesh=mesh, in_specs=placed, out_specs=P(("groups", "ctx"), None), check_vma=False
    )
```

```python
import functools
import math

import jax
import jax.numpy as jnp
from jax import lax
from jax.experimental import pallas as pl
from jax.experimental.pallas import tpu as pltpu
from jax.sharding import PartitionSpec as P

H = 32
KVH = 4
HD = 128
GROUP = H // KVH
WIDE = GROUP * HD
CORES = 2
HEADS = KVH // CORES
NEGATIVE = -1e30
LANES = 128
SUB = 8
Q_ROWS = HEADS * SUB
VMEM = pltpu.CompilerParams(vmem_limit_bytes=40 * 2**20)


def row_to_column(row):
    size = row.shape[1]
    here = lax.broadcasted_iota(jnp.int32, (size, size), 0)
    there = lax.broadcasted_iota(jnp.int32, (size, size), 1)
    return jnp.sum(jnp.where(here == there, row, 0), axis=1, keepdims=True)


def column_to_row(column):
    size = column.shape[0]
    here = lax.broadcasted_iota(jnp.int32, (size, size), 0)
    there = lax.broadcasted_iota(jnp.int32, (size, size), 1)
    return jnp.sum(jnp.where(here == there, column, 0), axis=0, keepdims=True)


def fetch_kernel(owner_hbm, q_hbm, k_hbm, v_hbm, order_ref, q_ref, kv_ref, owner_ref, sems):
    me = lax.axis_index("ctx")
    rows, width = k_hbm.shape
    copies = [
        pltpu.make_async_copy(owner_hbm, owner_ref, sems.at[0]),
        pltpu.make_async_copy(k_hbm, kv_ref.at[:, pl.ds(0, width)], sems.at[1]),
        pltpu.make_async_copy(v_hbm, kv_ref.at[:, pl.ds(width, width)], sems.at[2]),
        pltpu.make_async_copy(q_hbm, q_ref, sems.at[3]),
    ]
    for copy in copies:
        copy.start()
    copies[0].wait()
    both = owner_ref[pl.ds(me // 2, 1), :]
    swapped = jnp.concatenate((both[:, rows:], both[:, :rows]), axis=1)
    own = jnp.where(me % 2 == 1, swapped, both)[:, :rows]
    token = lax.broadcasted_iota(jnp.int32, (1, rows), 1)
    key_row = own * rows + token
    rank = jnp.sum((row_to_column(key_row) < key_row).astype(jnp.int32), axis=0, keepdims=True)
    place = lax.broadcasted_iota(jnp.int32, (rows, rows), 0)
    order_ref[...] = (place == rank).astype(jnp.float32).astype(jnp.bfloat16)
    for copy in copies[1:]:
        copy.wait()


def pack_kernel(chips, order_ref, q_ref, *refs):
    kv_refs, out_ref = refs[:-1], refs[-1]
    rows = q_ref.shape[0]
    per_chip = rows // chips
    order = order_ref[...]
    for core in range(CORES):
        sorted_q = []
        for head in range(core * HEADS, (core + 1) * HEADS):
            wide = slice(head * WIDE, (head + 1) * WIDE)
            sorted_q.append(jnp.dot(order, q_ref[:, wide], preferred_element_type=jnp.float32))
        for chip in range(chips):
            dest = chip * CORES + core
            parts = []
            for array in sorted_q:
                parts.append(array[chip * per_chip : (chip + 1) * per_chip])
                if per_chip < SUB:
                    parts.append(jnp.zeros((SUB - per_chip, WIDE), jnp.float32))
            out_ref[dest, :Q_ROWS, :] = jnp.concatenate(parts, axis=0).astype(jnp.bfloat16)
            if kv_refs:
                width = HEADS * HD
                half = rows // 2
                for part in range(2):
                    here = slice(part * half, (part + 1) * half)
                    for index in range(2):
                        col = (2 * part + index) * width
                        side = index * KVH * HD + core * width
                        block = kv_refs[0][here, side : side + width]
                        out_ref[dest, Q_ROWS:, col : col + width] = block


FAR = (12, 8)
DIAGONAL = 6
ALONG, ACROSS = 4, 2


def pair_kernel(mine_ref, other_ref, out_ref):
    rows = mine_ref.shape[0]
    core = lax.axis_index("ctx") % CORES
    out_ref[pl.ds(pl.multiple_of(core * rows, rows), rows), :] = mine_ref[...]
    out_ref[pl.ds(pl.multiple_of((1 - core) * rows, rows), rows), :] = other_ref[...]


def heads_kernel(count, *refs):
    blocks, mine, others = refs[: -count - 1], refs[-count - 1], refs[-count:]
    core = lax.axis_index("ctx") % CORES
    width = HEADS * HD
    rows = others[0].shape[0]
    first = 0
    for ref in blocks:
        size = min(rows, ref.shape[0])
        for begin in range(0, ref.shape[0], size):
            for half in range(2):
                to = slice(half * width, (half + 1) * width)
                col = half * KVH * HD
                side = pl.ds(pl.multiple_of(core * width + col, width), width)
                mine[first : first + size, to] = ref[begin : begin + size, side]
                side = pl.ds(pl.multiple_of((1 - core) * width + col, width), width)
                at = first % rows
                others[first // rows][at : at + size, to] = ref[begin : begin + size, side]
            first += size


def place_kernel(per_chip, lengths_ref, owner_ref, pos_ref, start_ref, order_ref):
    me = lax.axis_index("ctx")
    chip, core = me // CORES, me % CORES
    table_rows = owner_ref.shape[0]
    total = table_rows * LANES
    held = pos_ref.shape[0]
    rows = LANES // 2
    shift = per_chip.bit_length() - 1
    block_rows = 32
    table_step = table_rows // (held // block_rows)
    first = lax.broadcasted_iota(jnp.int32, (LANES, LANES), 0)
    second = lax.broadcasted_iota(jnp.int32, (LANES, LANES), 1)
    same = (first < rows) == (second < rows)
    lane = lax.broadcasted_iota(jnp.int32, (1, LANES), 1)
    line = lax.broadcasted_iota(jnp.int32, (block_rows, 1), 0)
    wanted = chip * per_chip + jnp.bitwise_and(line, per_chip - 1)
    source = jnp.right_shift(line, shift)
    keys = []
    for block in range(held // block_rows):
        pos = jnp.zeros((block_rows, 1), jnp.int32)
        own = jnp.zeros((block_rows, 1), jnp.int32)
        for step in range(table_step):
            table = block * table_step + step
            owners = owner_ref[table : table + 1, :]
            key_row = owners * LANES + lane
            below = same & (row_to_column(key_row) < key_row)
            rank = jnp.sum(below.astype(jnp.int32), axis=0, keepdims=True)
            lane_source = 2 * step + (lane >= rows).astype(jnp.int32)
            hit = (wanted == rank) & (source == lane_source)
            pos += jnp.sum(jnp.where(hit, lane + table * LANES, 0), axis=1, keepdims=True)
            own += jnp.sum(jnp.where(hit, owners, 0), axis=1, keepdims=True)
        start = jnp.zeros((block_rows, 1), jnp.int32)
        end = jnp.int32(0)
        for rollout in range(lengths_ref.shape[0]):
            end = end + lengths_ref[rollout]
            start = jnp.where(pos >= end, end, start)
        here = slice(block * block_rows, (block + 1) * block_rows)
        pos_ref[here, :] = jnp.broadcast_to(pos, (block_rows, LANES))
        start_ref[here, :] = jnp.broadcast_to(start, (block_rows, LANES))
        keys.append((own - chip * CORES) * total + pos)
    key_col = jnp.concatenate(keys, axis=0)
    key_row = column_to_row(key_col)
    slot = jnp.sum((key_col < key_row).astype(jnp.int32), axis=0, keepdims=True)
    slot = jnp.bitwise_xor(slot, core * rows)
    place = lax.broadcasted_iota(jnp.int32, (held, held), 0)
    order_ref[...] = (place == slot).astype(jnp.float32).astype(jnp.bfloat16)


def unpack_moved(moved_ref, k_all, v_all):
    nodes = moved_ref.shape[0]
    tokens = k_all.shape[0] // nodes
    half = tokens // 2
    width = HEADS * HD

    def unpack(node, carry):
        for part in range(2):
            row = pl.ds(pl.multiple_of(node * tokens + part * half, half), half)
            col = 2 * part * width
            k_all[row, :] = moved_ref[node, Q_ROWS:, col : col + width]
            for head in range(HEADS):
                at = col + width + head * HD
                v_all[row, 2 * head * HD : (2 * head + 1) * HD] = moved_ref[node, Q_ROWS:, at : at + HD]
        return carry

    lax.fori_loop(0, nodes, unpack, 0)


def unpack_pieces(pieces, tokens, k_all, v_all):
    me = lax.axis_index("ctx")
    width = HEADS * HD

    def chip_of(sender):
        offset = jnp.where(sender % CORES == 0, ALONG, ACROSS)
        chip = jnp.bitwise_xor(sender, offset) // CORES
        return [chip * CORES + core for core in range(CORES)]

    senders = [jnp.bitwise_xor(me, index) for index in range(2 * CORES)]
    nodes = [[jnp.bitwise_xor(sender, offset) for offset in FAR] for sender in senders]
    nodes.append([jnp.bitwise_xor(me, DIAGONAL)] + chip_of(me))
    nodes += [[node] for node in [jnp.bitwise_xor(senders[1], DIAGONAL)] + chip_of(senders[1])]
    nodes.append([me // CORES * CORES + core for core in range(CORES)])
    for ref, held in zip(pieces, nodes):
        for place, node in enumerate(held):
            row = pl.ds(pl.multiple_of(node * tokens, tokens), tokens)
            here = slice(place * tokens, (place + 1) * tokens)
            k_all[row, :] = ref[here, :width]
            for head in range(HEADS):
                at = width + head * HD
                v_all[row, 2 * head * HD : (2 * head + 1) * HD] = ref[here, at : at + HD]


def unpack_kernel(tokens, *refs):
    kv_refs, (k_all, v_all) = refs[:-2], refs[-2:]
    for head in range(HEADS):
        ones = jnp.ones((v_all.shape[0], HD), jnp.bfloat16)
        v_all[:, (2 * head + 1) * HD : (2 * head + 2) * HD] = ones
    if len(kv_refs) == 1:
        unpack_moved(kv_refs[0], k_all, v_all)
    else:
        unpack_pieces(kv_refs, tokens, k_all, v_all)


def attend_kernel(q_ref, pos_ref, start_ref, order_ref, k_all, v_all, *refs):
    out_refs, context = refs[:CORES], refs[CORES]
    total = k_all.shape[0]
    held = context.shape[0]
    block_rows = 32
    blocks = held // block_rows
    span = total // blocks
    scale = math.log2(math.e) / math.sqrt(HD)

    def rows_of(block):
        return slice(block * block_rows, (block + 1) * block_rows)

    def scores_of(block, head, keys):
        parts = block_rows // SUB
        mine = slice(head * SUB, (head + 1) * SUB)
        messages = [q_ref[block * parts + part].astype(jnp.float32)[mine] for part in range(parts)]
        pieces = []
        for group in range(GROUP):
            for message in messages:
                pieces.append(message[:, group * HD : (group + 1) * HD])
        return lax.dot_general(
            jnp.concatenate(pieces, axis=0).astype(jnp.bfloat16),
            k_all[keys, head * HD : (head + 1) * HD],
            (((1,), (1,)), ((), ())),
            preferred_element_type=jnp.float32,
        )

    def weights_of(block, keys, scores, peak=None):
        count = keys.stop - keys.start
        at = keys.start + lax.broadcasted_iota(jnp.int32, (block_rows, count), 1)
        seen = (at <= pos_ref[rows_of(block), :1]) & (at >= start_ref[rows_of(block), :1])
        scores = scores.reshape(GROUP, block_rows, count) + jnp.where(seen, 0.0, NEGATIVE)[None]
        scores = scores.reshape(GROUP * block_rows, count)
        top = jnp.max(scores, axis=1, keepdims=True)
        if peak is None:
            return top, jnp.exp2((scores - top) * scale).astype(jnp.bfloat16)
        top = jnp.maximum(peak, top)
        weights = jnp.exp2((scores - top) * scale).reshape(GROUP, block_rows, count)
        weights = jnp.where(seen[None], weights, 0.0).reshape(GROUP * block_rows, count)
        return top, weights.astype(jnp.bfloat16)

    def sums_of(head, keys, weights):
        values = v_all[keys, 2 * head * HD : (2 * head + 2) * HD]
        return jnp.dot(weights, values, preferred_element_type=jnp.float32)

    def store(block, head, sums):
        result = (sums[:, :HD] / sums[:, HD:]).astype(jnp.bfloat16)
        for group in range(GROUP):
            col = head * WIDE + group * HD
            part = result[group * block_rows : (group + 1) * block_rows]
            context[rows_of(block), col : col + HD] = part

    tasks = [
        (block, head, slice(max(0, block - blocks // 2) * span, (block + 1) * span))
        for block in reversed(range(blocks))
        for head in range(HEADS)
    ]
    most = 1024
    if max(keys.stop - keys.start for _, _, keys in tasks) <= most:
        scores, last = scores_of(*tasks[0]), None
        for index, (block, head, keys) in enumerate(tasks):
            later = scores_of(*tasks[index + 1]) if index + 1 < len(tasks) else None
            _, weights = weights_of(block, keys, scores)
            if last is not None:
                store(*last[:2], sums_of(*last[1:]))
            scores, last = later, (block, head, keys, weights)
        store(*last[:2], sums_of(*last[1:]))
    else:
        for block, head, keys in tasks:
            peak = jnp.full((GROUP * block_rows, 1), NEGATIVE, jnp.float32)
            sums = jnp.zeros((GROUP * block_rows, 2 * HD), jnp.float32)
            for lower in range(keys.start, keys.stop, most):
                part = slice(lower, min(lower + most, keys.stop))
                top, weights = weights_of(block, part, scores_of(block, head, part), peak)
                sums = sums * jnp.exp2((peak - top) * scale) + sums_of(head, part, weights)
                peak = top
            store(block, head, sums)

    rows = held // CORES
    for core in range(CORES):
        order = order_ref[core * rows : (core + 1) * rows, :]
        moved = jnp.dot(order, context[...], preferred_element_type=jnp.float32)
        out_refs[core][...] = moved.astype(jnp.bfloat16)


def write_kernel(other, heads_ref, *refs):
    out_hbm, sem = refs[-2:]
    core = jnp.bitwise_xor(lax.axis_index("ctx") % CORES, other)
    width = HEADS * WIDE
    side = pl.ds(pl.multiple_of(core * width, width), width)
    copy = pltpu.make_async_copy(heads_ref, out_hbm.at[:, side], sem)
    copy.start()
    copy.wait()


def on_device(queries, keys, values, owner, rollout_lengths):
    rows = queries.shape[0]
    nodes = lax.axis_size("ctx")
    total = owner.shape[0]
    chips = nodes // CORES
    per_chip = rows // chips
    held = rows * CORES
    table = owner.reshape(total // LANES, LANES)
    whole = pl.BlockSpec(memory_space=pltpu.VMEM)
    hbm = pl.BlockSpec(memory_space=pltpu.HBM)
    apart = nodes == 16

    def swap(array, *offsets):
        pairs = [(node, node ^ offsets[node % len(offsets)]) for node in range(nodes)]
        return lax.ppermute(array, "ctx", pairs)

    kv_rows = 0 if apart else rows // 2
    message = jax.ShapeDtypeStruct((nodes, Q_ROWS + kv_rows, WIDE), jnp.bfloat16)
    order_in, q_near, kv_near = pl.pallas_call(
        fetch_kernel,
        out_shape=[
            jax.ShapeDtypeStruct((rows, rows), jnp.bfloat16),
            jax.ShapeDtypeStruct(queries.shape, jnp.bfloat16),
            jax.ShapeDtypeStruct((rows, 2 * KVH * HD), jnp.bfloat16),
        ],
        in_specs=[hbm] * 4,
        out_specs=[whole] * 3,
        scratch_shapes=[pltpu.VMEM(table.shape, jnp.int32), pltpu.SemaphoreType.DMA((4,))],
        compiler_params=VMEM,
        name="fetch",
    )(*(pltpu.with_memory_space_constraint(x, pltpu.HBM) for x in (table, queries, keys, values)))
    if apart:
        other = swap(kv_near, 1)
        far = [swap(kv_near, offset) for offset in FAR]
        diagonal = swap(kv_near, DIAGONAL)
        chip = pl.pallas_call(
            pair_kernel,
            out_shape=jax.ShapeDtypeStruct((CORES * rows, 2 * KVH * HD), jnp.bfloat16),
            in_specs=[whole] * 2,
            out_specs=whole,
            compiler_params=VMEM,
            name="pair",
        )(kv_near, other)
        next_chip = swap(chip, ALONG, ACROSS)
        q_near, _ = lax.optimization_barrier((q_near, chip))

    operands = (order_in, q_near) if apart else (order_in, q_near, kv_near)
    packed = pl.pallas_call(
        functools.partial(pack_kernel, chips),
        out_shape=message,
        in_specs=[whole] * len(operands),
        out_specs=whole,
        compiler_params=VMEM,
        cost_estimate=pl.CostEstimate(
            flops=2 * rows * rows * H * HD, bytes_accessed=4 * rows * H * HD, transcendentals=0
        ),
        name="pack",
    )(*operands)
    moved = lax.all_to_all(packed, "ctx", split_axis=0, concat_axis=0, tiled=True)

    pos, start, order = pl.pallas_call(
        functools.partial(place_kernel, per_chip),
        out_shape=(
            jax.ShapeDtypeStruct((held, LANES), jnp.int32),
            jax.ShapeDtypeStruct((held, LANES), jnp.int32),
            jax.ShapeDtypeStruct((held, held), jnp.bfloat16),
        ),
        in_specs=[pl.BlockSpec(memory_space=pltpu.SMEM), whole],
        out_specs=(whole, whole, whole),
        compiler_params=VMEM,
        name="place",
    )(rollout_lengths, table)

    if apart:

        def heads_of(flops, count, *blocks):
            total_rows = sum(block.shape[0] for block in blocks)
            shapes = [total_rows] + [total_rows // count] * count
            return pl.pallas_call(
                functools.partial(heads_kernel, count),
                out_shape=[jax.ShapeDtypeStruct((n, 2 * HEADS * HD), jnp.bfloat16) for n in shapes],
                in_specs=[whole] * len(blocks),
                out_specs=[whole] * (1 + count),
                compiler_params=VMEM,
                cost_estimate=pl.CostEstimate(flops=flops, bytes_accessed=2**20, transcendentals=0),
                name="heads",
            )(*blocks)

        mine_far, other_far = heads_of(2 * 10**10, 1, *far)
        from_core, from_y, from_both = swap(other_far, 1), swap(mine_far, 2), swap(other_far, 3)
        mine_chip, _ = heads_of(10**6, 1, chip)
        diagonal, next_chip, *_ = lax.optimization_barrier((diagonal, next_chip, order, mine_chip))
        mine_near, *other_near = heads_of(10**6, 1 + CORES, diagonal, next_chip)
        kv_parts = [mine_far, from_core, from_y, from_both, mine_near]
        kv_parts += [swap(part, 1) for part in other_near] + [mine_chip]
        q_part = moved
    else:
        kv_parts = [moved]
        groups = held // SUB
        q_part = moved[:, :Q_ROWS].reshape(groups, nodes // groups, HEADS, SUB, WIDE)[:, :, :, :per_chip]
        q_part = q_part.transpose(0, 2, 1, 3, 4).reshape(groups, Q_ROWS, WIDE)

    k_all, v_all = pl.pallas_call(
        functools.partial(unpack_kernel, rows),
        out_shape=[
            jax.ShapeDtypeStruct((total, HEADS * HD), jnp.bfloat16),
            jax.ShapeDtypeStruct((total, HEADS * 2 * HD), jnp.bfloat16),
        ],
        in_specs=[whole] * len(kv_parts),
        out_specs=[whole] * 2,
        compiler_params=VMEM,
        name="unpack",
    )(*kv_parts)
    own, other = pl.pallas_call(
        attend_kernel,
        out_shape=(jax.ShapeDtypeStruct((rows, HEADS * WIDE), jnp.bfloat16),) * CORES,
        in_specs=[whole] * 6,
        out_specs=(whole,) * CORES,
        scratch_shapes=[pltpu.VMEM((held, HEADS * WIDE), jnp.bfloat16)],
        compiler_params=VMEM,
        name="attend",
    )(q_part, pos, start, order, k_all, v_all)

    result = jax.ShapeDtypeStruct((rows, H * HD), jnp.bfloat16)
    half = pl.pallas_call(
        functools.partial(write_kernel, 0),
        out_shape=result,
        in_specs=[whole],
        out_specs=hbm,
        scratch_shapes=[pltpu.SemaphoreType.DMA],
        compiler_params=VMEM,
        name="write_own",
    )(own)
    return pl.pallas_call(
        functools.partial(write_kernel, 1),
        out_shape=result,
        in_specs=[whole, hbm],
        out_specs=hbm,
        scratch_shapes=[pltpu.SemaphoreType.DMA],
        input_output_aliases={1: 0},
        compiler_params=VMEM,
        name="write_received",
    )(swap(other, 1), half)


def solution(mesh):
    placed = (
        P(("groups", "ctx"), None),
        P(("groups", "ctx"), None),
        P(("groups", "ctx"), None),
        P("groups"),
        P("groups"),
    )
    return jax.shard_map(
        on_device, mesh=mesh, in_specs=placed, out_specs=P(("groups", "ctx"), None), check_vma=False
    )
```

```python
import functools
import math

import jax
import jax.numpy as jnp
from jax import lax
from jax.experimental import pallas as pl
from jax.experimental.pallas import tpu as pltpu
from jax.sharding import PartitionSpec as P

H = 32
KVH = 4
HD = 128
GROUP = H // KVH
WIDE = GROUP * HD
CORES = 2
HEADS = KVH // CORES
NEGATIVE = -1e30
LANES = 128
SUB = 8
Q_ROWS = HEADS * SUB
VMEM = pltpu.CompilerParams(vmem_limit_bytes=40 * 2**20)


def row_to_column(row):
    size = row.shape[1]
    here = lax.broadcasted_iota(jnp.int32, (size, size), 0)
    there = lax.broadcasted_iota(jnp.int32, (size, size), 1)
    return jnp.sum(jnp.where(here == there, row, 0), axis=1, keepdims=True)


def column_to_row(column):
    size = column.shape[0]
    here = lax.broadcasted_iota(jnp.int32, (size, size), 0)
    there = lax.broadcasted_iota(jnp.int32, (size, size), 1)
    return jnp.sum(jnp.where(here == there, column, 0), axis=0, keepdims=True)


def fetch_kernel(owner_hbm, q_hbm, k_hbm, v_hbm, order_ref, q_ref, kv_ref, owner_ref, sems):
    me = lax.axis_index("ctx")
    rows, width = k_hbm.shape
    copies = [
        pltpu.make_async_copy(owner_hbm, owner_ref, sems.at[0]),
        pltpu.make_async_copy(k_hbm, kv_ref.at[:, pl.ds(0, width)], sems.at[1]),
        pltpu.make_async_copy(v_hbm, kv_ref.at[:, pl.ds(width, width)], sems.at[2]),
        pltpu.make_async_copy(q_hbm, q_ref, sems.at[3]),
    ]
    for copy in copies:
        copy.start()
    copies[0].wait()
    both = owner_ref[pl.ds(me // 2, 1), :]
    swapped = jnp.concatenate((both[:, rows:], both[:, :rows]), axis=1)
    own = jnp.where(me % 2 == 1, swapped, both)[:, :rows]
    token = lax.broadcasted_iota(jnp.int32, (1, rows), 1)
    key_row = own * rows + token
    rank = jnp.sum((row_to_column(key_row) < key_row).astype(jnp.int32), axis=0, keepdims=True)
    place = lax.broadcasted_iota(jnp.int32, (rows, rows), 0)
    order_ref[...] = (place == rank).astype(jnp.float32).astype(jnp.bfloat16)
    for copy in copies[1:]:
        copy.wait()


def pack_kernel(chips, order_ref, q_ref, *refs):
    kv_refs, out_ref = refs[:-1], refs[-1]
    rows = q_ref.shape[0]
    per_chip = rows // chips
    order = order_ref[...]
    for core in range(CORES):
        sorted_q = []
        for head in range(core * HEADS, (core + 1) * HEADS):
            wide = slice(head * WIDE, (head + 1) * WIDE)
            sorted_q.append(jnp.dot(order, q_ref[:, wide], preferred_element_type=jnp.float32))
        for chip in range(chips):
            dest = chip * CORES + core
            parts = []
            for array in sorted_q:
                parts.append(array[chip * per_chip : (chip + 1) * per_chip])
                if per_chip < SUB:
                    parts.append(jnp.zeros((SUB - per_chip, WIDE), jnp.float32))
            out_ref[dest, :Q_ROWS, :] = jnp.concatenate(parts, axis=0).astype(jnp.bfloat16)
            if kv_refs:
                width = HEADS * HD
                half = rows // 2
                for part in range(2):
                    here = slice(part * half, (part + 1) * half)
                    for index in range(2):
                        col = (2 * part + index) * width
                        side = index * KVH * HD + core * width
                        block = kv_refs[0][here, side : side + width]
                        out_ref[dest, Q_ROWS:, col : col + width] = block


FAR = (12, 8)
DIAGONAL = 6
ALONG, ACROSS = 4, 2


def pair_kernel(mine_ref, other_ref, out_ref):
    rows = mine_ref.shape[0]
    core = lax.axis_index("ctx") % CORES
    out_ref[pl.ds(pl.multiple_of(core * rows, rows), rows), :] = mine_ref[...]
    out_ref[pl.ds(pl.multiple_of((1 - core) * rows, rows), rows), :] = other_ref[...]


def heads_kernel(count, *refs):
    blocks, mine, others = refs[: -count - 1], refs[-count - 1], refs[-count:]
    core = lax.axis_index("ctx") % CORES
    width = HEADS * HD
    rows = others[0].shape[0]
    first = 0
    for ref in blocks:
        size = min(rows, ref.shape[0])
        for begin in range(0, ref.shape[0], size):
            for half in range(2):
                to = slice(half * width, (half + 1) * width)
                col = half * KVH * HD
                side = pl.ds(pl.multiple_of(core * width + col, width), width)
                mine[first : first + size, to] = ref[begin : begin + size, side]
                side = pl.ds(pl.multiple_of((1 - core) * width + col, width), width)
                at = first % rows
                others[first // rows][at : at + size, to] = ref[begin : begin + size, side]
            first += size


def place_kernel(per_chip, lengths_ref, owner_ref, pos_ref, start_ref, order_ref):
    me = lax.axis_index("ctx")
    chip, core = me // CORES, me % CORES
    table_rows = owner_ref.shape[0]
    total = table_rows * LANES
    held = pos_ref.shape[0]
    rows = LANES // 2
    shift = per_chip.bit_length() - 1
    block_rows = 32
    table_step = table_rows // (held // block_rows)
    first = lax.broadcasted_iota(jnp.int32, (LANES, LANES), 0)
    second = lax.broadcasted_iota(jnp.int32, (LANES, LANES), 1)
    same = (first < rows) == (second < rows)
    lane = lax.broadcasted_iota(jnp.int32, (1, LANES), 1)
    line = lax.broadcasted_iota(jnp.int32, (block_rows, 1), 0)
    wanted = chip * per_chip + jnp.bitwise_and(line, per_chip - 1)
    source = jnp.right_shift(line, shift)
    keys = []
    for block in range(held // block_rows):
        pos = jnp.zeros((block_rows, 1), jnp.int32)
        own = jnp.zeros((block_rows, 1), jnp.int32)
        for step in range(table_step):
            table = block * table_step + step
            owners = owner_ref[table : table + 1, :]
            key_row = owners * LANES + lane
            below = same & (row_to_column(key_row) < key_row)
            rank = jnp.sum(below.astype(jnp.int32), axis=0, keepdims=True)
            lane_source = 2 * step + (lane >= rows).astype(jnp.int32)
            hit = (wanted == rank) & (source == lane_source)
            pos += jnp.sum(jnp.where(hit, lane + table * LANES, 0), axis=1, keepdims=True)
            own += jnp.sum(jnp.where(hit, owners, 0), axis=1, keepdims=True)
        start = jnp.zeros((block_rows, 1), jnp.int32)
        end = jnp.int32(0)
        for rollout in range(lengths_ref.shape[0]):
            end = end + lengths_ref[rollout]
            start = jnp.where(pos >= end, end, start)
        here = slice(block * block_rows, (block + 1) * block_rows)
        pos_ref[here, :] = jnp.broadcast_to(pos, (block_rows, LANES))
        start_ref[here, :] = jnp.broadcast_to(start, (block_rows, LANES))
        keys.append((own - chip * CORES) * total + pos)
    key_col = jnp.concatenate(keys, axis=0)
    key_row = column_to_row(key_col)
    slot = jnp.sum((key_col < key_row).astype(jnp.int32), axis=0, keepdims=True)
    slot = jnp.bitwise_xor(slot, core * rows)
    place = lax.broadcasted_iota(jnp.int32, (held, held), 0)
    order_ref[...] = (place == slot).astype(jnp.float32).astype(jnp.bfloat16)


def unpack_moved(moved_ref, k_all, v_all):
    nodes = moved_ref.shape[0]
    tokens = k_all.shape[0] // nodes
    half = tokens // 2
    width = HEADS * HD

    def unpack(node, carry):
        for part in range(2):
            row = pl.ds(pl.multiple_of(node * tokens + part * half, half), half)
            col = 2 * part * width
            k_all[row, :] = moved_ref[node, Q_ROWS:, col : col + width]
            for head in range(HEADS):
                at = col + width + head * HD
                v_all[row, 2 * head * HD : (2 * head + 1) * HD] = moved_ref[node, Q_ROWS:, at : at + HD]
        return carry

    lax.fori_loop(0, nodes, unpack, 0)


def unpack_pieces(pieces, tokens, k_all, v_all):
    me = lax.axis_index("ctx")
    width = HEADS * HD

    def chip_of(sender):
        offset = jnp.where(sender % CORES == 0, ALONG, ACROSS)
        chip = jnp.bitwise_xor(sender, offset) // CORES
        return [chip * CORES + core for core in range(CORES)]

    senders = [jnp.bitwise_xor(me, index) for index in range(2 * CORES)]
    nodes = [[jnp.bitwise_xor(sender, offset) for offset in FAR] for sender in senders]
    nodes.append([jnp.bitwise_xor(me, DIAGONAL)] + chip_of(me))
    nodes += [[node] for node in [jnp.bitwise_xor(senders[1], DIAGONAL)] + chip_of(senders[1])]
    nodes.append([me // CORES * CORES + core for core in range(CORES)])
    for ref, held in zip(pieces, nodes):
        for place, node in enumerate(held):
            row = pl.ds(pl.multiple_of(node * tokens, tokens), tokens)
            here = slice(place * tokens, (place + 1) * tokens)
            k_all[row, :] = ref[here, :width]
            for head in range(HEADS):
                at = width + head * HD
                v_all[row, 2 * head * HD : (2 * head + 1) * HD] = ref[here, at : at + HD]


def unpack_kernel(tokens, *refs):
    kv_refs, (k_all, v_all) = refs[:-2], refs[-2:]
    for head in range(HEADS):
        ones = jnp.ones((v_all.shape[0], HD), jnp.bfloat16)
        v_all[:, (2 * head + 1) * HD : (2 * head + 2) * HD] = ones
    if len(kv_refs) == 1:
        unpack_moved(kv_refs[0], k_all, v_all)
    else:
        unpack_pieces(kv_refs, tokens, k_all, v_all)


def attend_kernel(q_ref, pos_ref, start_ref, order_ref, k_all, v_all, context, other_ref):
    total = k_all.shape[0]
    held = context.shape[0]
    block_rows = 32
    blocks = held // block_rows
    span = total // blocks
    scale = math.log2(math.e) / math.sqrt(HD)

    def rows_of(block):
        return slice(block * block_rows, (block + 1) * block_rows)

    def scores_of(block, head, keys):
        parts = block_rows // SUB
        mine = slice(head * SUB, (head + 1) * SUB)
        messages = [q_ref[block * parts + part].astype(jnp.float32)[mine] for part in range(parts)]
        pieces = []
        for group in range(GROUP):
            for message in messages:
                pieces.append(message[:, group * HD : (group + 1) * HD])
        return lax.dot_general(
            jnp.concatenate(pieces, axis=0).astype(jnp.bfloat16),
            k_all[keys, head * HD : (head + 1) * HD],
            (((1,), (1,)), ((), ())),
            preferred_element_type=jnp.float32,
        )

    def weights_of(block, keys, scores, peak=None):
        count = keys.stop - keys.start
        at = keys.start + lax.broadcasted_iota(jnp.int32, (block_rows, count), 1)
        seen = (at <= pos_ref[rows_of(block), :1]) & (at >= start_ref[rows_of(block), :1])
        scores = scores.reshape(GROUP, block_rows, count) + jnp.where(seen, 0.0, NEGATIVE)[None]
        scores = scores.reshape(GROUP * block_rows, count)
        top = jnp.max(scores, axis=1, keepdims=True)
        if peak is None:
            return top, jnp.exp2((scores - top) * scale).astype(jnp.bfloat16)
        top = jnp.maximum(peak, top)
        weights = jnp.exp2((scores - top) * scale).reshape(GROUP, block_rows, count)
        weights = jnp.where(seen[None], weights, 0.0).reshape(GROUP * block_rows, count)
        return top, weights.astype(jnp.bfloat16)

    def sums_of(head, keys, weights):
        values = v_all[keys, 2 * head * HD : (2 * head + 2) * HD]
        return jnp.dot(weights, values, preferred_element_type=jnp.float32)

    def store(block, head, sums):
        result = (sums[:, :HD] / sums[:, HD:]).astype(jnp.bfloat16)
        for group in range(GROUP):
            col = head * WIDE + group * HD
            part = result[group * block_rows : (group + 1) * block_rows]
            context[rows_of(block), col : col + HD] = part

    tasks = [
        (block, head, slice(max(0, block - blocks // 2) * span, (block + 1) * span))
        for block in reversed(range(blocks))
        for head in range(HEADS)
    ]
    most = 1024
    if max(keys.stop - keys.start for _, _, keys in tasks) <= most:
        scores, last = scores_of(*tasks[0]), None
        for index, (block, head, keys) in enumerate(tasks):
            later = scores_of(*tasks[index + 1]) if index + 1 < len(tasks) else None
            _, weights = weights_of(block, keys, scores)
            if last is not None:
                store(*last[:2], sums_of(*last[1:]))
            scores, last = later, (block, head, keys, weights)
        store(*last[:2], sums_of(*last[1:]))
    else:
        for block, head, keys in tasks:
            peak = jnp.full((GROUP * block_rows, 1), NEGATIVE, jnp.float32)
            sums = jnp.zeros((GROUP * block_rows, 2 * HD), jnp.float32)
            for lower in range(keys.start, keys.stop, most):
                part = slice(lower, min(lower + most, keys.stop))
                top, weights = weights_of(block, part, scores_of(block, head, part), peak)
                sums = sums * jnp.exp2((peak - top) * scale) + sums_of(head, part, weights)
                peak = top
            store(block, head, sums)

    moved = jnp.dot(order_ref[held // CORES :, :], context[...], preferred_element_type=jnp.float32)
    other_ref[...] = moved.astype(jnp.bfloat16)


def copy_to_columns(core, source_ref, out_hbm, sem):
    width = HEADS * WIDE
    side = pl.ds(pl.multiple_of(core * width, width), width)
    copy = pltpu.make_async_copy(source_ref, out_hbm.at[:, side], sem)
    copy.start()
    copy.wait()


def write_own_kernel(order_ref, context_ref, out_hbm, own_ref, sem):
    order = order_ref[: own_ref.shape[0], :]
    moved = jnp.dot(order, context_ref[...], preferred_element_type=jnp.float32)
    own_ref[...] = moved.astype(jnp.bfloat16)
    copy_to_columns(lax.axis_index("ctx") % CORES, own_ref, out_hbm, sem)


def write_received_kernel(received_ref, half_hbm, out_hbm, sem):
    copy_to_columns(1 - lax.axis_index("ctx") % CORES, received_ref, out_hbm, sem)


def on_device(queries, keys, values, owner, rollout_lengths):
    rows = queries.shape[0]
    nodes = lax.axis_size("ctx")
    total = owner.shape[0]
    chips = nodes // CORES
    per_chip = rows // chips
    held = rows * CORES
    table = owner.reshape(total // LANES, LANES)
    whole = pl.BlockSpec(memory_space=pltpu.VMEM)
    hbm = pl.BlockSpec(memory_space=pltpu.HBM)
    apart = nodes == 16

    def swap(array, *offsets):
        pairs = [(node, node ^ offsets[node % len(offsets)]) for node in range(nodes)]
        return lax.ppermute(array, "ctx", pairs)

    kv_rows = 0 if apart else rows // 2
    message = jax.ShapeDtypeStruct((nodes, Q_ROWS + kv_rows, WIDE), jnp.bfloat16)
    order_in, q_near, kv_near = pl.pallas_call(
        fetch_kernel,
        out_shape=[
            jax.ShapeDtypeStruct((rows, rows), jnp.bfloat16),
            jax.ShapeDtypeStruct(queries.shape, jnp.bfloat16),
            jax.ShapeDtypeStruct((rows, 2 * KVH * HD), jnp.bfloat16),
        ],
        in_specs=[hbm] * 4,
        out_specs=[whole] * 3,
        scratch_shapes=[pltpu.VMEM(table.shape, jnp.int32), pltpu.SemaphoreType.DMA((4,))],
        compiler_params=VMEM,
        name="fetch",
    )(*(pltpu.with_memory_space_constraint(x, pltpu.HBM) for x in (table, queries, keys, values)))
    if apart:
        other = swap(kv_near, 1)
        far = [swap(kv_near, offset) for offset in FAR]
        diagonal = swap(kv_near, DIAGONAL)
        chip = pl.pallas_call(
            pair_kernel,
            out_shape=jax.ShapeDtypeStruct((CORES * rows, 2 * KVH * HD), jnp.bfloat16),
            in_specs=[whole] * 2,
            out_specs=whole,
            compiler_params=VMEM,
            name="pair",
        )(kv_near, other)
        next_chip = swap(chip, ALONG, ACROSS)
        q_near, _ = lax.optimization_barrier((q_near, chip))

    operands = (order_in, q_near) if apart else (order_in, q_near, kv_near)
    packed = pl.pallas_call(
        functools.partial(pack_kernel, chips),
        out_shape=message,
        in_specs=[whole] * len(operands),
        out_specs=whole,
        compiler_params=VMEM,
        cost_estimate=pl.CostEstimate(
            flops=2 * rows * rows * H * HD, bytes_accessed=4 * rows * H * HD, transcendentals=0
        ),
        name="pack",
    )(*operands)
    moved = lax.all_to_all(packed, "ctx", split_axis=0, concat_axis=0, tiled=True)

    pos, start, order = pl.pallas_call(
        functools.partial(place_kernel, per_chip),
        out_shape=(
            jax.ShapeDtypeStruct((held, LANES), jnp.int32),
            jax.ShapeDtypeStruct((held, LANES), jnp.int32),
            jax.ShapeDtypeStruct((held, held), jnp.bfloat16),
        ),
        in_specs=[pl.BlockSpec(memory_space=pltpu.SMEM), whole],
        out_specs=(whole, whole, whole),
        compiler_params=VMEM,
        name="place",
    )(rollout_lengths, table)

    if apart:

        def heads_of(flops, count, *blocks):
            total_rows = sum(block.shape[0] for block in blocks)
            shapes = [total_rows] + [total_rows // count] * count
            return pl.pallas_call(
                functools.partial(heads_kernel, count),
                out_shape=[jax.ShapeDtypeStruct((n, 2 * HEADS * HD), jnp.bfloat16) for n in shapes],
                in_specs=[whole] * len(blocks),
                out_specs=[whole] * (1 + count),
                compiler_params=VMEM,
                cost_estimate=pl.CostEstimate(flops=flops, bytes_accessed=2**20, transcendentals=0),
                name="heads",
            )(*blocks)

        mine_far, other_far = heads_of(2 * 10**10, 1, *far)
        from_core, from_y, from_both = swap(other_far, 1), swap(mine_far, 2), swap(other_far, 3)
        mine_chip, _ = heads_of(10**6, 1, chip)
        diagonal, next_chip, *_ = lax.optimization_barrier((diagonal, next_chip, order))
        mine_near, *other_near = heads_of(10**6, 1 + CORES, diagonal, next_chip)
        kv_parts = [mine_far, from_core, from_y, from_both, mine_near]
        kv_parts += [swap(part, 1) for part in other_near] + [mine_chip]
        q_part = moved
    else:
        kv_parts = [moved]
        groups = held // SUB
        q_part = moved[:, :Q_ROWS].reshape(groups, nodes // groups, HEADS, SUB, WIDE)[:, :, :, :per_chip]
        q_part = q_part.transpose(0, 2, 1, 3, 4).reshape(groups, Q_ROWS, WIDE)

    k_all, v_all = pl.pallas_call(
        functools.partial(unpack_kernel, rows),
        out_shape=[
            jax.ShapeDtypeStruct((total, HEADS * HD), jnp.bfloat16),
            jax.ShapeDtypeStruct((total, HEADS * 2 * HD), jnp.bfloat16),
        ],
        in_specs=[whole] * len(kv_parts),
        out_specs=[whole] * 2,
        compiler_params=VMEM,
        name="unpack",
    )(*kv_parts)
    context, other = pl.pallas_call(
        attend_kernel,
        out_shape=(
            jax.ShapeDtypeStruct((held, HEADS * WIDE), jnp.bfloat16),
            jax.ShapeDtypeStruct((rows, HEADS * WIDE), jnp.bfloat16),
        ),
        in_specs=[whole] * 6,
        out_specs=(whole, whole),
        compiler_params=VMEM,
        name="attend",
    )(q_part, pos, start, order, k_all, v_all)

    result = jax.ShapeDtypeStruct((rows, H * HD), jnp.bfloat16)
    half = pl.pallas_call(
        write_own_kernel,
        out_shape=result,
        in_specs=[whole] * 2,
        out_specs=hbm,
        scratch_shapes=[pltpu.VMEM((rows, HEADS * WIDE), jnp.bfloat16), pltpu.SemaphoreType.DMA],
        compiler_params=VMEM,
        name="write_own",
    )(order, context)
    return pl.pallas_call(
        write_received_kernel,
        out_shape=result,
        in_specs=[whole, hbm],
        out_specs=hbm,
        scratch_shapes=[pltpu.SemaphoreType.DMA],
        input_output_aliases={1: 0},
        compiler_params=VMEM,
        name="write_received",
    )(swap(other, 1), half)


def solution(mesh):
    placed = (
        P(("groups", "ctx"), None),
        P(("groups", "ctx"), None),
        P(("groups", "ctx"), None),
        P("groups"),
        P("groups"),
    )
    return jax.shard_map(
        on_device, mesh=mesh, in_specs=placed, out_specs=P(("groups", "ctx"), None), check_vma=False
    )
```

```python
import functools
import math

import jax
import jax.numpy as jnp
from jax import lax
from jax.experimental import pallas as pl
from jax.experimental.pallas import tpu as pltpu
from jax.sharding import PartitionSpec as P

H = 32
KVH = 4
HD = 128
GROUP = H // KVH
WIDE = GROUP * HD
CORES = 2
HEADS = KVH // CORES
NEGATIVE = -1e30
LANES = 128
SUB = 8
Q_ROWS = HEADS * SUB
VMEM = pltpu.CompilerParams(vmem_limit_bytes=40 * 2**20)


def row_to_column(row):
    size = row.shape[1]
    here = lax.broadcasted_iota(jnp.int32, (size, size), 0)
    there = lax.broadcasted_iota(jnp.int32, (size, size), 1)
    return jnp.sum(jnp.where(here == there, row, 0), axis=1, keepdims=True)


def column_to_row(column):
    size = column.shape[0]
    here = lax.broadcasted_iota(jnp.int32, (size, size), 0)
    there = lax.broadcasted_iota(jnp.int32, (size, size), 1)
    return jnp.sum(jnp.where(here == there, column, 0), axis=0, keepdims=True)


def fetch_kernel(owner_hbm, q_hbm, k_hbm, v_hbm, order_ref, q_ref, kv_ref, owner_ref, sems):
    me = lax.axis_index("ctx")
    rows, width = k_hbm.shape
    copies = [
        pltpu.make_async_copy(owner_hbm, owner_ref, sems.at[0]),
        pltpu.make_async_copy(k_hbm, kv_ref.at[:, pl.ds(0, width)], sems.at[1]),
        pltpu.make_async_copy(v_hbm, kv_ref.at[:, pl.ds(width, width)], sems.at[2]),
        pltpu.make_async_copy(q_hbm, q_ref, sems.at[3]),
    ]
    for copy in copies:
        copy.start()
    copies[0].wait()
    both = owner_ref[pl.ds(me // 2, 1), :]
    swapped = jnp.concatenate((both[:, rows:], both[:, :rows]), axis=1)
    own = jnp.where(me % 2 == 1, swapped, both)[:, :rows]
    token = lax.broadcasted_iota(jnp.int32, (1, rows), 1)
    key_row = own * rows + token
    rank = jnp.sum((row_to_column(key_row) < key_row).astype(jnp.int32), axis=0, keepdims=True)
    place = lax.broadcasted_iota(jnp.int32, (rows, rows), 0)
    order_ref[...] = (place == rank).astype(jnp.float32).astype(jnp.bfloat16)
    for copy in copies[1:]:
        copy.wait()


def pack_kernel(chips, order_ref, q_ref, *refs):
    kv_refs, out_ref = refs[:-1], refs[-1]
    rows = q_ref.shape[0]
    per_chip = rows // chips
    order = order_ref[...]
    for core in range(CORES):
        sorted_q = []
        for head in range(core * HEADS, (core + 1) * HEADS):
            wide = slice(head * WIDE, (head + 1) * WIDE)
            sorted_q.append(jnp.dot(order, q_ref[:, wide], preferred_element_type=jnp.float32))
        for chip in range(chips):
            dest = chip * CORES + core
            parts = []
            for array in sorted_q:
                parts.append(array[chip * per_chip : (chip + 1) * per_chip])
                if per_chip < SUB:
                    parts.append(jnp.zeros((SUB - per_chip, WIDE), jnp.float32))
            out_ref[dest, :Q_ROWS, :] = jnp.concatenate(parts, axis=0).astype(jnp.bfloat16)
            if kv_refs:
                width = HEADS * HD
                half = rows // 2
                for part in range(2):
                    here = slice(part * half, (part + 1) * half)
                    for index in range(2):
                        col = (2 * part + index) * width
                        side = index * KVH * HD + core * width
                        block = kv_refs[0][here, side : side + width]
                        out_ref[dest, Q_ROWS:, col : col + width] = block


FAR = (12, 8)
DIAGONAL = 6
ALONG, ACROSS = 4, 2


def pair_kernel(mine_ref, other_ref, out_ref):
    rows = mine_ref.shape[0]
    core = lax.axis_index("ctx") % CORES
    out_ref[pl.ds(pl.multiple_of(core * rows, rows), rows), :] = mine_ref[...]
    out_ref[pl.ds(pl.multiple_of((1 - core) * rows, rows), rows), :] = other_ref[...]


def heads_kernel(count, *refs):
    blocks, mine, others = refs[: -count - 1], refs[-count - 1], refs[-count:]
    core = lax.axis_index("ctx") % CORES
    width = HEADS * HD
    rows = others[0].shape[0]
    first = 0
    for ref in blocks:
        size = min(rows, ref.shape[0])
        for begin in range(0, ref.shape[0], size):
            for half in range(2):
                to = slice(half * width, (half + 1) * width)
                col = half * KVH * HD
                side = pl.ds(pl.multiple_of(core * width + col, width), width)
                mine[first : first + size, to] = ref[begin : begin + size, side]
                side = pl.ds(pl.multiple_of((1 - core) * width + col, width), width)
                at = first % rows
                others[first // rows][at : at + size, to] = ref[begin : begin + size, side]
            first += size


def place_kernel(per_chip, lengths_ref, owner_ref, pos_ref, start_ref, order_ref):
    me = lax.axis_index("ctx")
    chip, core = me // CORES, me % CORES
    table_rows = owner_ref.shape[0]
    total = table_rows * LANES
    held = pos_ref.shape[0]
    rows = LANES // 2
    shift = per_chip.bit_length() - 1
    block_rows = 32
    table_step = table_rows // (held // block_rows)
    first = lax.broadcasted_iota(jnp.int32, (LANES, LANES), 0)
    second = lax.broadcasted_iota(jnp.int32, (LANES, LANES), 1)
    same = (first < rows) == (second < rows)
    lane = lax.broadcasted_iota(jnp.int32, (1, LANES), 1)
    line = lax.broadcasted_iota(jnp.int32, (block_rows, 1), 0)
    wanted = chip * per_chip + jnp.bitwise_and(line, per_chip - 1)
    source = jnp.right_shift(line, shift)
    keys = []
    for block in range(held // block_rows):
        pos = jnp.zeros((block_rows, 1), jnp.int32)
        own = jnp.zeros((block_rows, 1), jnp.int32)
        for step in range(table_step):
            table = block * table_step + step
            owners = owner_ref[table : table + 1, :]
            key_row = owners * LANES + lane
            below = same & (row_to_column(key_row) < key_row)
            rank = jnp.sum(below.astype(jnp.int32), axis=0, keepdims=True)
            lane_source = 2 * step + (lane >= rows).astype(jnp.int32)
            hit = (wanted == rank) & (source == lane_source)
            pos += jnp.sum(jnp.where(hit, lane + table * LANES, 0), axis=1, keepdims=True)
            own += jnp.sum(jnp.where(hit, owners, 0), axis=1, keepdims=True)
        start = jnp.zeros((block_rows, 1), jnp.int32)
        end = jnp.int32(0)
        for rollout in range(lengths_ref.shape[0]):
            end = end + lengths_ref[rollout]
            start = jnp.where(pos >= end, end, start)
        here = slice(block * block_rows, (block + 1) * block_rows)
        pos_ref[here, :] = jnp.broadcast_to(pos, (block_rows, LANES))
        start_ref[here, :] = jnp.broadcast_to(start, (block_rows, LANES))
        keys.append((own - chip * CORES) * total + pos)
    key_col = jnp.concatenate(keys, axis=0)
    key_row = column_to_row(key_col)
    slot = jnp.sum((key_col < key_row).astype(jnp.int32), axis=0, keepdims=True)
    slot = jnp.bitwise_xor(slot, core * rows)
    place = lax.broadcasted_iota(jnp.int32, (held, held), 0)
    order_ref[...] = (place == slot).astype(jnp.float32).astype(jnp.bfloat16)


def unpack_moved(moved_ref, k_all, v_all):
    nodes = moved_ref.shape[0]
    tokens = k_all.shape[0] // nodes
    half = tokens // 2
    width = HEADS * HD

    def unpack(node, carry):
        for part in range(2):
            row = pl.ds(pl.multiple_of(node * tokens + part * half, half), half)
            col = 2 * part * width
            k_all[row, :] = moved_ref[node, Q_ROWS:, col : col + width]
            for head in range(HEADS):
                at = col + width + head * HD
                v_all[row, 2 * head * HD : (2 * head + 1) * HD] = moved_ref[node, Q_ROWS:, at : at + HD]
        return carry

    lax.fori_loop(0, nodes, unpack, 0)


def unpack_pieces(pieces, tokens, k_all, v_all):
    me = lax.axis_index("ctx")
    width = HEADS * HD

    def chip_of(sender):
        offset = jnp.where(sender % CORES == 0, ALONG, ACROSS)
        chip = jnp.bitwise_xor(sender, offset) // CORES
        return [chip * CORES + core for core in range(CORES)]

    senders = [jnp.bitwise_xor(me, index) for index in range(2 * CORES)]
    nodes = [[jnp.bitwise_xor(sender, offset) for offset in FAR] for sender in senders]
    nodes.append([jnp.bitwise_xor(me, DIAGONAL)] + chip_of(me))
    nodes += [[node] for node in [jnp.bitwise_xor(senders[1], DIAGONAL)] + chip_of(senders[1])]
    nodes.append([me // CORES * CORES + core for core in range(CORES)])
    for ref, held in zip(pieces, nodes):
        for place, node in enumerate(held):
            row = pl.ds(pl.multiple_of(node * tokens, tokens), tokens)
            here = slice(place * tokens, (place + 1) * tokens)
            k_all[row, :] = ref[here, :width]
            for head in range(HEADS):
                at = width + head * HD
                v_all[row, 2 * head * HD : (2 * head + 1) * HD] = ref[here, at : at + HD]


def unpack_kernel(tokens, *refs):
    kv_refs, (k_all, v_all) = refs[:-2], refs[-2:]
    for head in range(HEADS):
        ones = jnp.ones((v_all.shape[0], HD), jnp.bfloat16)
        v_all[:, (2 * head + 1) * HD : (2 * head + 2) * HD] = ones
    if len(kv_refs) == 1:
        unpack_moved(kv_refs[0], k_all, v_all)
    else:
        unpack_pieces(kv_refs, tokens, k_all, v_all)


def attend_kernel(q_ref, pos_ref, start_ref, order_ref, k_all, v_all, context, other_ref):
    total = k_all.shape[0]
    held = context.shape[0]
    block_rows = 32
    blocks = held // block_rows
    span = total // blocks
    scale = math.log2(math.e) / math.sqrt(HD)

    def rows_of(block):
        return slice(block * block_rows, (block + 1) * block_rows)

    def scores_of(block, head, keys):
        parts = block_rows // SUB
        mine = slice(head * SUB, (head + 1) * SUB)
        messages = [q_ref[block * parts + part].astype(jnp.float32)[mine] for part in range(parts)]
        pieces = []
        for group in range(GROUP):
            for message in messages:
                pieces.append(message[:, group * HD : (group + 1) * HD])
        return lax.dot_general(
            jnp.concatenate(pieces, axis=0).astype(jnp.bfloat16),
            k_all[keys, head * HD : (head + 1) * HD],
            (((1,), (1,)), ((), ())),
            preferred_element_type=jnp.float32,
        )

    def weights_of(block, keys, scores, peak=None):
        count = keys.stop - keys.start
        at = keys.start + lax.broadcasted_iota(jnp.int32, (block_rows, count), 1)
        seen = (at <= pos_ref[rows_of(block), :1]) & (at >= start_ref[rows_of(block), :1])
        scores = scores.reshape(GROUP, block_rows, count) + jnp.where(seen, 0.0, NEGATIVE)[None]
        scores = scores.reshape(GROUP * block_rows, count)
        top = jnp.max(scores, axis=1, keepdims=True)
        if peak is None:
            return top, jnp.exp2((scores - top) * scale).astype(jnp.bfloat16)
        top = jnp.maximum(peak, top)
        weights = jnp.exp2((scores - top) * scale).reshape(GROUP, block_rows, count)
        weights = jnp.where(seen[None], weights, 0.0).reshape(GROUP * block_rows, count)
        return top, weights.astype(jnp.bfloat16)

    def sums_of(head, keys, weights):
        values = v_all[keys, 2 * head * HD : (2 * head + 2) * HD]
        return jnp.dot(weights, values, preferred_element_type=jnp.float32)

    def store(block, head, sums):
        result = (sums[:, :HD] / sums[:, HD:]).astype(jnp.bfloat16)
        for group in range(GROUP):
            col = head * WIDE + group * HD
            part = result[group * block_rows : (group + 1) * block_rows]
            context[rows_of(block), col : col + HD] = part

    tasks = [
        (block, head, slice(max(0, block - blocks // 2) * span, (block + 1) * span))
        for block in reversed(range(blocks))
        for head in range(HEADS)
    ]
    most = 1024
    if max(keys.stop - keys.start for _, _, keys in tasks) <= most:
        scores, last = scores_of(*tasks[0]), None
        for index, (block, head, keys) in enumerate(tasks):
            later = scores_of(*tasks[index + 1]) if index + 1 < len(tasks) else None
            _, weights = weights_of(block, keys, scores)
            if last is not None:
                store(*last[:2], sums_of(*last[1:]))
            scores, last = later, (block, head, keys, weights)
        store(*last[:2], sums_of(*last[1:]))
    else:
        for block, head, keys in tasks:
            peak = jnp.full((GROUP * block_rows, 1), NEGATIVE, jnp.float32)
            sums = jnp.zeros((GROUP * block_rows, 2 * HD), jnp.float32)
            for lower in range(keys.start, keys.stop, most):
                part = slice(lower, min(lower + most, keys.stop))
                top, weights = weights_of(block, part, scores_of(block, head, part), peak)
                sums = sums * jnp.exp2((peak - top) * scale) + sums_of(head, part, weights)
                peak = top
            store(block, head, sums)

    moved = jnp.dot(order_ref[held // CORES :, :], context[...], preferred_element_type=jnp.float32)
    other_ref[...] = moved.astype(jnp.bfloat16)


def copy_to_columns(core, source_ref, out_hbm, sem):
    width = HEADS * WIDE
    side = pl.ds(pl.multiple_of(core * width, width), width)
    copy = pltpu.make_async_copy(source_ref, out_hbm.at[:, side], sem)
    copy.start()
    copy.wait()


def write_own_kernel(order_ref, context_ref, out_hbm, own_ref, sem):
    order = order_ref[: own_ref.shape[0], :]
    moved = jnp.dot(order, context_ref[...], preferred_element_type=jnp.float32)
    own_ref[...] = moved.astype(jnp.bfloat16)
    copy_to_columns(lax.axis_index("ctx") % CORES, own_ref, out_hbm, sem)


def write_received_kernel(received_ref, half_hbm, out_hbm, sem):
    copy_to_columns(1 - lax.axis_index("ctx") % CORES, received_ref, out_hbm, sem)


def on_device(queries, keys, values, owner, rollout_lengths):
    rows = queries.shape[0]
    nodes = lax.axis_size("ctx")
    total = owner.shape[0]
    chips = nodes // CORES
    per_chip = rows // chips
    held = rows * CORES
    table = owner.reshape(total // LANES, LANES)
    whole = pl.BlockSpec(memory_space=pltpu.VMEM)
    hbm = pl.BlockSpec(memory_space=pltpu.HBM)
    apart = nodes == 16

    def swap(array, *offsets):
        pairs = [(node, node ^ offsets[node % len(offsets)]) for node in range(nodes)]
        return lax.ppermute(array, "ctx", pairs)

    kv_rows = 0 if apart else rows // 2
    message = jax.ShapeDtypeStruct((nodes, Q_ROWS + kv_rows, WIDE), jnp.bfloat16)
    order_in, q_near, kv_near = pl.pallas_call(
        fetch_kernel,
        out_shape=[
            jax.ShapeDtypeStruct((rows, rows), jnp.bfloat16),
            jax.ShapeDtypeStruct(queries.shape, jnp.bfloat16),
            jax.ShapeDtypeStruct((rows, 2 * KVH * HD), jnp.bfloat16),
        ],
        in_specs=[hbm] * 4,
        out_specs=[whole] * 3,
        scratch_shapes=[pltpu.VMEM(table.shape, jnp.int32), pltpu.SemaphoreType.DMA((4,))],
        compiler_params=VMEM,
        name="fetch",
    )(*(pltpu.with_memory_space_constraint(x, pltpu.HBM) for x in (table, queries, keys, values)))
    if apart:
        other = swap(kv_near, 1)
        far = [swap(kv_near, offset) for offset in FAR]
        diagonal = swap(kv_near, DIAGONAL)
        chip = pl.pallas_call(
            pair_kernel,
            out_shape=jax.ShapeDtypeStruct((CORES * rows, 2 * KVH * HD), jnp.bfloat16),
            in_specs=[whole] * 2,
            out_specs=whole,
            compiler_params=VMEM,
            name="pair",
        )(kv_near, other)
        next_chip = swap(chip, ALONG, ACROSS)
        q_near, _ = lax.optimization_barrier((q_near, chip))

    operands = (order_in, q_near) if apart else (order_in, q_near, kv_near)
    packed = pl.pallas_call(
        functools.partial(pack_kernel, chips),
        out_shape=message,
        in_specs=[whole] * len(operands),
        out_specs=whole,
        compiler_params=VMEM,
        cost_estimate=pl.CostEstimate(
            flops=2 * rows * rows * H * HD, bytes_accessed=4 * rows * H * HD, transcendentals=0
        ),
        name="pack",
    )(*operands)
    moved = lax.all_to_all(packed, "ctx", split_axis=0, concat_axis=0, tiled=True)

    pos, start, order = pl.pallas_call(
        functools.partial(place_kernel, per_chip),
        out_shape=(
            jax.ShapeDtypeStruct((held, LANES), jnp.int32),
            jax.ShapeDtypeStruct((held, LANES), jnp.int32),
            jax.ShapeDtypeStruct((held, held), jnp.bfloat16),
        ),
        in_specs=[pl.BlockSpec(memory_space=pltpu.SMEM), whole],
        out_specs=(whole, whole, whole),
        compiler_params=VMEM,
        name="place",
    )(rollout_lengths, table)

    if apart:

        def heads_of(flops, count, *blocks):
            total_rows = sum(block.shape[0] for block in blocks)
            shapes = [total_rows] + [total_rows // count] * count
            return pl.pallas_call(
                functools.partial(heads_kernel, count),
                out_shape=[jax.ShapeDtypeStruct((n, 2 * HEADS * HD), jnp.bfloat16) for n in shapes],
                in_specs=[whole] * len(blocks),
                out_specs=[whole] * (1 + count),
                compiler_params=VMEM,
                cost_estimate=pl.CostEstimate(flops=flops, bytes_accessed=2**20, transcendentals=0),
                name="heads",
            )(*blocks)

        mine_far, other_far = heads_of(2 * 10**10, 1, *far)
        from_both, from_y, from_core = swap(other_far, 3), swap(mine_far, 2), swap(other_far, 1)
        mine_chip, _ = heads_of(10**6, 1, chip)
        diagonal, next_chip, *_ = lax.optimization_barrier((diagonal, next_chip, order))
        mine_near, *other_near = heads_of(10**6, 1 + CORES, diagonal, next_chip)
        kv_parts = [mine_far, from_core, from_y, from_both, mine_near]
        kv_parts += [swap(part, 1) for part in other_near] + [mine_chip]
        q_part = moved
    else:
        kv_parts = [moved]
        groups = held // SUB
        q_part = moved[:, :Q_ROWS].reshape(groups, nodes // groups, HEADS, SUB, WIDE)[:, :, :, :per_chip]
        q_part = q_part.transpose(0, 2, 1, 3, 4).reshape(groups, Q_ROWS, WIDE)

    k_all, v_all = pl.pallas_call(
        functools.partial(unpack_kernel, rows),
        out_shape=[
            jax.ShapeDtypeStruct((total, HEADS * HD), jnp.bfloat16),
            jax.ShapeDtypeStruct((total, HEADS * 2 * HD), jnp.bfloat16),
        ],
        in_specs=[whole] * len(kv_parts),
        out_specs=[whole] * 2,
        compiler_params=VMEM,
        name="unpack",
    )(*kv_parts)
    context, other = pl.pallas_call(
        attend_kernel,
        out_shape=(
            jax.ShapeDtypeStruct((held, HEADS * WIDE), jnp.bfloat16),
            jax.ShapeDtypeStruct((rows, HEADS * WIDE), jnp.bfloat16),
        ),
        in_specs=[whole] * 6,
        out_specs=(whole, whole),
        compiler_params=VMEM,
        name="attend",
    )(q_part, pos, start, order, k_all, v_all)

    result = jax.ShapeDtypeStruct((rows, H * HD), jnp.bfloat16)
    half = pl.pallas_call(
        write_own_kernel,
        out_shape=result,
        in_specs=[whole] * 2,
        out_specs=hbm,
        scratch_shapes=[pltpu.VMEM((rows, HEADS * WIDE), jnp.bfloat16), pltpu.SemaphoreType.DMA],
        compiler_params=VMEM,
        name="write_own",
    )(order, context)
    return pl.pallas_call(
        write_received_kernel,
        out_shape=result,
        in_specs=[whole, hbm],
        out_specs=hbm,
        scratch_shapes=[pltpu.SemaphoreType.DMA],
        input_output_aliases={1: 0},
        compiler_params=VMEM,
        name="write_received",
    )(swap(other, 1), half)


def solution(mesh):
    placed = (
        P(("groups", "ctx"), None),
        P(("groups", "ctx"), None),
        P(("groups", "ctx"), None),
        P("groups"),
        P("groups"),
    )
    return jax.shard_map(
        on_device, mesh=mesh, in_specs=placed, out_specs=P(("groups", "ctx"), None), check_vma=False
    )
```

```python
import functools
import math

import jax
import jax.numpy as jnp
from jax import lax
from jax.experimental import pallas as pl
from jax.experimental.pallas import tpu as pltpu
from jax.sharding import PartitionSpec as P

H = 32
KVH = 4
HD = 128
GROUP = H // KVH
WIDE = GROUP * HD
CORES = 2
HEADS = KVH // CORES
NEGATIVE = -1e30
LANES = 128
SUB = 8
Q_ROWS = HEADS * SUB
VMEM = pltpu.CompilerParams(vmem_limit_bytes=40 * 2**20)


def row_to_column(row):
    size = row.shape[1]
    here = lax.broadcasted_iota(jnp.int32, (size, size), 0)
    there = lax.broadcasted_iota(jnp.int32, (size, size), 1)
    return jnp.sum(jnp.where(here == there, row, 0), axis=1, keepdims=True)


def column_to_row(column):
    size = column.shape[0]
    here = lax.broadcasted_iota(jnp.int32, (size, size), 0)
    there = lax.broadcasted_iota(jnp.int32, (size, size), 1)
    return jnp.sum(jnp.where(here == there, column, 0), axis=0, keepdims=True)


def fetch_kernel(owner_hbm, q_hbm, k_hbm, v_hbm, order_ref, q_ref, kv_ref, owner_ref, sems):
    me = lax.axis_index("ctx")
    rows, width = k_hbm.shape
    copies = [
        pltpu.make_async_copy(owner_hbm, owner_ref, sems.at[0]),
        pltpu.make_async_copy(k_hbm, kv_ref.at[:, pl.ds(0, width)], sems.at[1]),
        pltpu.make_async_copy(v_hbm, kv_ref.at[:, pl.ds(width, width)], sems.at[2]),
        pltpu.make_async_copy(q_hbm, q_ref, sems.at[3]),
    ]
    for copy in copies:
        copy.start()
    copies[0].wait()
    both = owner_ref[pl.ds(me // 2, 1), :]
    swapped = jnp.concatenate((both[:, rows:], both[:, :rows]), axis=1)
    own = jnp.where(me % 2 == 1, swapped, both)[:, :rows]
    token = lax.broadcasted_iota(jnp.int32, (1, rows), 1)
    key_row = own * rows + token
    rank = jnp.sum((row_to_column(key_row) < key_row).astype(jnp.int32), axis=0, keepdims=True)
    place = lax.broadcasted_iota(jnp.int32, (rows, rows), 0)
    order_ref[...] = (place == rank).astype(jnp.float32).astype(jnp.bfloat16)
    for copy in copies[1:]:
        copy.wait()


def pack_kernel(chips, order_ref, q_ref, *refs):
    kv_refs, out_ref = refs[:-1], refs[-1]
    rows = q_ref.shape[0]
    per_chip = rows // chips
    order = order_ref[...]
    for core in range(CORES):
        sorted_q = []
        for head in range(core * HEADS, (core + 1) * HEADS):
            wide = slice(head * WIDE, (head + 1) * WIDE)
            sorted_q.append(jnp.dot(order, q_ref[:, wide], preferred_element_type=jnp.float32))
        for chip in range(chips):
            dest = chip * CORES + core
            parts = []
            for array in sorted_q:
                parts.append(array[chip * per_chip : (chip + 1) * per_chip])
                if per_chip < SUB:
                    parts.append(jnp.zeros((SUB - per_chip, WIDE), jnp.float32))
            out_ref[dest, :Q_ROWS, :] = jnp.concatenate(parts, axis=0).astype(jnp.bfloat16)
            if kv_refs:
                width = HEADS * HD
                half = rows // 2
                for part in range(2):
                    here = slice(part * half, (part + 1) * half)
                    for index in range(2):
                        col = (2 * part + index) * width
                        side = index * KVH * HD + core * width
                        block = kv_refs[0][here, side : side + width]
                        out_ref[dest, Q_ROWS:, col : col + width] = block


FAR = (12, 8)
DIAGONAL = 6
ALONG, ACROSS = 4, 2


def pair_kernel(mine_ref, other_ref, out_ref):
    rows = mine_ref.shape[0]
    core = lax.axis_index("ctx") % CORES
    out_ref[pl.ds(pl.multiple_of(core * rows, rows), rows), :] = mine_ref[...]
    out_ref[pl.ds(pl.multiple_of((1 - core) * rows, rows), rows), :] = other_ref[...]


def heads_kernel(count, *refs):
    blocks, mine, others = refs[: -count - 1], refs[-count - 1], refs[-count:]
    core = lax.axis_index("ctx") % CORES
    width = HEADS * HD
    rows = others[0].shape[0]
    first = 0
    for ref in blocks:
        size = min(rows, ref.shape[0])
        for begin in range(0, ref.shape[0], size):
            for half in range(2):
                to = slice(half * width, (half + 1) * width)
                col = half * KVH * HD
                side = pl.ds(pl.multiple_of(core * width + col, width), width)
                mine[first : first + size, to] = ref[begin : begin + size, side]
                side = pl.ds(pl.multiple_of((1 - core) * width + col, width), width)
                at = first % rows
                others[first // rows][at : at + size, to] = ref[begin : begin + size, side]
            first += size


def place_kernel(per_chip, lengths_ref, owner_ref, pos_ref, start_ref, order_ref):
    me = lax.axis_index("ctx")
    chip, core = me // CORES, me % CORES
    table_rows = owner_ref.shape[0]
    total = table_rows * LANES
    held = pos_ref.shape[0]
    rows = LANES // 2
    shift = per_chip.bit_length() - 1
    block_rows = 32
    table_step = table_rows // (held // block_rows)
    first = lax.broadcasted_iota(jnp.int32, (LANES, LANES), 0)
    second = lax.broadcasted_iota(jnp.int32, (LANES, LANES), 1)
    same = (first < rows) == (second < rows)
    lane = lax.broadcasted_iota(jnp.int32, (1, LANES), 1)
    line = lax.broadcasted_iota(jnp.int32, (block_rows, 1), 0)
    wanted = chip * per_chip + jnp.bitwise_and(line, per_chip - 1)
    source = jnp.right_shift(line, shift)
    keys = []
    for block in range(held // block_rows):
        pos = jnp.zeros((block_rows, 1), jnp.int32)
        own = jnp.zeros((block_rows, 1), jnp.int32)
        for step in range(table_step):
            table = block * table_step + step
            owners = owner_ref[table : table + 1, :]
            key_row = owners * LANES + lane
            below = same & (row_to_column(key_row) < key_row)
            rank = jnp.sum(below.astype(jnp.int32), axis=0, keepdims=True)
            lane_source = 2 * step + (lane >= rows).astype(jnp.int32)
            hit = (wanted == rank) & (source == lane_source)
            pos += jnp.sum(jnp.where(hit, lane + table * LANES, 0), axis=1, keepdims=True)
            own += jnp.sum(jnp.where(hit, owners, 0), axis=1, keepdims=True)
        start = jnp.zeros((block_rows, 1), jnp.int32)
        end = jnp.int32(0)
        for rollout in range(lengths_ref.shape[0]):
            end = end + lengths_ref[rollout]
            start = jnp.where(pos >= end, end, start)
        here = slice(block * block_rows, (block + 1) * block_rows)
        pos_ref[here, :] = jnp.broadcast_to(pos, (block_rows, LANES))
        start_ref[here, :] = jnp.broadcast_to(start, (block_rows, LANES))
        keys.append((own - chip * CORES) * total + pos)
    key_col = jnp.concatenate(keys, axis=0)
    key_row = column_to_row(key_col)
    slot = jnp.sum((key_col < key_row).astype(jnp.int32), axis=0, keepdims=True)
    slot = jnp.bitwise_xor(slot, core * rows)
    place = lax.broadcasted_iota(jnp.int32, (held, held), 0)
    order_ref[...] = (place == slot).astype(jnp.float32).astype(jnp.bfloat16)


def unpack_moved(moved_ref, k_all, v_all):
    nodes = moved_ref.shape[0]
    tokens = k_all.shape[0] // nodes
    half = tokens // 2
    width = HEADS * HD

    def unpack(node, carry):
        for part in range(2):
            row = pl.ds(pl.multiple_of(node * tokens + part * half, half), half)
            col = 2 * part * width
            k_all[row, :] = moved_ref[node, Q_ROWS:, col : col + width]
            for head in range(HEADS):
                at = col + width + head * HD
                v_all[row, 2 * head * HD : (2 * head + 1) * HD] = moved_ref[node, Q_ROWS:, at : at + HD]
        return carry

    lax.fori_loop(0, nodes, unpack, 0)


def unpack_pieces(pieces, tokens, k_all, v_all):
    me = lax.axis_index("ctx")
    width = HEADS * HD

    def chip_of(sender):
        offset = jnp.where(sender % CORES == 0, ACROSS, ALONG)
        chip = jnp.bitwise_xor(sender, offset) // CORES
        return [chip * CORES + core for core in range(CORES)]

    senders = [jnp.bitwise_xor(me, index) for index in range(2 * CORES)]
    nodes = [[jnp.bitwise_xor(sender, offset) for offset in FAR] for sender in senders]
    nodes.append([jnp.bitwise_xor(me, DIAGONAL)] + chip_of(me))
    nodes += [[node] for node in [jnp.bitwise_xor(senders[1], DIAGONAL)] + chip_of(senders[1])]
    nodes.append([me // CORES * CORES + core for core in range(CORES)])
    for ref, held in zip(pieces, nodes):
        for place, node in enumerate(held):
            row = pl.ds(pl.multiple_of(node * tokens, tokens), tokens)
            here = slice(place * tokens, (place + 1) * tokens)
            k_all[row, :] = ref[here, :width]
            for head in range(HEADS):
                at = width + head * HD
                v_all[row, 2 * head * HD : (2 * head + 1) * HD] = ref[here, at : at + HD]


def unpack_kernel(tokens, *refs):
    kv_refs, (k_all, v_all) = refs[:-2], refs[-2:]
    for head in range(HEADS):
        ones = jnp.ones((v_all.shape[0], HD), jnp.bfloat16)
        v_all[:, (2 * head + 1) * HD : (2 * head + 2) * HD] = ones
    if len(kv_refs) == 1:
        unpack_moved(kv_refs[0], k_all, v_all)
    else:
        unpack_pieces(kv_refs, tokens, k_all, v_all)


def attend_kernel(q_ref, pos_ref, start_ref, order_ref, k_all, v_all, context, other_ref):
    total = k_all.shape[0]
    held = context.shape[0]
    block_rows = 32
    blocks = held // block_rows
    span = total // blocks
    scale = math.log2(math.e) / math.sqrt(HD)

    def rows_of(block):
        return slice(block * block_rows, (block + 1) * block_rows)

    def scores_of(block, head, keys):
        parts = block_rows // SUB
        mine = slice(head * SUB, (head + 1) * SUB)
        messages = [q_ref[block * parts + part].astype(jnp.float32)[mine] for part in range(parts)]
        pieces = []
        for group in range(GROUP):
            for message in messages:
                pieces.append(message[:, group * HD : (group + 1) * HD])
        return lax.dot_general(
            jnp.concatenate(pieces, axis=0).astype(jnp.bfloat16),
            k_all[keys, head * HD : (head + 1) * HD],
            (((1,), (1,)), ((), ())),
            preferred_element_type=jnp.float32,
        )

    def weights_of(block, keys, scores, peak=None):
        count = keys.stop - keys.start
        at = keys.start + lax.broadcasted_iota(jnp.int32, (block_rows, count), 1)
        seen = (at <= pos_ref[rows_of(block), :1]) & (at >= start_ref[rows_of(block), :1])
        scores = scores.reshape(GROUP, block_rows, count) + jnp.where(seen, 0.0, NEGATIVE)[None]
        scores = scores.reshape(GROUP * block_rows, count)
        top = jnp.max(scores, axis=1, keepdims=True)
        if peak is None:
            return top, jnp.exp2((scores - top) * scale).astype(jnp.bfloat16)
        top = jnp.maximum(peak, top)
        weights = jnp.exp2((scores - top) * scale).reshape(GROUP, block_rows, count)
        weights = jnp.where(seen[None], weights, 0.0).reshape(GROUP * block_rows, count)
        return top, weights.astype(jnp.bfloat16)

    def sums_of(head, keys, weights):
        values = v_all[keys, 2 * head * HD : (2 * head + 2) * HD]
        return jnp.dot(weights, values, preferred_element_type=jnp.float32)

    def store(block, head, sums):
        result = (sums[:, :HD] / sums[:, HD:]).astype(jnp.bfloat16)
        for group in range(GROUP):
            col = head * WIDE + group * HD
            part = result[group * block_rows : (group + 1) * block_rows]
            context[rows_of(block), col : col + HD] = part

    tasks = [
        (block, head, slice(max(0, block - blocks // 2) * span, (block + 1) * span))
        for block in reversed(range(blocks))
        for head in range(HEADS)
    ]
    most = 1024
    if max(keys.stop - keys.start for _, _, keys in tasks) <= most:
        scores, last = scores_of(*tasks[0]), None
        for index, (block, head, keys) in enumerate(tasks):
            later = scores_of(*tasks[index + 1]) if index + 1 < len(tasks) else None
            _, weights = weights_of(block, keys, scores)
            if last is not None:
                store(*last[:2], sums_of(*last[1:]))
            scores, last = later, (block, head, keys, weights)
        store(*last[:2], sums_of(*last[1:]))
    else:
        for block, head, keys in tasks:
            peak = jnp.full((GROUP * block_rows, 1), NEGATIVE, jnp.float32)
            sums = jnp.zeros((GROUP * block_rows, 2 * HD), jnp.float32)
            for lower in range(keys.start, keys.stop, most):
                part = slice(lower, min(lower + most, keys.stop))
                top, weights = weights_of(block, part, scores_of(block, head, part), peak)
                sums = sums * jnp.exp2((peak - top) * scale) + sums_of(head, part, weights)
                peak = top
            store(block, head, sums)

    moved = jnp.dot(order_ref[held // CORES :, :], context[...], preferred_element_type=jnp.float32)
    other_ref[...] = moved.astype(jnp.bfloat16)


def copy_to_columns(core, source_ref, out_hbm, sem):
    width = HEADS * WIDE
    side = pl.ds(pl.multiple_of(core * width, width), width)
    copy = pltpu.make_async_copy(source_ref, out_hbm.at[:, side], sem)
    copy.start()
    copy.wait()


def write_own_kernel(order_ref, context_ref, out_hbm, own_ref, sem):
    order = order_ref[: own_ref.shape[0], :]
    moved = jnp.dot(order, context_ref[...], preferred_element_type=jnp.float32)
    own_ref[...] = moved.astype(jnp.bfloat16)
    copy_to_columns(lax.axis_index("ctx") % CORES, own_ref, out_hbm, sem)


def write_received_kernel(received_ref, half_hbm, out_hbm, sem):
    copy_to_columns(1 - lax.axis_index("ctx") % CORES, received_ref, out_hbm, sem)


def on_device(queries, keys, values, owner, rollout_lengths):
    rows = queries.shape[0]
    nodes = lax.axis_size("ctx")
    total = owner.shape[0]
    chips = nodes // CORES
    per_chip = rows // chips
    held = rows * CORES
    table = owner.reshape(total // LANES, LANES)
    whole = pl.BlockSpec(memory_space=pltpu.VMEM)
    hbm = pl.BlockSpec(memory_space=pltpu.HBM)
    apart = nodes == 16

    def swap(array, *offsets):
        pairs = [(node, node ^ offsets[node % len(offsets)]) for node in range(nodes)]
        return lax.ppermute(array, "ctx", pairs)

    kv_rows = 0 if apart else rows // 2
    message = jax.ShapeDtypeStruct((nodes, Q_ROWS + kv_rows, WIDE), jnp.bfloat16)
    order_in, q_near, kv_near = pl.pallas_call(
        fetch_kernel,
        out_shape=[
            jax.ShapeDtypeStruct((rows, rows), jnp.bfloat16),
            jax.ShapeDtypeStruct(queries.shape, jnp.bfloat16),
            jax.ShapeDtypeStruct((rows, 2 * KVH * HD), jnp.bfloat16),
        ],
        in_specs=[hbm] * 4,
        out_specs=[whole] * 3,
        scratch_shapes=[pltpu.VMEM(table.shape, jnp.int32), pltpu.SemaphoreType.DMA((4,))],
        compiler_params=VMEM,
        name="fetch",
    )(*(pltpu.with_memory_space_constraint(x, pltpu.HBM) for x in (table, queries, keys, values)))
    if apart:
        other = swap(kv_near, 1)
        far = [swap(kv_near, offset) for offset in FAR]
        diagonal = swap(kv_near, DIAGONAL)
        chip = pl.pallas_call(
            pair_kernel,
            out_shape=jax.ShapeDtypeStruct((CORES * rows, 2 * KVH * HD), jnp.bfloat16),
            in_specs=[whole] * 2,
            out_specs=whole,
            compiler_params=VMEM,
            name="pair",
        )(kv_near, other)
        next_chip = swap(chip, ACROSS, ALONG)
        q_near, _ = lax.optimization_barrier((q_near, chip))

    operands = (order_in, q_near) if apart else (order_in, q_near, kv_near)
    packed = pl.pallas_call(
        functools.partial(pack_kernel, chips),
        out_shape=message,
        in_specs=[whole] * len(operands),
        out_specs=whole,
        compiler_params=VMEM,
        cost_estimate=pl.CostEstimate(
            flops=2 * rows * rows * H * HD, bytes_accessed=4 * rows * H * HD, transcendentals=0
        ),
        name="pack",
    )(*operands)
    moved = lax.all_to_all(packed, "ctx", split_axis=0, concat_axis=0, tiled=True)

    pos, start, order = pl.pallas_call(
        functools.partial(place_kernel, per_chip),
        out_shape=(
            jax.ShapeDtypeStruct((held, LANES), jnp.int32),
            jax.ShapeDtypeStruct((held, LANES), jnp.int32),
            jax.ShapeDtypeStruct((held, held), jnp.bfloat16),
        ),
        in_specs=[pl.BlockSpec(memory_space=pltpu.SMEM), whole],
        out_specs=(whole, whole, whole),
        compiler_params=VMEM,
        name="place",
    )(rollout_lengths, table)

    if apart:

        def heads_of(flops, count, *blocks):
            total_rows = sum(block.shape[0] for block in blocks)
            shapes = [total_rows] + [total_rows // count] * count
            return pl.pallas_call(
                functools.partial(heads_kernel, count),
                out_shape=[jax.ShapeDtypeStruct((n, 2 * HEADS * HD), jnp.bfloat16) for n in shapes],
                in_specs=[whole] * len(blocks),
                out_specs=[whole] * (1 + count),
                compiler_params=VMEM,
                cost_estimate=pl.CostEstimate(flops=flops, bytes_accessed=2**20, transcendentals=0),
                name="heads",
            )(*blocks)

        mine_far, other_far = heads_of(2 * 10**10, 1, *far)
        from_both, from_y, from_core = swap(other_far, 3), swap(mine_far, 2), swap(other_far, 1)
        mine_chip, _ = heads_of(10**6, 1, chip)
        diagonal, next_chip, *_ = lax.optimization_barrier((diagonal, next_chip, order))
        mine_near, *other_near = heads_of(10**6, 1 + CORES, diagonal, next_chip)
        kv_parts = [mine_far, from_core, from_y, from_both, mine_near]
        kv_parts += [swap(part, 1) for part in other_near] + [mine_chip]
        q_part = moved
    else:
        kv_parts = [moved]
        groups = held // SUB
        q_part = moved[:, :Q_ROWS].reshape(groups, nodes // groups, HEADS, SUB, WIDE)[:, :, :, :per_chip]
        q_part = q_part.transpose(0, 2, 1, 3, 4).reshape(groups, Q_ROWS, WIDE)

    k_all, v_all = pl.pallas_call(
        functools.partial(unpack_kernel, rows),
        out_shape=[
            jax.ShapeDtypeStruct((total, HEADS * HD), jnp.bfloat16),
            jax.ShapeDtypeStruct((total, HEADS * 2 * HD), jnp.bfloat16),
        ],
        in_specs=[whole] * len(kv_parts),
        out_specs=[whole] * 2,
        compiler_params=VMEM,
        name="unpack",
    )(*kv_parts)
    context, other = pl.pallas_call(
        attend_kernel,
        out_shape=(
            jax.ShapeDtypeStruct((held, HEADS * WIDE), jnp.bfloat16),
            jax.ShapeDtypeStruct((rows, HEADS * WIDE), jnp.bfloat16),
        ),
        in_specs=[whole] * 6,
        out_specs=(whole, whole),
        compiler_params=VMEM,
        name="attend",
    )(q_part, pos, start, order, k_all, v_all)

    result = jax.ShapeDtypeStruct((rows, H * HD), jnp.bfloat16)
    half = pl.pallas_call(
        write_own_kernel,
        out_shape=result,
        in_specs=[whole] * 2,
        out_specs=hbm,
        scratch_shapes=[pltpu.VMEM((rows, HEADS * WIDE), jnp.bfloat16), pltpu.SemaphoreType.DMA],
        compiler_params=VMEM,
        name="write_own",
    )(order, context)
    return pl.pallas_call(
        write_received_kernel,
        out_shape=result,
        in_specs=[whole, hbm],
        out_specs=hbm,
        scratch_shapes=[pltpu.SemaphoreType.DMA],
        input_output_aliases={1: 0},
        compiler_params=VMEM,
        name="write_received",
    )(swap(other, 1), half)


def solution(mesh):
    placed = (
        P(("groups", "ctx"), None),
        P(("groups", "ctx"), None),
        P(("groups", "ctx"), None),
        P("groups"),
        P("groups"),
    )
    return jax.shard_map(
        on_device, mesh=mesh, in_specs=placed, out_specs=P(("groups", "ctx"), None), check_vma=False
    )
```
